32 devices in a mesh: dp: 8 (over y, x, core), mp: 4 (over z).
Axes of the slice: x: 2, y: 2, z: 4, core: 2. Of those that a mesh axis runs over, the one named last changes fastest.
Arguments:
- patches: bfloat16 [12288, 768], P(('dp', 'mp')), may hold values from -6 to 6
- cotangent: bfloat16 [12288, 768], P(('dp', 'mp')), may hold values from -6 to 6
- conditioning: bfloat16 [24, 768], P('dp'), may hold values from -6 to 6
- lengths: int32 [8, 3], P('dp'), may hold values from 1 to 768, 1536 in all within a row
- routes: int32 [12288, 2], P('dp'), may hold values from 0 to 7, all different within a row; in each aligned block of 1536 rows (0 to 1535, 1536 to 3071, ...) at most 480 rows name the same one
- ada_weight: float32 [768, 4608], P(None, ('dp', 'mp')), may hold values from -0.21875 to 0.21875
- ada_first: float32 [768, 4608], P(None, ('dp', 'mp')), may hold values from -32 to 32
- ada_second: float32 [768, 4608], P(None, ('dp', 'mp')), may hold values from 81.1008 to 1290.24
- router_weight: float32 [6144], P(('dp', 'mp')), may hold values from -0.15625 to 0.15625
- router_first: float32 [6144], P(('dp', 'mp')), may hold values from -32 to 32
- router_second: float32 [6144], P(('dp', 'mp')), may hold values from 81.1008 to 1290.24
- qkv_weight: float32 [768, 2304], P('dp', 'mp'), may hold values from -0.21875 to 0.21875
- qkv_first: float32 [768, 2304], P('dp', 'mp'), may hold values from -20 to 20
- qkv_second: float32 [768, 2304], P('dp', 'mp'), may hold values from 29.4912 to 466.944
- proj_weight: float32 [768, 768], P('mp', 'dp'), may hold values from -1.5 to 1.5
- proj_first: float32 [768, 768], P('mp', 'dp'), may hold values from -32 to 32
- proj_second: float32 [768, 768], P('mp', 'dp'), may hold values from 61.44 to 983.04
- shared_in_weight: float32 [768, 3072], P('dp', 'mp'), may hold values from -0.21875 to 0.21875
- shared_in_first: float32 [768, 3072], P('dp', 'mp'), may hold values from -28 to 28
- shared_in_second: float32 [768, 3072], P('dp', 'mp'), may hold values from 51.6096 to 823.296
- shared_out_weight: float32 [3072, 768], P('mp', 'dp'), may hold values from -0.109375 to 0.109375
- shared_out_first: float32 [3072, 768], P('mp', 'dp'), may hold values from -28 to 28
- shared_out_second: float32 [3072, 768], P('mp', 'dp'), may hold values from 51.6096 to 823.296
- expert_in_weight: float32 [8, 768, 3072], P(None, 'dp', 'mp'), may hold values from -0.21875 to 0.21875
- expert_in_first: float32 [8, 768, 3072], P(None, 'dp', 'mp'), may hold values from -7 to 7
- expert_in_second: float32 [8, 768, 3072], P(None, 'dp', 'mp'), may hold values from 3.19488 to 51.6096
- expert_out_weight: float32 [8, 3072, 768], P(None, 'mp', 'dp'), may hold values from -0.109375 to 0.109375
- expert_out_first: float32 [8, 3072, 768], P(None, 'mp', 'dp'), may hold values from -7 to 7
- expert_out_second: float32 [8, 3072, 768], P(None, 'mp', 'dp'), may hold values from 3.19488 to 51.6096
Outputs:
- result: bfloat16 [12288, 768], P(('dp', 'mp'))
- patch_grad: bfloat16 [12288, 768], P(('dp', 'mp'))
- ada_weight_new: float32 [768, 4608], P(None, ('dp', 'mp'))
- ada_first_new: float32 [768, 4608], P(None, ('dp', 'mp'))
- ada_second_new: float32 [768, 4608], P(None, ('dp', 'mp'))
- ada_weight_low: bfloat16 [768, 4608], P(None, ('dp', 'mp'))
- router_weight_new: float32 [6144], P(('dp', 'mp'))
- router_first_new: float32 [6144], P(('dp', 'mp'))
- router_second_new: float32 [6144], P(('dp', 'mp'))
- router_weight_low: bfloat16 [6144], P(('dp', 'mp'))
- qkv_weight_new: float32 [768, 2304], P('dp', 'mp')
- qkv_first_new: float32 [768, 2304], P('dp', 'mp')
- qkv_second_new: float32 [768, 2304], P('dp', 'mp')
- qkv_weight_low: bfloat16 [768, 2304], P('dp', 'mp')
- proj_weight_new: float32 [768, 768], P('mp', 'dp')
- proj_first_new: float32 [768, 768], P('mp', 'dp')
- proj_second_new: float32 [768, 768], P('mp', 'dp')
- proj_weight_low: bfloat16 [768, 768], P('mp', 'dp')
- shared_in_weight_new: float32 [768, 3072], P('dp', 'mp')
- shared_in_first_new: float32 [768, 3072], P('dp', 'mp')
- shared_in_second_new: float32 [768, 3072], P('dp', 'mp')
- shared_in_weight_low: bfloat16 [768, 3072], P('dp', 'mp')
- shared_out_weight_new: float32 [3072, 768], P('mp', 'dp')
- shared_out_first_new: float32 [3072, 768], P('mp', 'dp')
- shared_out_second_new: float32 [3072, 768], P('mp', 'dp')
- shared_out_weight_low: bfloat16 [3072, 768], P('mp', 'dp')
- expert_in_weight_new: float32 [8, 768, 3072], P(None, 'dp', 'mp')
- expert_in_first_new: float32 [8, 768, 3072], P(None, 'dp', 'mp')
- expert_in_second_new: float32 [8, 768, 3072], P(None, 'dp', 'mp')
- expert_in_weight_low: bfloat16 [8, 768, 3072], P(None, 'dp', 'mp')
- expert_out_weight_new: float32 [8, 3072, 768], P(None, 'mp', 'dp')
- expert_out_first_new: float32 [8, 3072, 768], P(None, 'mp', 'dp')
- expert_out_second_new: float32 [8, 3072, 768], P(None, 'mp', 'dp')
- expert_out_weight_low: bfloat16 [8, 3072, 768], P(None, 'mp', 'dp')
The draws below stay inside these ranges and needn't reach their ends.
Inputs may be any that keep to these rules, and one draw needn't show every extreme that they name: Each group's 3 lengths add up to 1536; the largest is exactly 768. `routes`: A row names two different experts; within each group's 1536 rows no expert is named by more than 480 rows, a bound that some block reaches.
All inputs are finite; a program needn't handle non-finite values.
Results may differ from the reference program's by a relative error of at most 0.033.
The reference program's roundings to bfloat16 on the way count: a program that leaves them out, or rounds other values in their place, can miss the bound.
Values may be sent and summed in bfloat16 or wider, within the bound.
No kernel may reach another device: no remote copies, remote signals or barrier semaphores. Data moves between devices by JAX's collectives and lax.ppermute only.
A program may use at most 256 MiB of HBM per device.

```python
import math
import jax
import jax.numpy as jnp
import numpy as np
from jax import lax

D = 768
H = 12
HD = 64
FF = 3072
E = 8
ITEMS = 3
STEP = 10
GROUP = 1536
TOKENS = 12288
CAP = 480
LONGEST = 768
N_DP = 8


def shard_levels(rng, extent, shards, smallest, top_value):
    def one(dim, shards_of):
        heights = jax.random.uniform(jax.random.fold_in(jax.random.fold_in(rng, 6), dim), (shards_of,), jnp.float32, smallest / len(shards), top_value / len(shards))
        return jnp.repeat(jnp.exp(heights), extent[dim] // shards_of).reshape((-1,) + (1,) * (len(extent) - dim - 1))

    gain = one(*shards[0])
    for cut in shards[1:]:
        gain = gain * one(*cut)
    return gain


def length_profile(number_of, total, most, slope):
    loads = [(1 << 20) // math.isqrt(grade ** slope) + 1 for grade in range(2, number_of + 1)]
    surplus, given = total - most - (number_of - 1), [1] * (number_of - 1)
    while surplus > 0:
        free = [i for i in range(number_of - 1) if given[i] < most]
        whole, left = sum([loads[i] for i in free]), surplus
        for i in free:
            extra = min(most - given[i], max(1, left * loads[i] // whole), surplus)
            given[i] = given[i] + extra
            surplus = surplus - extra
    return np.array([most] + given)


def uneven(rng, count, total, bound, lean):
    if count == 2:
        one = jax.random.randint(rng, (), max(1, total - bound), min(bound, total - 1) + 1)
        return jnp.stack([one, total - one])
    sizes = jnp.asarray(length_profile(count, total, bound, lean), jnp.int32)
    couples = (count - 1) // 2
    source_of, sink = sizes[1:1 + 2 * couples:2], sizes[2:2 + 2 * couples:2]
    slack = jnp.minimum(source_of - 1, bound - sink)
    shifted = jax.random.randint(jax.random.fold_in(rng, 1), (couples,), 0, 1 << 20) % (slack + 1)
    sizes = sizes.at[1:1 + 2 * couples:2].set(source_of - shifted).at[2:2 + 2 * couples:2].set(sink + shifted)
    return sizes[jax.random.permutation(jax.random.fold_in(rng, 2), count)]


def deal_out(stream_key, own, number, rows, count, top, reach, skew):
    ranking = jax.random.permutation(stream_key, count)
    packed, usual = portions_of(count, rows * top, reach, skew, True), portions_of(count, rows * top, reach, skew, False)
    places = jnp.arange(count)

    def named(sizes, turn):
        used = int((sizes > 0).sum())
        fixed = max(1, used // 4)
        shifted = fixed + (places - fixed + turn * (used - fixed)) % max(1, count - fixed)
        return jnp.zeros((count,), jnp.int32).at[ranking[jnp.where(places < fixed, places, shifted)]].set(jnp.asarray(sizes, jnp.int32))

    sizes = jnp.where(number % 4 == 0, named(packed, number // 4), named(usual, number - number // 4 - 1))
    mixed = jax.random.permutation(jax.random.fold_in(own, 3), count)
    source_of, receiver = mixed[0:count // 2 * 2:2], mixed[1:count // 2 * 2:2]
    slack = jnp.minimum(sizes[source_of] - 1, reach - sizes[receiver]) // 2
    slack = jnp.where((source_of == ranking[0]) | (receiver == ranking[0]) | (sizes[receiver] == 0), 0, jnp.maximum(slack, 0))
    shifted = jax.random.randint(jax.random.fold_in(own, 4), (count // 2,), 0, 1 << 20) % (slack + 1)
    sizes = sizes.at[source_of].add(-shifted).at[receiver].add(shifted)
    labels = jnp.searchsorted(jnp.cumsum(sizes), jnp.arange(rows * top), side="right").astype(jnp.int32)
    listing = labels.reshape(top, rows).T
    listing = listing[jax.random.permutation(jax.random.fold_in(own, 1), rows)]
    turn = jax.random.randint(jax.random.fold_in(own, 2), (rows, 1), 0, top)
    return jnp.take_along_axis(listing, (jnp.arange(top)[None, :] + turn) % top, axis=1)


def portions_of(amount, total, limit, slope, full):
    portions = [(1 << 20) // math.isqrt(standing ** slope) + 1 for standing in range(1, amount + 1)]
    largest = limit if full else min(limit, max(-(-total // amount), total * portions[0] // sum(portions)))
    least = 1 if total - largest >= amount - 1 else 0
    counts, surplus = [largest] + [least] * (amount - 1), total - largest - least * (amount - 1)
    while surplus > 0:
        candidates = [i for i in range(1, amount) if counts[i] < largest] or [i for i in range(1, amount) if counts[i] < limit]
        pool, left = sum([portions[i] for i in candidates]), surplus
        for i in candidates:
            extra = min(limit - counts[i], max(1, left * portions[i] // pool), surplus)
            counts[i] = counts[i] + extra
            surplus = surplus - extra
    return np.array(counts)


def normal_values(stream_key, extent, width, reach, cuts=(), held_as=jnp.bfloat16):
    values = jax.random.normal(stream_key, extent, jnp.float32) * width
    if len(cuts) > 0:
        values = shard_levels(stream_key, extent, cuts, -0.22, 0.18) * values
    return jnp.clip(values, min=-reach, max=reach).astype(held_as)


def setup_inputs(seed: int = 0) -> dict:
    streams_of = jax.random.split(jax.random.key(seed), 30)
    patches = normal_values(streams_of[0], (TOKENS, D), 1.0, 6.0, ((0, 32),))
    cotangent = normal_values(streams_of[1], (TOKENS, D), 1.0, 6.0, ((0, 32),))
    conditioning = normal_values(streams_of[2], (N_DP * ITEMS, D), 1.0, 6.0, ((0, 8),))
    lengths = jax.vmap(lambda own: uneven(own, ITEMS, GROUP, LONGEST, 1))(jax.random.split(streams_of[3], N_DP)).reshape((N_DP, ITEMS)).astype(jnp.int32)
    routes_keys = jax.random.split(jax.random.fold_in(streams_of[4], 1), TOKENS // GROUP)
    routes_turns = jax.random.permutation(jax.random.fold_in(streams_of[4], 3), TOKENS // GROUP)
    routes = jax.vmap(lambda own, number: deal_out(jax.random.fold_in(streams_of[4], 2), own, number, GROUP, E, 2, CAP, 1))(routes_keys, routes_turns).reshape((TOKENS, 2))
    ada_weight = normal_values(streams_of[5], (D, 6 * D), D ** -0.5, 0.21875, ((1, 32),), jnp.float32)
    ada_first = normal_values(streams_of[6], (D, 6 * D), (0.055 * TOKENS ** 0.5), 32.0, ((1, 32),), jnp.float32)
    ada_second = jnp.clip(jnp.exp(math.log(1290.24) - 2.7668907 * jax.random.uniform(streams_of[7], (D, 6 * D), jnp.float32) ** shard_levels(streams_of[7], (D, 6 * D), ((1, 32),), -0.2, 0.2)), 81.1008, 1290.24)
    router_weight = normal_values(streams_of[8], (D * E,), (2 * D) ** -0.5, 0.15625, ((0, 32),), jnp.float32)
    router_first = normal_values(streams_of[9], (D * E,), (0.055 * TOKENS ** 0.5), 32.0, ((0, 32),), jnp.float32)
    router_second = jnp.clip(jnp.exp(math.log(1290.24) - 2.7668907 * jax.random.uniform(streams_of[10], (D * E,), jnp.float32) ** shard_levels(streams_of[10], (D * E,), ((0, 32),), -0.2, 0.2)), 81.1008, 1290.24)
    qkv_weight = normal_values(streams_of[11], (D, 3 * D), D ** -0.5, 0.21875, ((0, 8), (1, 4)), jnp.float32)
    qkv_first = normal_values(streams_of[12], (D, 3 * D), (0.033 * TOKENS ** 0.5), 20.0, ((0, 8), (1, 4)), jnp.float32)
    qkv_second = jnp.clip(jnp.exp(math.log(466.944) - 2.7621174 * jax.random.uniform(streams_of[13], (D, 3 * D), jnp.float32) ** shard_levels(streams_of[13], (D, 3 * D), ((0, 8), (1, 4)), -0.2, 0.2)), 29.4912, 466.944)
    proj_weight = normal_values(streams_of[14], (D, D), (D * 32 // GROUP) ** -0.5, 1.5, ((0, 4), (1, 8)), jnp.float32)
    proj_first = normal_values(streams_of[15], (D, D), (0.05 * TOKENS ** 0.5), 32.0, ((0, 4), (1, 8)), jnp.float32)
    proj_second = jnp.clip(jnp.exp(math.log(983.04) - 2.7725887 * jax.random.uniform(streams_of[16], (D, D), jnp.float32) ** shard_levels(streams_of[16], (D, D), ((0, 4), (1, 8)), -0.2, 0.2)), 61.44, 983.04)
    shared_in_weight = normal_values(streams_of[17], (D, FF), D ** -0.5, 0.21875, ((0, 8), (1, 4)), jnp.float32)
    shared_in_first = normal_values(streams_of[18], (D, FF), (0.044 * TOKENS ** 0.5), 28.0, ((0, 8), (1, 4)), jnp.float32)
    shared_in_second = jnp.clip(jnp.exp(math.log(823.296) - 2.769608 * jax.random.uniform(streams_of[19], (D, FF), jnp.float32) ** shard_levels(streams_of[19], (D, FF), ((0, 8), (1, 4)), -0.2, 0.2)), 51.6096, 823.296)
    shared_out_weight = normal_values(streams_of[20], (FF, D), FF ** -0.5, 0.109375, ((0, 4), (1, 8)), jnp.float32)
    shared_out_first = normal_values(streams_of[21], (FF, D), (0.044 * TOKENS ** 0.5), 28.0, ((0, 4), (1, 8)), jnp.float32)
    shared_out_second = jnp.clip(jnp.exp(math.log(823.296) - 2.769608 * jax.random.uniform(streams_of[22], (FF, D), jnp.float32) ** shard_levels(streams_of[22], (FF, D), ((0, 4), (1, 8)), -0.2, 0.2)), 51.6096, 823.296)
    expert_in_weight = normal_values(streams_of[23], (E, D, FF), D ** -0.5, 0.21875, ((1, 8), (2, 4)), jnp.float32)
    expert_in_first = normal_values(streams_of[24], (E, D, FF), (0.011 * TOKENS ** 0.5), 7.0, ((1, 8), (2, 4)), jnp.float32)
    expert_in_second = jnp.clip(jnp.exp(math.log(51.6096) - 2.7821582 * jax.random.uniform(streams_of[25], (E, D, FF), jnp.float32) ** shard_levels(streams_of[25], (E, D, FF), ((1, 8), (2, 4)), -0.2, 0.2)), 3.19488, 51.6096)
    expert_out_weight = normal_values(streams_of[26], (E, FF, D), FF ** -0.5, 0.109375, ((1, 4), (2, 8)), jnp.float32)
    expert_out_first = normal_values(streams_of[27], (E, FF, D), (0.011 * TOKENS ** 0.5), 7.0, ((1, 4), (2, 8)), jnp.float32)
    expert_out_second = jnp.clip(jnp.exp(math.log(51.6096) - 2.7821582 * jax.random.uniform(streams_of[28], (E, FF, D), jnp.float32) ** shard_levels(streams_of[28], (E, FF, D), ((1, 4), (2, 8)), -0.2, 0.2)), 3.19488, 51.6096)
    return {"patches": patches, "cotangent": cotangent, "conditioning": conditioning, "lengths": lengths, "routes": routes, "ada_weight": ada_weight, "ada_first": ada_first, "ada_second": ada_second, "router_weight": router_weight, "router_first": router_first, "router_second": router_second, "qkv_weight": qkv_weight, "qkv_first": qkv_first, "qkv_second": qkv_second, "proj_weight": proj_weight, "proj_first": proj_first, "proj_second": proj_second, "shared_in_weight": shared_in_weight, "shared_in_first": shared_in_first, "shared_in_second": shared_in_second, "shared_out_weight": shared_out_weight, "shared_out_first": shared_out_first, "shared_out_second": shared_out_second, "expert_in_weight": expert_in_weight, "expert_in_first": expert_in_first, "expert_in_second": expert_in_second, "expert_out_weight": expert_out_weight, "expert_out_first": expert_out_first, "expert_out_second": expert_out_second}


beta_one = 0.9
beta_two = 0.95
epsilon = 1e-08
weight_decay = 0.1
norm_floor = 1e-06
highest = lax.Precision.HIGHEST

@jax.custom_vjp
def low(v):
    return lax.optimization_barrier(v.astype(jnp.bfloat16)).astype(jnp.float32)

@jax.custom_vjp
def low_back(v):
    return v

def low_keep(v):
    return (low(v), None)

def low_pass(kept, grad):
    return (grad,)

def back_keep(v):
    return (v, None)

def back_low(kept, grad):
    return (low(grad),)
low.defvjp(low_keep, low_pass)
low_back.defvjp(back_keep, back_low)

def layer_norm(values):
    centred = values - lax.optimization_barrier(jnp.mean(values, axis=1, keepdims=True))
    spread = lax.optimization_barrier(jnp.mean(centred * centred, axis=1, keepdims=True))
    return centred * lax.rsqrt(spread + norm_floor)

def modulate(values, shift_term, scaling):
    return layer_norm(values) * (1.0 + scaling) + shift_term

def slot_tables(route_ids, capacity):
    flattened = route_ids.reshape(-1)
    markers = (flattened[:, None] == jnp.arange(E, dtype=jnp.int32)[None, :]).astype(jnp.int32)
    earlier = (jnp.cumsum(markers, axis=0) - markers).astype(jnp.int32)
    positions = lax.optimization_barrier(jnp.sum(earlier * markers, axis=1)).astype(jnp.int32)
    destination = (flattened * capacity + positions).astype(jnp.int32)
    owner_rows = (jnp.arange(flattened.shape[0], dtype=jnp.int32) // 2).astype(jnp.int32)
    slot_token = jnp.zeros((E * capacity,), jnp.int32).at[destination].set(owner_rows)
    occupied = jnp.zeros((E * capacity,), jnp.int32).at[destination].set(1)
    return (destination.reshape(-1, 2), slot_token, occupied)

def attention(queries, key_rows, value_rows, segment):
    qrows = 512 if GROUP % 512 == 0 else GROUP
    scaling = HD ** (-0.5)

    @jax.checkpoint
    def attend_block(row_start):
        query_rows = lax.dynamic_slice_in_dim(queries, row_start, qrows, 0)
        query_items = lax.dynamic_slice_in_dim(segment, row_start, qrows, 0)
        scores = low_back(jnp.einsum('qhd,khd->hqk', query_rows, key_rows, precision=highest) * scaling)
        allowed = query_items[:, None] == segment[None, :]
        scores = jnp.where(allowed[None], scores, -1e+30)
        attn_probs = low(jax.nn.softmax(scores, axis=2))
        return jnp.einsum('hqk,khd->qhd', attn_probs, value_rows, precision=highest)
    starts = jnp.arange(GROUP // qrows, dtype=jnp.int32) * qrows
    mixed = lax.map(attend_block, starts)
    return mixed.reshape(GROUP, H * HD)

def forward(states, params, cond_rows, item_lengths, route_ids):
    ada_matrix, router_flat, qkv_matrix, proj_matrix, shared_in, shared_out, expert_in, expert_out = [low(p) for p in params]
    bounds = jnp.cumsum(item_lengths).astype(jnp.int32)
    positions = jnp.arange(GROUP, dtype=jnp.int32)
    segment = lax.optimization_barrier(jnp.sum((positions[:, None] >= bounds[None, :]).astype(jnp.int32), axis=1)).astype(jnp.int32)
    modulation = jnp.dot(low(jax.nn.silu(cond_rows)), ada_matrix, precision=highest)
    token_mod = modulation[segment]
    shift_one, scale_one, gate_one, shift_two, scale_two, gate_two = jnp.split(token_mod, 6, axis=1)
    h_one = low(modulate(states, shift_one, scale_one))
    qkv = low(low_back(jnp.dot(h_one, qkv_matrix, precision=highest))).reshape(GROUP, H, 3, HD)
    mixed = attention(qkv[:, :, 0], qkv[:, :, 1], qkv[:, :, 2], segment)
    mixed = low(low_back(mixed))
    attn_branch = low_back(jnp.dot(mixed, proj_matrix, precision=highest))
    x_one = states + gate_one * attn_branch
    h_two = low(modulate(x_one, shift_two, scale_two))
    shared_act = low(jax.nn.gelu(low_back(jnp.dot(h_two, shared_in, precision=highest))))
    shared_res = jnp.dot(shared_act, shared_out, precision=highest)
    logits = jnp.dot(h_two, router_flat.reshape(D, E), precision=highest)
    markers = (route_ids[:, :, None] == jnp.arange(E, dtype=jnp.int32)[None, None, :]).astype(jnp.float32)
    picked = lax.optimization_barrier(jnp.sum(markers * logits[:, None, :], axis=2))
    gates = jax.nn.softmax(picked, axis=1)
    destination, slot_token, occupied = slot_tables(route_ids, CAP)
    dispatched = jnp.where(occupied[:, None] > 0, h_two[slot_token], 0.0).reshape(E, CAP, D)
    expert_pre = low_back(jnp.einsum('ecd,edf->ecf', dispatched, expert_in, precision=highest))
    expert_act = low(jax.nn.gelu(expert_pre))
    expert_res = low_back(jnp.einsum('ecf,efd->ecd', expert_act, expert_out, precision=highest)).reshape(E * CAP, D)
    mixture = gates[:, 0:1] * expert_res[destination[:, 0]] + gates[:, 1:2] * expert_res[destination[:, 1]]
    mlp_branch = low_back(shared_res + mixture)
    return x_one + gate_two * mlp_branch

def adamw_update(master, first, second, gradient, fan_in):
    step_rate = 0.5 * fan_in ** (-0.5)
    first_new = beta_one * first + (1.0 - beta_one) * gradient
    second_new = beta_two * second + (1.0 - beta_two) * gradient * gradient
    first_hat = first_new / (1.0 - beta_one ** STEP)
    second_hat = second_new / (1.0 - beta_two ** STEP)
    master_new = master - step_rate * (first_hat / (jnp.sqrt(second_hat) + epsilon) + weight_decay * master)
    return (master_new, first_new, second_new, master_new.astype(jnp.bfloat16))

def reference(patches, cotangent, conditioning, lengths, routes, ada_weight, ada_first, ada_second, router_weight, router_first, router_second, qkv_weight, qkv_first, qkv_second, proj_weight, proj_first, proj_second, shared_in_weight, shared_in_first, shared_in_second, shared_out_weight, shared_out_first, shared_out_second, expert_in_weight, expert_in_first, expert_in_second, expert_out_weight, expert_out_first, expert_out_second):
    masters = (ada_weight, router_weight, qkv_weight, proj_weight, shared_in_weight, shared_out_weight, expert_in_weight, expert_out_weight)
    firsts = (ada_first, router_first, qkv_first, proj_first, shared_in_first, shared_out_first, expert_in_first, expert_out_first)
    seconds = (ada_second, router_second, qkv_second, proj_second, shared_in_second, shared_out_second, expert_in_second, expert_out_second)
    fan_ins = (D, D, D, 8.0 * D / GROUP, D, FF, D, FF)
    group_states = patches.astype(jnp.float32).reshape(N_DP, GROUP, D)
    group_grads = cotangent.astype(jnp.float32).reshape(N_DP, GROUP, D)
    group_conds = conditioning.astype(jnp.float32).reshape(N_DP, ITEMS, D)
    group_routes = routes.reshape(N_DP, GROUP, 2)

    def advance(totals, inputs):
        states, grad_out, cond_rows, item_lengths, route_ids = inputs

        def closed(values, params):
            return forward(values, params, cond_rows, item_lengths, route_ids)
        outcome, pull = jax.vjp(closed, states, masters)
        grad_states, grad_params = pull(grad_out)
        totals = tuple((a + b for a, b in zip(totals, grad_params)))
        return (totals, (outcome.astype(jnp.bfloat16), grad_states.astype(jnp.bfloat16)))
    zeros_start = tuple((jnp.zeros_like(w) for w in masters))
    gradients, (outcomes, input_grads) = lax.scan(advance, zeros_start, (group_states, group_grads, group_conds, lengths, group_routes))
    updates = []
    for master, first, second, gradient, fan_in in zip(masters, firsts, seconds, gradients, fan_ins):
        updates.extend(adamw_update(master, first, second, gradient, fan_in))
    return tuple([outcomes.reshape(TOKENS, D), input_grads.reshape(TOKENS, D)] + updates)
```

```python
import jax
import jax.numpy as jnp
from jax import lax
from jax.sharding import PartitionSpec as P

H = 12
HD = 64
E = 8
STEP = 10

beta_one = 0.9
beta_two = 0.95
epsilon = 1e-08
weight_decay = 0.1
norm_floor = 1e-06
highest = lax.Precision.HIGHEST
f32 = jnp.float32
bf16 = jnp.bfloat16


def norm_parts(values):
    centred = values - jnp.mean(values, axis=1, keepdims=True)
    inverse = lax.rsqrt(jnp.mean(centred * centred, axis=1, keepdims=True) + norm_floor)
    return centred * inverse, inverse


def norm_back(normed, inverse, gradient):
    first = jnp.mean(gradient, axis=1, keepdims=True)
    second = jnp.mean(gradient * normed, axis=1, keepdims=True)
    return inverse * (gradient - first - normed * second)


def gelu_back(before, gradient):
    return jax.vjp(jax.nn.gelu, before)[1](gradient)[0]


def by_item(table, segment):
    picked = table[0][None, :]
    for item in range(1, table.shape[0]):
        picked = jnp.where(segment[:, None] >= item, table[item][None, :], picked)
    return picked


def line_gather(block):
    width = lax.axis_size("mp")
    rank = lax.axis_index("mp")
    ups, downs = [block], [block]
    for step in range(1, width):
        up_pairs = [(i, i + 1) for i in range(step - 1, width - 1)]
        down_pairs = [(i + 1, i) for i in range(width - step)]
        ups.append(lax.ppermute(ups[-1], "mp", up_pairs))
        downs.append(lax.ppermute(downs[-1], "mp", down_pairs))
    rows = block.shape[0]
    whole = jnp.zeros((rows * width,) + block.shape[1:], block.dtype)
    for offset in range(width):
        piece = block if offset == 0 else jnp.where(rank >= offset, ups[offset], downs[width - offset])
        owner = lax.rem(rank - offset + width, width)
        whole = lax.dynamic_update_slice_in_dim(whole, piece, owner * rows, 0)
    return whole


def line_scatter(partial, axis=0):
    width = lax.axis_size("mp")
    rank = lax.axis_index("mp")
    extent = partial.shape[axis] // width

    def part(index):
        index = jnp.clip(index, 0, width - 1)
        return lax.dynamic_slice_in_dim(partial, index * extent, extent, axis)

    up, down = None, None
    for step in range(1, width):
        up_send, down_send = part(rank + width - step), part(rank - width + step)
        if up is not None:
            up_send = (up_send.astype(f32) + up.astype(f32)).astype(bf16)
            down_send = (down_send.astype(f32) + down.astype(f32)).astype(bf16)
        up = lax.ppermute(up_send, "mp", [(i, i + 1) for i in range(step)])
        down = lax.ppermute(down_send, "mp", [(i, i - 1) for i in range(width - step, width)])
    return part(rank).astype(f32) + up.astype(f32) + down.astype(f32)


def adamw_update(master, first, second, gradient, fan_in):
    step_rate = 0.5 * fan_in ** (-0.5)
    first_new = beta_one * first + (1.0 - beta_one) * gradient
    second_new = beta_two * second + (1.0 - beta_two) * gradient * gradient
    first_hat = first_new / (1.0 - beta_one**STEP)
    second_hat = second_new / (1.0 - beta_two**STEP)
    master_new = master - step_rate * (
        first_hat / (jnp.sqrt(second_hat) + epsilon) + weight_decay * master
    )
    return (master_new, first_new, second_new, master_new.astype(bf16))


def body(
    patches,
    cotangent,
    conditioning,
    lengths,
    routes,
    ada_weight,
    ada_first,
    ada_second,
    router_weight,
    router_first,
    router_second,
    qkv_weight,
    qkv_first,
    qkv_second,
    proj_weight,
    proj_first,
    proj_second,
    shared_in_weight,
    shared_in_first,
    shared_in_second,
    shared_out_weight,
    shared_out_first,
    shared_out_second,
    expert_in_weight,
    expert_in_first,
    expert_in_second,
    expert_out_weight,
    expert_out_first,
    expert_out_second,
):
    rows, D = patches.shape
    width = lax.axis_size("mp")
    n_dp = lax.axis_size("dp")
    devices = width * n_dp
    group = rows * width
    capacity = 5 * group // 16
    heads_here = H // width
    qrows = 512
    block_count = group // qrows
    scaling = HD ** (-0.5)
    model_rank = lax.axis_index("mp")
    item_count = lengths.shape[1]
    hidden = shared_in_weight.shape[1]
    ada_cols = ada_weight.shape[1]
    router_cols = router_weight.shape[0]

    def mine(values, axis=0):
        extent = values.shape[axis] // width
        return lax.dynamic_slice_in_dim(values, model_rank * extent, extent, axis)

    patches_all = line_gather(patches)
    cond_all = lax.all_gather(conditioning, "dp", axis=0, tiled=True)
    qkv_here = lax.all_gather(qkv_weight.astype(bf16), "dp", axis=0, tiled=True)
    proj_rows = line_gather(proj_weight.astype(bf16))
    proj_t = lax.all_gather(proj_rows.T, "dp", axis=0, tiled=True)
    cot_all = line_gather(cotangent)
    out_slab = jnp.concatenate(
        [
            jnp.swapaxes(expert_out_weight.astype(bf16), 1, 2),
            shared_out_weight.astype(bf16).T[None],
        ],
        axis=0,
    )
    in_slab = jnp.concatenate(
        [expert_in_weight.astype(bf16), shared_in_weight.astype(bf16)[None]], axis=0
    )
    out_t = lax.all_gather(out_slab, "dp", axis=1, tiled=True)
    in_w = lax.all_gather(in_slab, "dp", axis=1, tiled=True)

    cond_act = jax.nn.silu(cond_all.astype(f32)).astype(bf16)
    columns = jnp.dot(cond_act, ada_weight.astype(bf16), preferred_element_type=f32)
    columns = jnp.repeat(columns.reshape(n_dp, item_count * ada_cols), width, axis=0)
    router_low = router_weight.astype(bf16).astype(f32)
    payload = jnp.concatenate(
        [columns, jnp.broadcast_to(router_low[None], (devices, router_cols))], axis=1
    )
    received = lax.all_to_all(payload, ("dp", "mp"), 0, 0, tiled=True)
    modulation = (
        received[:, : item_count * ada_cols]
        .reshape(devices, item_count, ada_cols)
        .transpose(1, 0, 2)
        .reshape(item_count, devices * ada_cols)
    )
    router_matrix = received[:, item_count * ada_cols :].reshape(D, E).astype(bf16)

    bounds = jnp.cumsum(lengths[0])
    places = jnp.arange(group, dtype=jnp.int32)
    segment = jnp.sum((places[:, None] >= bounds[None, :]).astype(jnp.int32), axis=1)
    segment_mine = mine(segment)
    terms = jnp.split(modulation, 6, axis=1)
    shift_one, scale_one, gate_one, shift_two, scale_two, gate_two = [
        by_item(t, segment) for t in terms
    ]
    _, scale_one_mine, gate_one_mine, _, scale_two_mine, gate_two_mine = [
        by_item(t, segment_mine) for t in terms
    ]

    names = (routes[:, :, None] == jnp.arange(E, dtype=jnp.int32)[None, None, :]).any(axis=1)
    below = (places[:, None] > places[None, :]).astype(bf16)
    earlier = jnp.dot(below, names.astype(bf16), preferred_element_type=f32).astype(jnp.int32)
    place_of = jnp.where(names, earlier, -1).T
    picks = place_of[:, None, :] == jnp.arange(capacity, dtype=jnp.int32)[None, :, None]
    picks_low = picks.astype(bf16)

    normed_one, _ = norm_parts(patches_all.astype(f32))
    h_one_all = (normed_one * (1.0 + scale_one) + shift_one).astype(bf16)
    qkv = jnp.dot(h_one_all, qkv_here, preferred_element_type=f32).astype(bf16)
    qkv = qkv.reshape(group, heads_here, 3, HD)
    queries, key_rows, value_rows = qkv[:, :, 0], qkv[:, :, 1], qkv[:, :, 2]
    starts = jnp.arange(block_count, dtype=jnp.int32) * qrows

    def block_scores(row_start):
        query_rows = lax.dynamic_slice_in_dim(queries, row_start, qrows, 0)
        query_items = lax.dynamic_slice_in_dim(segment, row_start, qrows, 0)
        scores = (
            jnp.einsum("qhd,khd->hqk", query_rows, key_rows, preferred_element_type=f32) * scaling
        )
        allowed = query_items[:, None] == segment[None, :]
        return (query_rows, jnp.where(allowed[None], scores, -1e30))

    def attend_block(row_start):
        query_rows, scores = block_scores(row_start)
        row_peak = jnp.max(scores, axis=2, keepdims=True)
        exps = jnp.exp(scores - row_peak)
        row_total = jnp.sum(exps, axis=2, keepdims=True)
        attn_probs = (exps / row_total).astype(bf16)
        mixed_block = jnp.einsum("hqk,khd->qhd", attn_probs, value_rows, preferred_element_type=f32)
        return (mixed_block.astype(bf16), (row_peak + jnp.log(row_total))[:, :, 0])

    mixed_blocks, log_totals = lax.map(attend_block, starts)
    mixed_here = mixed_blocks.reshape(group, heads_here * HD)
    mixed_parts = line_gather(mixed_here)
    mixed_all = (
        mixed_parts.reshape(width, group, heads_here * HD).transpose(1, 0, 2).reshape(group, H * HD)
    )
    attn_branch = jnp.einsum("gc,dc->gd", mixed_all, proj_t, preferred_element_type=f32)
    x_one = patches_all.astype(f32) + gate_one * attn_branch
    normed_two, _ = norm_parts(x_one)
    h_two = (normed_two * (1.0 + scale_two) + shift_two).astype(bf16)

    grad_branch = (gate_two * cot_all.astype(f32)).astype(bf16)
    branch_slots = jnp.einsum("ect,td->ecd", picks_low, grad_branch, preferred_element_type=f32)
    branch_slots = branch_slots.astype(bf16)
    back_slots = jnp.einsum("ecd,edf->ecf", branch_slots, out_t[:E], preferred_element_type=f32)
    back_shared = jnp.dot(grad_branch, out_t[E], preferred_element_type=f32)

    logits = jnp.dot(h_two, router_matrix, preferred_element_type=f32).T
    names_t = place_of >= 0
    peak = jnp.max(jnp.where(names_t, logits, -jnp.inf), axis=0, keepdims=True)
    weights = jnp.where(names_t, jnp.exp(logits - peak), 0.0)
    gates = weights / jnp.sum(weights, axis=0, keepdims=True)
    gate_slots = jnp.sum(jnp.where(picks, gates[:, None, :], 0.0), axis=2)
    shared_pre = jnp.dot(h_two, in_w[E], preferred_element_type=f32)
    shared_act = jax.nn.gelu(shared_pre).astype(bf16)
    grad_shared_pre = gelu_back(shared_pre, back_shared).astype(bf16)
    dispatched = jnp.einsum(
        "ect,td->ecd", picks_low, h_two, preferred_element_type=f32
    ).astype(bf16)
    expert_pre = jnp.einsum("ecd,edf->ecf", dispatched, in_w[:E], preferred_element_type=f32)
    expert_act = jax.nn.gelu(expert_pre).astype(bf16)
    grad_expert_pre = gelu_back(expert_pre, gate_slots[:, :, None] * back_slots).astype(bf16)
    grad_gate_slots = jnp.sum(back_slots * expert_act.astype(f32), axis=2)
    grad_gates = jnp.sum(jnp.where(picks, grad_gate_slots[:, :, None], 0.0), axis=1)
    grad_logits = gates * (grad_gates - jnp.sum(gates * grad_gates, axis=0, keepdims=True))
    grad_dispatched = jnp.einsum(
        "ecf,edf->ecd", grad_expert_pre, in_w[:E], preferred_element_type=f32
    ).astype(bf16)
    grad_h_two = (
        jnp.einsum("gf,df->gd", grad_shared_pre, in_w[E], preferred_element_type=f32)
        + jnp.einsum("ect,ecd->td", picks_low, grad_dispatched, preferred_element_type=f32)
        + jnp.einsum("eg,de->gd", grad_logits, router_matrix.astype(f32), precision=highest)
    )
    grad_h_two_mine = line_scatter(grad_h_two.astype(bf16))

    grad_res = (gate_slots[:, :, None] * branch_slots.astype(f32)).astype(bf16)
    grad_out_slab = jnp.concatenate(
        [
            jnp.einsum("ecd,ecf->edf", grad_res, expert_act, preferred_element_type=f32).astype(bf16),
            jnp.einsum("gd,gf->df", grad_branch, shared_act, preferred_element_type=f32).astype(bf16)[
                None
            ],
        ],
        axis=0,
    )
    grad_in_slab = jnp.concatenate(
        [
            jnp.einsum("ecd,ecf->edf", dispatched, grad_expert_pre, preferred_element_type=f32).astype(
                bf16
            ),
            jnp.einsum("gd,gf->df", h_two, grad_shared_pre, preferred_element_type=f32).astype(bf16)[
                None
            ],
        ],
        axis=0,
    )
    grad_out_mine = lax.psum_scatter(grad_out_slab, "dp", scatter_dimension=1, tiled=True).astype(f32)
    grad_in_mine = lax.psum_scatter(grad_in_slab, "dp", scatter_dimension=1, tiled=True).astype(f32)
    grad_router = jnp.einsum("gd,eg->de", h_two.astype(f32), grad_logits, precision=highest)
    expert_res = jnp.einsum("ecf,edf->ecd", expert_act, out_t[:E], preferred_element_type=f32)
    expert_res = (gate_slots[:, :, None] * expert_res).astype(bf16)
    mlp_part = jnp.einsum("gf,df->gd", shared_act, out_t[E], preferred_element_type=f32) + jnp.einsum(
        "ect,ecd->td", picks_low, expert_res, preferred_element_type=f32
    )
    mlp_branch = line_scatter(mlp_part.astype(bf16))

    x_one_mine = mine(x_one)
    attn_mine = mine(attn_branch)
    grad_out = cotangent.astype(f32)
    outcome = x_one_mine + gate_two_mine * mlp_branch
    grad_gate_two = grad_out * mlp_branch
    normed_two_mine, inverse_two = norm_parts(x_one_mine)
    grad_scale_two = grad_h_two_mine * normed_two_mine
    grad_x_one = grad_out + norm_back(
        normed_two_mine, inverse_two, grad_h_two_mine * (1.0 + scale_two_mine)
    )
    grad_gate_one = grad_x_one * attn_mine
    grad_attn = (gate_one_mine * grad_x_one).astype(bf16)
    grad_mixed_mine = jnp.dot(grad_attn, proj_t, preferred_element_type=f32).astype(bf16)
    grad_mixed = lax.all_to_all(
        grad_mixed_mine.reshape(rows, width, heads_here * HD).transpose(1, 0, 2),
        "mp",
        0,
        0,
        tiled=True,
    ).reshape(group, heads_here, HD)
    grad_proj_t = jnp.einsum("gd,gc->dc", grad_attn, mine(mixed_all), preferred_element_type=f32)
    grad_proj_t = line_scatter(grad_proj_t.astype(bf16), axis=1)

    def attend_back(carry, inputs):
        grad_keys, grad_values = carry
        row_start, log_block = inputs
        query_rows, scores = block_scores(row_start)
        grad_rows = lax.dynamic_slice_in_dim(grad_mixed, row_start, qrows, 0)
        soft_rows = jnp.exp(scores - log_block[:, :, None])
        soft_low = soft_rows.astype(bf16)
        grad_values = grad_values + jnp.einsum(
            "hqk,qhd->khd", soft_low, grad_rows, preferred_element_type=f32
        )
        grad_soft = jnp.einsum("qhd,khd->hqk", grad_rows, value_rows, preferred_element_type=f32)
        middle = jnp.sum(soft_rows * grad_soft, axis=2, keepdims=True)
        grad_scores = (soft_rows * (grad_soft - middle)).astype(bf16)
        grad_query = (
            jnp.einsum("hqk,khd->qhd", grad_scores, key_rows, preferred_element_type=f32) * scaling
        )
        grad_keys = (
            grad_keys
            + jnp.einsum("hqk,qhd->khd", grad_scores, query_rows, preferred_element_type=f32)
            * scaling
        )
        return ((grad_keys, grad_values), grad_query)

    zero_rows = jnp.zeros((group, heads_here, HD), f32)
    (grad_keys, grad_values), grad_queries = lax.scan(
        attend_back, (zero_rows, zero_rows), (starts, log_totals)
    )
    grad_queries = grad_queries.reshape(group, heads_here, HD)
    grad_qkv = (
        jnp.stack([grad_queries, grad_keys, grad_values], axis=2)
        .astype(bf16)
        .reshape(group, heads_here * 3 * HD)
    )
    grad_h_one = line_scatter(
        jnp.einsum("gc,dc->gd", grad_qkv, qkv_here, preferred_element_type=f32).astype(bf16)
    )
    grad_qkv_weight = jnp.einsum("gd,gc->dc", h_one_all, grad_qkv, preferred_element_type=f32)
    grad_attn_slab = jnp.concatenate([grad_qkv_weight.astype(bf16), grad_proj_t.astype(bf16)], axis=1)
    grad_attn_mine = lax.psum_scatter(grad_attn_slab, "dp", scatter_dimension=0, tiled=True).astype(f32)

    normed_one_mine, inverse_one = norm_parts(patches.astype(f32))
    grad_scale_one = grad_h_one * normed_one_mine
    grad_states = grad_x_one + norm_back(
        normed_one_mine, inverse_one, grad_h_one * (1.0 + scale_one_mine)
    )
    grad_token_mod = jnp.concatenate(
        [grad_h_one, grad_scale_one, grad_gate_one, grad_h_two_mine, grad_scale_two, grad_gate_two],
        axis=1,
    )
    marks_mine = (
        segment_mine[:, None] == jnp.arange(item_count, dtype=jnp.int32)[None, :]
    ).astype(f32)
    grad_modulation = jnp.einsum("ti,tc->ic", marks_mine, grad_token_mod, precision=highest)
    payload = jnp.concatenate(
        [
            grad_modulation.reshape(item_count, devices, ada_cols)
            .transpose(1, 0, 2)
            .reshape(devices, item_count * ada_cols),
            grad_router.reshape(devices, router_cols),
        ],
        axis=1,
    )
    received = lax.all_to_all(payload, ("dp", "mp"), 0, 0, tiled=True)
    router_grad = jnp.sum(received[:, item_count * ada_cols :], axis=0)
    columns = jnp.sum(
        received[:, : item_count * ada_cols].reshape(n_dp, width, item_count, ada_cols), axis=1
    ).reshape(n_dp * item_count, ada_cols)
    ada_grad = jnp.einsum("id,ic->dc", cond_act.astype(f32), columns, precision=highest)

    qkv_cols = qkv_weight.shape[1]
    gradients = (
        ada_grad,
        router_grad,
        grad_attn_mine[:, :qkv_cols],
        grad_attn_mine[:, qkv_cols:].T,
        grad_in_mine[E],
        grad_out_mine[E].T,
        grad_in_mine[:E],
        jnp.swapaxes(grad_out_mine[:E], 1, 2),
    )
    states_of = (
        (ada_weight, ada_first, ada_second),
        (router_weight, router_first, router_second),
        (qkv_weight, qkv_first, qkv_second),
        (proj_weight, proj_first, proj_second),
        (shared_in_weight, shared_in_first, shared_in_second),
        (shared_out_weight, shared_out_first, shared_out_second),
        (expert_in_weight, expert_in_first, expert_in_second),
        (expert_out_weight, expert_out_first, expert_out_second),
    )
    total_hidden = float(hidden * width)
    fan_ins = (D, D, D, 8.0 * D / group, D, total_hidden, D, total_hidden)
    updates = []
    for (master, first, second), gradient, fan_in in zip(states_of, gradients, fan_ins):
        updates.extend(adamw_update(master, first, second, gradient, float(fan_in)))
    return tuple([outcome.astype(bf16), grad_states.astype(bf16)] + updates)


def solution(mesh):
    tokens, data = P(("dp", "mp"), None), P("dp", None)
    ada, router = P(None, ("dp", "mp")), P(("dp", "mp"))
    deep, wide = P("dp", "mp"), P("mp", "dp")
    deep_experts, wide_experts = P(None, "dp", "mp"), P(None, "mp", "dp")
    kinds = (ada, router, deep, wide, deep, wide, deep_experts, wide_experts)
    in_specs = (tokens, tokens, data, data, data) + tuple(k for k in kinds for _ in range(3))
    out_specs = (tokens, tokens) + tuple(k for k in kinds for _ in range(4))
    return jax.shard_map(body, mesh=mesh, in_specs=in_specs, out_specs=out_specs, check_vma=False)
```

```python
import functools
import math

import jax
import jax.numpy as jnp
from jax import lax
from jax.experimental import pallas as pl
from jax.experimental.pallas import tpu as pltpu
from jax.sharding import PartitionSpec as P

H = 12
HD = 64
E = 8
STEP = 10

beta_one = 0.9
beta_two = 0.95
epsilon = 1e-08
weight_decay = 0.1
norm_floor = 1e-06
highest = lax.Precision.HIGHEST
f32 = jnp.float32
bf16 = jnp.bfloat16


def norm_parts(values):
    centred = values - jnp.mean(values, axis=1, keepdims=True)
    inverse = lax.rsqrt(jnp.mean(centred * centred, axis=1, keepdims=True) + norm_floor)
    return centred * inverse, inverse


def norm_back(normed, inverse, gradient):
    first = jnp.mean(gradient, axis=1, keepdims=True)
    second = jnp.mean(gradient * normed, axis=1, keepdims=True)
    return inverse * (gradient - first - normed * second)


def after(values, *earlier):
    return lax.optimization_barrier((values, earlier))[0]


class Gather:
    def __init__(self, block):
        self.ups, self.downs = [block], [block]

    def send(self):
        width, step = lax.axis_size("mp"), len(self.ups)
        up_pairs = [(i, i + 1) for i in range(step - 1, width - 1)]
        down_pairs = [(i + 1, i) for i in range(width - step)]
        return (
            lax.ppermute(self.ups[-1], "mp", up_pairs),
            lax.ppermute(self.downs[-1], "mp", down_pairs),
        )

    def take(self, pair):
        self.ups.append(pair[0])
        self.downs.append(pair[1])

    def blocks(self):
        width, rank = lax.axis_size("mp"), lax.axis_index("mp")
        pairs = zip(range(1, width), self.ups[1:], reversed(self.downs[1:]))
        return [self.ups[0]] + [jnp.where(rank >= i, u, d) for i, u, d in pairs]

    def whole(self, axis=0):
        width, rank = lax.axis_size("mp"), lax.axis_index("mp")
        return jnp.concatenate(
            [
                functools.reduce(
                    lambda kept, r: jnp.where(rank == r, self.block_of(index, r), kept),
                    range(1, width),
                    self.block_of(index, 0),
                )
                for index in range(width)
            ],
            axis=axis,
        )

    def block_of(self, index, rank):
        return self.ups[rank - index] if rank >= index else self.downs[index - rank]


class Scatter:
    def __init__(self, partial, axis=0):
        self.partial, self.axis, self.step = partial, axis, 1
        self.up, self.down = None, None

    def part(self, offset):
        width, rank = lax.axis_size("mp"), lax.axis_index("mp")
        extent = self.partial.shape[self.axis] // width
        index = jnp.clip(rank + offset, 0, width - 1)
        return lax.dynamic_slice_in_dim(self.partial, index * extent, extent, self.axis)

    def send(self):
        width, step = lax.axis_size("mp"), self.step
        up, down = self.part(width - step), self.part(step - width)
        if self.up is not None:
            up = (up.astype(f32) + self.up.astype(f32)).astype(bf16)
            down = (down.astype(f32) + self.down.astype(f32)).astype(bf16)
        return (
            lax.ppermute(up, "mp", [(i, i + 1) for i in range(step)]),
            lax.ppermute(down, "mp", [(i, i - 1) for i in range(width - step, width)]),
        )

    def take(self, pair):
        self.up, self.down = pair
        self.step += 1

    def terms(self):
        return self.part(0), self.up, self.down

    def total(self):
        return sum(t.astype(f32) for t in self.terms())


def phase(transfers, work):
    pairs, work = lax.optimization_barrier(([t.send() for t in transfers], work))
    for transfer, pair in zip(transfers, pairs):
        transfer.take(pair)
    return work


LANES = 128
Q_BLOCK = 256
FAR = 2.0**50
NT = (((1,), (1,)), ((), ()))
TN = (((0,), (0,)), ((), ()))
NN = (((1,), (0,)), ((), ()))


def dot(a, b, dims=NN):
    return lax.dot_general(a, b, dims, preferred_element_type=f32)


def key_widths(group):
    return sorted({min(w, group) for w in (512, 768, 1024, group)})


def key_windows(lengths, group):
    ends = jnp.cumsum(lengths)
    begins = ends - lengths
    first = jnp.arange(group // Q_BLOCK, dtype=jnp.int32) * Q_BLOCK
    last = first + Q_BLOCK - 1
    low = jnp.max(jnp.where(begins[None, :] <= first[:, None], begins[None, :], 0), axis=1)
    high = jnp.min(jnp.where(ends[None, :] > last[:, None], ends[None, :], group), axis=1)
    low = low // LANES * LANES
    widths = jnp.array(key_widths(group), jnp.int32)
    kind = jnp.sum((high - low)[:, None] > widths[None, :], axis=1).astype(jnp.int32)
    return jnp.minimum(low, group - widths[kind]).astype(jnp.int32), kind


def attend_kernel(start_ref, kind_ref, qkv_ref, mixed_ref, log_ref, *, group):
    block = pl.program_id(1)
    rows = pl.ds(pl.multiple_of(block * Q_BLOCK, Q_BLOCK), Q_BLOCK)
    query = qkv_ref[rows, 0:LANES] * jnp.asarray(HD**-0.5, bf16)
    for index, extent in enumerate(key_widths(group)):

        @pl.when(kind_ref[block] == index)
        def _():
            keys = pl.ds(pl.multiple_of(start_ref[block], LANES), extent)
            scores = dot(qkv_ref[keys, LANES : 2 * LANES], query, NT)
            peak = jnp.max(scores, axis=0, keepdims=True)
            exps = jnp.exp(scores - peak)
            total = jnp.sum(exps, axis=0, keepdims=True)
            probs = (exps * (1.0 / total)).astype(bf16)
            mixed = dot(qkv_ref[keys, 2 * LANES : 3 * LANES], probs, TN)
            mixed_ref[...] = mixed[:HD].astype(bf16)
            log_ref[...] = (peak + jnp.log(total))[None]


def attend(qkv, start, kind):
    group = qkv.shape[0]
    heads = qkv.shape[1] // (3 * LANES)
    blocks = group // Q_BLOCK
    return pl.pallas_call(
        functools.partial(attend_kernel, group=group),
        out_shape=(
            jax.ShapeDtypeStruct((heads * HD, group), bf16),
            jax.ShapeDtypeStruct((heads, 1, group), f32),
        ),
        grid_spec=pltpu.PrefetchScalarGridSpec(
            num_scalar_prefetch=2,
            grid=(heads, blocks),
            in_specs=[pl.BlockSpec((group, 3 * LANES), lambda h, i, *_: (0, h))],
            out_specs=(
                pl.BlockSpec((HD, Q_BLOCK), lambda h, i, *_: (h, i)),
                pl.BlockSpec((1, 1, Q_BLOCK), lambda h, i, *_: (h, 0, i)),
            ),
        ),
        compiler_params=pltpu.CompilerParams(vmem_limit_bytes=40 * 2**20),
        cost_estimate=pl.CostEstimate(
            flops=16 * heads * group * group * HD, bytes_accessed=6 * 2**20, transcendentals=heads * group * group
        ),
        name="attend",
    )(start, kind, qkv)


def attend_back_kernel(
    start_ref, kind_ref, qkv_ref, grad_ref, log_ref, out_ref, key_total, value_total, *, group
):
    block = pl.program_id(1)

    @pl.when(block == 0)
    def _():
        key_total[...] = jnp.zeros_like(key_total)
        value_total[...] = jnp.zeros_like(value_total)

    rows = pl.ds(pl.multiple_of(block * Q_BLOCK, Q_BLOCK), Q_BLOCK)
    scaling = HD**-0.5
    query = qkv_ref[rows, 0:LANES] * jnp.asarray(scaling, bf16)
    grad = grad_ref[...]
    kept = lax.broadcasted_iota(jnp.int32, (1, LANES), 1) < HD
    for index, extent in enumerate(key_widths(group)):

        @pl.when(kind_ref[block] == index)
        def _():
            keys = pl.ds(pl.multiple_of(start_ref[block], LANES), extent)
            key_rows = qkv_ref[keys, LANES : 2 * LANES]
            value_rows = qkv_ref[keys, 2 * LANES : 3 * LANES]
            probs = jnp.exp(dot(key_rows, query, NT) - log_ref[0])
            grad_probs = dot(value_rows[:, :HD], grad)
            middle = jnp.sum(probs * grad_probs, axis=0, keepdims=True)
            grad_scores = (probs * (grad_probs - middle)).astype(bf16)
            value_total[keys, :HD] += dot(probs.astype(bf16), grad, NT)
            key_total[keys, :] += dot(grad_scores, query)
            grad_query = dot(key_rows, grad_scores, TN).T * scaling
            out_ref[rows, 0:LANES] = jnp.where(kept, grad_query, 0.0).astype(bf16)

    @pl.when(block == pl.num_programs(1) - 1)
    def _():
        out_ref[:, LANES : 2 * LANES] = jnp.where(kept, key_total[...], 0.0).astype(bf16)
        out_ref[:, 2 * LANES : 3 * LANES] = value_total[...].astype(bf16)


def attend_back(qkv, grad_mixed, logs, start, kind):
    group = qkv.shape[0]
    heads = qkv.shape[1] // (3 * LANES)
    blocks = group // Q_BLOCK
    return pl.pallas_call(
        functools.partial(attend_back_kernel, group=group),
        out_shape=jax.ShapeDtypeStruct(qkv.shape, bf16),
        grid_spec=pltpu.PrefetchScalarGridSpec(
            num_scalar_prefetch=2,
            grid=(heads, blocks),
            in_specs=[
                pl.BlockSpec((group, 3 * LANES), lambda h, i, *_: (0, h)),
                pl.BlockSpec((HD, Q_BLOCK), lambda h, i, *_: (h, i)),
                pl.BlockSpec((1, 1, Q_BLOCK), lambda h, i, *_: (h, 0, i)),
            ],
            out_specs=pl.BlockSpec((group, 3 * LANES), lambda h, i, *_: (0, h)),
            scratch_shapes=[pltpu.VMEM((group, LANES), f32), pltpu.VMEM((group, LANES), f32)],
        ),
        compiler_params=pltpu.CompilerParams(vmem_limit_bytes=40 * 2**20),
        cost_estimate=pl.CostEstimate(
            flops=40 * heads * group * group * HD, bytes_accessed=12 * 2**20, transcendentals=heads * group * group
        ),
        name="attend_back",
    )(start, kind, qkv, grad_mixed, logs)


def item_rows(table_ref, term, width, segment, items):
    columns = slice(term * width, (term + 1) * width)
    rows = table_ref[0:1, columns]
    for item in range(1, items):
        rows = jnp.where(segment >= item, table_ref[item : item + 1, columns], rows)
    return rows


def item_sums(values, segment, items):
    return jnp.concatenate(
        [jnp.sum(jnp.where(segment == item, values, 0.0), axis=0, keepdims=True) for item in range(items)], axis=0
    )


def norm_one_kernel(*refs, width_mp, items):
    rank_ref, segment_ref, table_ref = refs[:3]
    block_refs, (rows_ref, h_ref) = refs[3 : 3 + width_mp], refs[3 + width_mp :]
    step = pl.program_id(0)
    segment = segment_ref[...]
    width = rows_ref.shape[1]
    for place in range(width_mp):

        @pl.when(step == place)
        def _():
            rows = block_refs[place][...]
            rows_ref[...] = rows
            normed, _ = norm_parts(rows.astype(f32))
            shift = item_rows(table_ref, 0, width, segment, items)
            scale = item_rows(table_ref, 1, width, segment, items)
            h_ref[...] = (normed * (1.0 + scale) + shift).astype(bf16)


def norm_one(blocks, table, segment):
    width_mp, (rows, width) = len(blocks), blocks[0].shape
    group, items = rows * width_mp, table.shape[0]

    def placed(i, rank):
        return (lax.rem(rank[0] - i + width_mp, width_mp), 0)

    def plain(*shape):
        return pl.BlockSpec(shape, lambda i, rank: (0,) * len(shape))

    return pl.pallas_call(
        functools.partial(norm_one_kernel, width_mp=width_mp, items=items),
        out_shape=(jax.ShapeDtypeStruct((group, width), bf16),) * 2,
        grid_spec=pltpu.PrefetchScalarGridSpec(
            num_scalar_prefetch=1,
            grid=(width_mp,),
            in_specs=[pl.BlockSpec((rows, 1), placed), plain(*table.shape)]
            + [plain(rows, width)] * width_mp,
            out_specs=(pl.BlockSpec((rows, width), placed),) * 2,
        ),
        compiler_params=pltpu.CompilerParams(vmem_limit_bytes=40 * 2**20),
        cost_estimate=pl.CostEstimate(flops=2 * 10**7, bytes_accessed=8 * 2**20, transcendentals=0),
        name="norm_one",
    )(lax.axis_index("mp").reshape(1), segment, table, *blocks)


def norm_two_kernel(*refs, width_mp, items):
    rank_ref, segment_ref, table_ref, rows_ref, proj_ref = refs[:5]
    mixed_refs = refs[5 : 5 + width_mp]
    h_ref, x_mine_ref, attn_mine_ref, mixed_mine_ref = refs[5 + width_mp :]
    step = pl.program_id(0)
    rank = rank_ref[0]
    segment = segment_ref[...]
    width = rows_ref.shape[1]
    heads = mixed_refs[0].shape[0]
    attn = jnp.zeros(rows_ref.shape, f32)
    for place in range(width_mp):
        owner = lax.rem(rank - place + width_mp, width_mp)
        here = pl.ds(pl.multiple_of(owner * heads, heads), heads)
        mixed = mixed_refs[place][...]
        attn += dot(mixed, proj_ref[here, :], TN)

        @pl.when(step == rank)
        def _():
            mixed_mine_ref[here, :] = mixed

    x_one = rows_ref[...].astype(f32) + item_rows(table_ref, 2, width, segment, items) * attn

    @pl.when(step == rank)
    def _():
        x_mine_ref[...] = x_one
        attn_mine_ref[...] = attn

    normed, _ = norm_parts(x_one)
    shift = item_rows(table_ref, 3, width, segment, items)
    scale = item_rows(table_ref, 4, width, segment, items)
    h_ref[...] = (normed * (1.0 + scale) + shift).astype(bf16)


def norm_two(blocks, patches, proj, table, segment):
    width_mp, (heads, group) = len(blocks), blocks[0].shape
    rows, width, items = group // width_mp, patches.shape[1], table.shape[0]

    def plain(*shape):
        return pl.BlockSpec(shape, lambda i, rank: (0,) * len(shape))

    return pl.pallas_call(
        functools.partial(norm_two_kernel, width_mp=width_mp, items=items),
        out_shape=(
            jax.ShapeDtypeStruct((group, width), bf16),
            jax.ShapeDtypeStruct((rows, width), f32),
            jax.ShapeDtypeStruct((rows, width), f32),
            jax.ShapeDtypeStruct((heads * width_mp, rows), bf16),
        ),
        grid_spec=pltpu.PrefetchScalarGridSpec(
            num_scalar_prefetch=1,
            grid=(width_mp,),
            in_specs=[
                pl.BlockSpec((rows, 1), lambda i, rank: (i, 0)),
                plain(*table.shape),
                pl.BlockSpec((rows, width), lambda i, rank: (i, 0)),
                plain(*proj.shape),
            ]
            + [pl.BlockSpec((heads, rows), lambda i, rank: (0, i))] * width_mp,
            out_specs=(
                pl.BlockSpec((rows, width), lambda i, rank: (i, 0)),
                plain(rows, width),
                plain(rows, width),
                plain(heads * width_mp, rows),
            ),
        ),
        compiler_params=pltpu.CompilerParams(vmem_limit_bytes=40 * 2**20),
        cost_estimate=pl.CostEstimate(flops=2 * 10**9, bytes_accessed=13 * 2**20, transcendentals=0),
        name="norm_two",
    )(lax.axis_index("mp").reshape(1), segment, table, patches, proj, *blocks)


def back_two_kernel(
    segment_ref,
    table_ref,
    own_ref,
    up_ref,
    down_ref,
    x_ref,
    attn_ref,
    cot_ref,
    proj_ref,
    grad_x_ref,
    grad_attn_ref,
    grad_mixed_ref,
    sums_ref,
    *,
    items,
):
    segment = segment_ref[...]
    width = x_ref.shape[1]
    grad = own_ref[...].astype(f32) + up_ref[...].astype(f32) + down_ref[...].astype(f32)
    normed, inverse = norm_parts(x_ref[...])
    scale = item_rows(table_ref, 4, width, segment, items)
    grad_x = cot_ref[...].astype(f32) + norm_back(normed, inverse, grad * (1.0 + scale))
    grad_x_ref[...] = grad_x
    grad_attn = (item_rows(table_ref, 2, width, segment, items) * grad_x).astype(bf16)
    grad_attn_ref[...] = grad_attn
    grad_mixed_ref[...] = dot(proj_ref[...], grad_attn, NT).astype(bf16)
    sums_ref[:, 0:width] = item_sums(grad_x * attn_ref[...], segment, items)
    sums_ref[:, width : 2 * width] = item_sums(grad, segment, items)
    sums_ref[:, 2 * width :] = item_sums(grad * normed, segment, items)


def back_two(terms, x_one, attn, cotangent, proj, table, segment):
    rows, width = x_one.shape
    items = table.shape[0]
    return pl.pallas_call(
        functools.partial(back_two_kernel, items=items),
        out_shape=(
            jax.ShapeDtypeStruct((rows, width), f32),
            jax.ShapeDtypeStruct((rows, width), bf16),
            jax.ShapeDtypeStruct((proj.shape[0], rows), bf16),
            jax.ShapeDtypeStruct((items, 3 * width), f32),
        ),
        compiler_params=pltpu.CompilerParams(vmem_limit_bytes=40 * 2**20),
        cost_estimate=pl.CostEstimate(flops=10**9, bytes_accessed=9 * 2**20, transcendentals=0),
        name="back_two",
    )(segment, table, *terms, x_one, attn, cotangent, proj)


def back_one_kernel(
    segment_ref,
    table_ref,
    own_ref,
    up_ref,
    down_ref,
    patches_ref,
    grad_x_ref,
    grad_ref,
    sums_ref,
    *,
    items,
):
    segment = segment_ref[...]
    width = patches_ref.shape[1]
    grad = own_ref[...].astype(f32) + up_ref[...].astype(f32) + down_ref[...].astype(f32)
    normed, inverse = norm_parts(patches_ref[...].astype(f32))
    scale = item_rows(table_ref, 1, width, segment, items)
    grad_ref[...] = (grad_x_ref[...] + norm_back(normed, inverse, grad * (1.0 + scale))).astype(bf16)
    sums_ref[:, 0:width] = item_sums(grad, segment, items)
    sums_ref[:, width:] = item_sums(grad * normed, segment, items)


def back_one(terms, patches, grad_x, table, segment):
    rows, width = patches.shape
    items = table.shape[0]
    return pl.pallas_call(
        functools.partial(back_one_kernel, items=items),
        out_shape=(
            jax.ShapeDtypeStruct((rows, width), bf16),
            jax.ShapeDtypeStruct((items, 2 * width), f32),
        ),
        compiler_params=pltpu.CompilerParams(vmem_limit_bytes=40 * 2**20),
        cost_estimate=pl.CostEstimate(flops=10**7, bytes_accessed=5 * 2**20, transcendentals=0),
        name="back_one",
    )(segment, table, *terms, patches, grad_x)


def outcome_kernel(
    segment_ref, table_ref, own_ref, up_ref, down_ref, x_ref, cot_ref, out_ref, sums_ref, *, items
):
    segment = segment_ref[...]
    width = x_ref.shape[1]
    branch = own_ref[...].astype(f32) + up_ref[...].astype(f32) + down_ref[...].astype(f32)
    gate = item_rows(table_ref, 5, width, segment, items)
    out_ref[...] = (x_ref[...] + gate * branch).astype(bf16)
    sums_ref[...] = item_sums(cot_ref[...].astype(f32) * branch, segment, items)


def outcome(terms, x_one, cotangent, table, segment):
    rows, width = x_one.shape
    items = table.shape[0]
    return pl.pallas_call(
        functools.partial(outcome_kernel, items=items),
        out_shape=(
            jax.ShapeDtypeStruct((rows, width), bf16),
            jax.ShapeDtypeStruct((items, width), f32),
        ),
        compiler_params=pltpu.CompilerParams(vmem_limit_bytes=40 * 2**20),
        cost_estimate=pl.CostEstimate(flops=10**7, bytes_accessed=5 * 2**20, transcendentals=0),
        name="outcome",
    )(segment, table, *terms, x_one, cotangent)


def gelu_terms(before):
    slope = (2.0 / math.pi) ** 0.5
    square = before * before
    curve = jnp.tanh(slope * before * (1.0 + 0.044715 * square))
    half = 0.5 * (1.0 + curve)
    value = before * half
    derivative = half + (0.5 * slope) * before * (1.0 - curve * curve) * (1.0 + 0.134145 * square)
    return value, derivative


def slot_picks(place_row, capacity):
    slots = lax.broadcasted_iota(jnp.int32, (capacity, place_row.shape[1]), 0)
    return slots == place_row


def row_chunks(group):
    return [slice(first, first + 512) for first in range(0, group, 512)]


def before_kernel(
    place_ref, named_ref, branch_ref, weight_ref, slots_ref, named_slots_ref, back_ref, shared_ref, *, experts
):
    step = pl.program_id(0)

    @pl.when(step < experts)
    def _():
        picks = slot_picks(place_ref[0], slots_ref.shape[1]).astype(bf16)
        slots = dot(picks, branch_ref[...]).astype(bf16)
        slots_ref[0] = slots
        named_slots_ref[0] = dot(picks, named_ref[...]).astype(bf16)
        back_ref[0] = dot(slots, weight_ref[0]).astype(bf16)

    @pl.when(step == experts)
    def _():
        for chunk in row_chunks(shared_ref.shape[0]):
            shared_ref[chunk, :] = dot(branch_ref[chunk, :], weight_ref[0]).astype(bf16)


def whole(*shape):
    return pl.BlockSpec(shape, lambda *_: (0,) * len(shape))


def per_expert(experts, *shape):
    return pl.BlockSpec(
        (1,) + shape, lambda e, *_: (jnp.minimum(e, experts - 1),) + (0,) * len(shape)
    )


def per_slab(*shape):
    return pl.BlockSpec((1,) + shape, lambda e, *_: (e,) + (0,) * len(shape))


def experts_before(places, named, branch, out_t, capacity):
    group, width = branch.shape
    experts, hidden = out_t.shape[0] - 1, out_t.shape[2]
    return pl.pallas_call(
        functools.partial(before_kernel, experts=experts),
        out_shape=(
            jax.ShapeDtypeStruct((experts, capacity, width), bf16),
            jax.ShapeDtypeStruct((experts, capacity, LANES), bf16),
            jax.ShapeDtypeStruct((experts, capacity, hidden), bf16),
            jax.ShapeDtypeStruct((group, hidden), bf16),
        ),
        grid=(experts + 1,),
        in_specs=[
            per_expert(experts, 1, group),
            whole(group, LANES),
            whole(group, width),
            per_slab(width, hidden),
        ],
        out_specs=(
            per_expert(experts, capacity, width),
            per_expert(experts, capacity, LANES),
            per_expert(experts, capacity, hidden),
            whole(group, hidden),
        ),
        compiler_params=pltpu.CompilerParams(vmem_limit_bytes=48 * 2**20),
        cost_estimate=pl.CostEstimate(
            flops=16 * 10**9, bytes_accessed=30 * 2**20, transcendentals=0
        ),
        name="experts_before",
    )(places.reshape(experts, 1, group), named, branch, out_t)


def slots_of(picked, slots):
    index = lax.broadcasted_iota(jnp.int32, (picked.shape[0], slots), 1)
    return ((index == picked[:, 0:1]) | (index == picked[:, 1:2])).astype(bf16)


def experts_kernel(
    place_ref,
    places_ref,
    picked_ref,
    rows_ref,
    weight_ref,
    router_ref,
    router_wide_ref,
    slots_ref,
    named_ref,
    back_ref,
    shared_back_ref,
    dispatched_ref,
    act_ref,
    grad_pre_ref,
    grad_res_ref,
    gate_ref,
    shared_act_ref,
    shared_grad_ref,
    grad_logits_ref,
    grad_rows_ref,
    grad_gates_ref,
    grad_slots_ref,
    *,
    experts,
):
    step = pl.program_id(0)
    group = rows_ref.shape[0]
    capacity = slots_ref.shape[1]

    @pl.when(step < experts)
    def _():
        picks = slot_picks(place_ref[0], capacity)
        dispatched = dot(picks.astype(bf16), rows_ref[...]).astype(bf16)
        dispatched_ref[0] = dispatched
        pre = dot(dispatched, weight_ref[0])
        logits = dot(dispatched, router_wide_ref[...])
        lane = lax.broadcasted_iota(jnp.int32, logits.shape, 1)
        named = named_ref[0].astype(f32) > 0.0
        peak = jnp.max(jnp.where(named, logits, -jnp.inf), axis=1, keepdims=True)
        shares = jnp.where(named, jnp.exp(logits - peak), 0.0)
        total = jnp.sum(shares, axis=1, keepdims=True)
        own = jnp.sum(jnp.where(lane == step, shares, 0.0), axis=1, keepdims=True)
        gate = jnp.where(total > 0.0, own / jnp.maximum(total, 1.0), 0.0)
        gate_ref[0] = gate
        value, slope = gelu_terms(pre)
        act = value.astype(bf16)
        act_ref[0] = act
        back = back_ref[0].astype(f32)
        grad_pre = (gate * back * slope).astype(bf16)
        grad_pre_ref[0] = grad_pre
        grad_res_ref[0] = (gate * slots_ref[0].astype(f32)).astype(bf16)
        grad_gate = jnp.sum(back * act.astype(f32), axis=1, keepdims=True)
        grad_gates_ref[step] = jnp.sum(jnp.where(picks, grad_gate, 0.0), axis=0, keepdims=True)
        here = pl.ds(pl.multiple_of(step * capacity, capacity), capacity)
        grad_slots_ref[here, :] = dot(grad_pre, weight_ref[0], NT).astype(bf16)

    @pl.when(step == experts)
    def _():
        logits = dot(router_ref[...], rows_ref[...], NT)
        named = places_ref[...] >= 0
        peak = jnp.max(jnp.where(named, logits, -jnp.inf), axis=0, keepdims=True)
        shares = jnp.where(named, jnp.exp(logits - peak), 0.0)
        gates = shares / jnp.sum(shares, axis=0, keepdims=True)
        grad_gates = jnp.concatenate([grad_gates_ref[e] for e in range(experts)], axis=0)
        grad_logits = gates * (grad_gates - jnp.sum(gates * grad_gates, axis=0, keepdims=True))
        grad_logits_ref[...] = grad_logits
        high = grad_logits.astype(bf16)
        rest = (grad_logits - high.astype(f32)).astype(bf16)
        for chunk in row_chunks(group):
            value, slope = gelu_terms(dot(rows_ref[chunk, :], weight_ref[0]))
            shared_act_ref[chunk, :] = value.astype(bf16)
            grad_pre = (shared_back_ref[chunk, :].astype(f32) * slope).astype(bf16)
            shared_grad_ref[chunk, :] = grad_pre
            total = dot(slots_of(picked_ref[chunk, :], experts * capacity), grad_slots_ref[...])
            total += dot(grad_pre, weight_ref[0], NT)
            total += dot(high[:, chunk], router_ref[...], TN)
            total += dot(rest[:, chunk], router_ref[...], TN)
            grad_rows_ref[chunk, :] = total.astype(bf16)


def experts_main(places, picked, h_two, in_w, router, slots, named, back, shared_back):
    group, width = h_two.shape
    experts, capacity, hidden = back.shape
    slot_shape = jax.ShapeDtypeStruct((experts, capacity, width), bf16)
    unit_shape = jax.ShapeDtypeStruct((experts, capacity, hidden), bf16)
    return pl.pallas_call(
        functools.partial(experts_kernel, experts=experts),
        out_shape=(
            slot_shape,
            unit_shape,
            unit_shape,
            slot_shape,
            jax.ShapeDtypeStruct((experts, capacity, 1), f32),
            jax.ShapeDtypeStruct((group, hidden), bf16),
            jax.ShapeDtypeStruct((group, hidden), bf16),
            jax.ShapeDtypeStruct((experts, group), f32),
            jax.ShapeDtypeStruct((group, width), bf16),
        ),
        grid=(experts + 1,),
        in_specs=[
            per_expert(experts, 1, group),
            whole(experts, group),
            whole(group, 2),
            whole(group, width),
            per_slab(width, hidden),
            whole(experts, width),
            whole(width, LANES),
            per_expert(experts, capacity, width),
            per_expert(experts, capacity, LANES),
            per_expert(experts, capacity, hidden),
            whole(group, hidden),
        ],
        out_specs=(
            per_expert(experts, capacity, width),
            per_expert(experts, capacity, hidden),
            per_expert(experts, capacity, hidden),
            per_expert(experts, capacity, width),
            per_expert(experts, capacity, 1),
            whole(group, hidden),
            whole(group, hidden),
            whole(experts, group),
            whole(group, width),
        ),
        scratch_shapes=[
            pltpu.VMEM((experts, 1, group), f32),
            pltpu.VMEM((experts * capacity, width), bf16),
        ],
        compiler_params=pltpu.CompilerParams(vmem_limit_bytes=58 * 2**20),
        cost_estimate=pl.CostEstimate(
            flops=32 * 10**9, bytes_accessed=50 * 2**20, transcendentals=5 * 10**6
        ),
        name="experts_main",
    )(
        places.reshape(experts, 1, group),
        places,
        picked,
        h_two,
        in_w,
        router.T,
        jnp.pad(router, ((0, 0), (0, LANES - experts))),
        slots,
        named,
        back,
        shared_back,
    )


def slab_kernel(a_ref, b_ref, a_shared_ref, b_shared_ref, out_ref, *, experts):
    step = pl.program_id(0)

    @pl.when(step < experts)
    def _():
        out_ref[0] = dot(a_ref[0], b_ref[0], TN).astype(bf16)

    @pl.when(step == experts)
    def _():
        out_ref[0] = dot(a_shared_ref[...], b_shared_ref[...], TN).astype(bf16)


def slab_product(a, b, a_shared, b_shared, name):
    experts, capacity, width = a.shape
    hidden = b.shape[2]
    group = a_shared.shape[0]
    return pl.pallas_call(
        functools.partial(slab_kernel, experts=experts),
        out_shape=jax.ShapeDtypeStruct((experts + 1, width, hidden), bf16),
        grid=(experts + 1,),
        in_specs=[
            per_expert(experts, capacity, width),
            per_expert(experts, capacity, hidden),
            whole(group, width),
            whole(group, hidden),
        ],
        out_specs=per_slab(width, hidden),
        compiler_params=pltpu.CompilerParams(vmem_limit_bytes=48 * 2**20),
        cost_estimate=pl.CostEstimate(
            flops=7 * 10**9, bytes_accessed=28 * 2**20, transcendentals=0
        ),
        name=name,
    )(a, b, a_shared, b_shared)


def branch_kernel(picked_ref, gate_ref, act_ref, weight_ref, shared_ref, out_ref, res_ref, *, experts):
    step = pl.program_id(0)
    capacity = act_ref.shape[1]

    @pl.when(step < experts)
    def _():
        here = pl.ds(pl.multiple_of(step * capacity, capacity), capacity)
        res_ref[here, :] = (gate_ref[0] * dot(act_ref[0], weight_ref[0], NT)).astype(bf16)

    @pl.when(step == experts)
    def _():
        for chunk in row_chunks(out_ref.shape[0]):
            total = dot(slots_of(picked_ref[chunk, :], experts * capacity), res_ref[...])
            total += dot(shared_ref[chunk, :], weight_ref[0], NT)
            out_ref[chunk, :] = total.astype(bf16)


def experts_out(picked, gates, act, out_t, shared_act):
    experts, capacity, hidden = act.shape
    group = shared_act.shape[0]
    width = out_t.shape[1]
    return pl.pallas_call(
        functools.partial(branch_kernel, experts=experts),
        out_shape=jax.ShapeDtypeStruct((group, width), bf16),
        grid=(experts + 1,),
        in_specs=[
            whole(group, 2),
            per_expert(experts, capacity, 1),
            per_expert(experts, capacity, hidden),
            per_slab(width, hidden),
            whole(group, hidden),
        ],
        out_specs=whole(group, width),
        scratch_shapes=[pltpu.VMEM((experts * capacity, width), bf16)],
        compiler_params=pltpu.CompilerParams(vmem_limit_bytes=48 * 2**20),
        cost_estimate=pl.CostEstimate(
            flops=16 * 10**9, bytes_accessed=22 * 2**20, transcendentals=0
        ),
        name="experts_out",
    )(picked, gates, act, out_t, shared_act)


def adamw_update(master, first, second, gradient, fan_in):
    step_rate = 0.5 * fan_in ** (-0.5)
    first_new = beta_one * first + (1.0 - beta_one) * gradient
    second_new = beta_two * second + (1.0 - beta_two) * gradient * gradient
    first_hat = first_new / (1.0 - beta_one**STEP)
    second_hat = second_new / (1.0 - beta_two**STEP)
    master_new = master - step_rate * (
        first_hat / (jnp.sqrt(second_hat) + epsilon) + weight_decay * master
    )
    return (master_new, first_new, second_new, master_new.astype(bf16))


def body(
    patches,
    cotangent,
    conditioning,
    lengths,
    routes,
    ada_weight,
    ada_first,
    ada_second,
    router_weight,
    router_first,
    router_second,
    qkv_weight,
    qkv_first,
    qkv_second,
    proj_weight,
    proj_first,
    proj_second,
    shared_in_weight,
    shared_in_first,
    shared_in_second,
    shared_out_weight,
    shared_out_first,
    shared_out_second,
    expert_in_weight,
    expert_in_first,
    expert_in_second,
    expert_out_weight,
    expert_out_first,
    expert_out_second,
):
    rows, D = patches.shape
    width = lax.axis_size("mp")
    n_dp = lax.axis_size("dp")
    devices = width * n_dp
    group = rows * width
    capacity = 5 * group // 16
    heads_here = H // width
    model_rank = lax.axis_index("mp")
    item_count = lengths.shape[1]
    hidden = shared_in_weight.shape[1]
    ada_cols = ada_weight.shape[1]
    router_cols = router_weight.shape[0]

    out_slab = jnp.concatenate(
        [
            jnp.swapaxes(expert_out_weight.astype(bf16), 1, 2),
            shared_out_weight.astype(bf16).T[None],
        ],
        axis=0,
    )
    in_slab = jnp.concatenate(
        [expert_in_weight.astype(bf16), shared_in_weight.astype(bf16)[None]], axis=0
    )
    out_t = lax.all_gather(out_slab, "dp", axis=1, tiled=True)
    patches_line = Gather(after(patches, out_slab))
    proj_line = Gather(proj_weight.astype(bf16).T)
    cond_all = phase(
        [patches_line, proj_line], lax.all_gather(conditioning, "dp", axis=0, tiled=True)
    )
    cond_act = jax.nn.silu(cond_all.astype(f32)).astype(bf16)
    columns = jnp.dot(cond_act, ada_weight.astype(bf16), preferred_element_type=f32)
    columns = jnp.repeat(columns.reshape(n_dp, item_count * ada_cols), width, axis=0)
    router_low = router_weight.astype(bf16).astype(f32)
    payload = jnp.concatenate(
        [columns, jnp.broadcast_to(router_low[None], (devices, router_cols))], axis=1
    )
    received = phase(
        [patches_line, proj_line], lax.all_to_all(payload, ("dp", "mp"), 0, 0, tiled=True)
    )
    qkv_here = lax.all_gather(
        after(qkv_weight.astype(bf16), received), "dp", axis=0, tiled=True
    )
    modulation = (
        received[:, : item_count * ada_cols]
        .reshape(devices, item_count, ada_cols)
        .transpose(1, 0, 2)
        .reshape(item_count, devices * ada_cols)
    )
    router_matrix = received[:, item_count * ada_cols :].reshape(D, E).astype(bf16)
    qkv_wide = jnp.pad(qkv_here.reshape(D, heads_here * 3, HD), ((0, 0), (0, 0), (0, LANES - HD)))
    qkv_wide = qkv_wide.reshape(D, heads_here * 3 * LANES)

    bounds = jnp.cumsum(lengths[0])
    places = jnp.arange(group, dtype=jnp.int32)
    segment = jnp.sum((places[:, None] >= bounds[None, :]).astype(jnp.int32), axis=1)
    segment_column = segment[:, None]
    segment_mine = lax.dynamic_slice_in_dim(segment_column, model_rank * rows, rows, 0)
    start, kind = key_windows(lengths[0], group)

    chosen = routes[:, :, None] == jnp.arange(E, dtype=jnp.int32)[None, None, :]
    names = chosen.any(axis=1)
    below = (places[:, None] > places[None, :]).astype(bf16)
    earlier = jnp.dot(below, names.astype(bf16), preferred_element_type=f32).astype(jnp.int32)
    place_of = jnp.where(names, earlier, -1).T
    picked = routes * capacity + jnp.sum(jnp.where(chosen, earlier[:, None, :], 0), axis=2)
    names_low = jnp.pad(names.astype(bf16), ((0, 0), (0, LANES - E)))
    lane = jnp.arange(qkv_wide.shape[1], dtype=jnp.int32)
    item, role = lane % LANES - HD, lane // LANES % 3
    same = segment[:, None] == item[None, :]
    marks = jnp.where(
        same, jnp.where(role == 0, FAR, 0.0)[None, :], jnp.where(role == 1, -FAR, 0.0)[None, :]
    )
    marks = jnp.where(((item >= 0) & (item < item_count))[None, :], marks, 0.0)
    modulation, router_matrix, qkv_wide, place_of, picked = phase(
        [patches_line, proj_line], (modulation, router_matrix, qkv_wide, place_of, picked)
    )

    cot_line = Gather(after(cotangent, patches_line.ups[-1]))
    patches_all, h_one_all = norm_one(patches_line.blocks(), modulation, segment_column)
    proj_rows = proj_line.whole(axis=1)
    qkv = (jnp.dot(h_one_all, qkv_wide, preferred_element_type=f32) + marks).astype(bf16)
    qkv, proj_rows = phase([cot_line], (qkv, proj_rows))
    (mixed_here, logs), out_t = phase([cot_line], (attend(qkv, start, kind), out_t))
    in_w = lax.all_gather(after(in_slab, out_t), "dp", axis=1, tiled=True)
    mixed_line = Gather(mixed_here)
    half = proj_rows.shape[1] // 2
    proj_first_half = phase(
        [cot_line, mixed_line], lax.all_gather(proj_rows[:, :half], "dp", axis=0, tiled=True)
    )
    gate_two = modulation[:, 5 * D :]
    gate_rows = functools.reduce(
        lambda kept, i: jnp.where(segment_column >= i, gate_two[i : i + 1], kept),
        range(1, item_count),
        gate_two[0:1],
    )
    grad_branch = (gate_rows * cot_line.whole().astype(f32)).astype(bf16)
    branch_slots, named_slots, back_slots, back_shared = phase(
        [mixed_line], experts_before(place_of, names_low, grad_branch, out_t, capacity)
    )
    proj_other_half = phase(
        [mixed_line], lax.all_gather(proj_rows[:, half:], "dp", axis=0, tiled=True)
    )
    proj = jnp.concatenate([proj_first_half, proj_other_half], axis=1).T
    h_two, x_one_mine, attn_mine, mixed_mine = norm_two(
        mixed_line.blocks(), patches_all, proj, modulation, segment_column
    )

    (
        dispatched,
        expert_act,
        grad_expert_pre,
        grad_res,
        gates,
        shared_act,
        grad_shared_pre,
        grad_logits,
        grad_h_two,
    ) = experts_main(
        place_of,
        picked,
        h_two,
        in_w,
        router_matrix,
        branch_slots,
        named_slots,
        back_slots,
        back_shared,
    )
    two_line = Scatter(grad_h_two)
    grad_out_slab = phase(
        [two_line], slab_product(grad_res, expert_act, grad_branch, shared_act, "grad_out")
    )
    grad_out_mine = lax.psum_scatter(grad_out_slab, "dp", scatter_dimension=1, tiled=True)
    grad_in_slab = phase(
        [two_line], slab_product(dispatched, grad_expert_pre, h_two, grad_shared_pre, "grad_in")
    )
    grad_router = phase(
        [two_line],
        jnp.einsum("gd,eg->de", h_two.astype(f32), grad_logits, precision=highest),
    )
    grad_x_one, grad_attn, grad_mixed_mine, sums_two = back_two(
        two_line.terms(), x_one_mine, attn_mine, cotangent, proj, modulation, segment_mine
    )
    grad_mixed, mlp_part = phase(
        [],
        (
            lax.all_to_all(
                grad_mixed_mine.reshape(width, heads_here * HD, rows), "mp", 0, 0, tiled=True
            ),
            experts_out(
                picked, after(gates, grad_mixed_mine), expert_act, out_t, shared_act
            ),
        ),
    )
    grad_mixed = grad_mixed.transpose(1, 0, 2).reshape(heads_here * HD, group)
    mlp_line = Scatter(mlp_part)
    grad_proj_t = jnp.einsum("gd,cg->dc", grad_attn, mixed_mine, preferred_element_type=f32)
    proj_sums = Scatter(grad_proj_t.astype(bf16), axis=1)
    grad_qkv, grad_out_mine = phase(
        [mlp_line, proj_sums], (attend_back(qkv, grad_mixed, logs, start, kind), grad_out_mine)
    )
    grad_in_mine = lax.psum_scatter(
        after(grad_in_slab, grad_out_mine), "dp", scatter_dimension=1, tiled=True
    )
    partial = phase(
        [mlp_line, proj_sums],
        jnp.einsum("gc,dc->gd", grad_qkv, qkv_wide, preferred_element_type=f32).astype(bf16),
    )
    one_line = Scatter(partial)
    grad_qkv_weight = jnp.einsum("gd,gc->dc", h_one_all, grad_qkv, preferred_element_type=f32)
    grad_qkv_weight = grad_qkv_weight.reshape(D, heads_here * 3, LANES)[:, :, :HD]
    grad_qkv_weight = phase(
        [one_line, mlp_line, proj_sums], grad_qkv_weight.reshape(D, heads_here * 3 * HD).astype(bf16)
    )
    result, sums_gate = phase(
        [one_line], outcome(mlp_line.terms(), x_one_mine, cotangent, modulation, segment_mine)
    )
    grad_attn_slab, grad_in_mine = phase(
        [one_line],
        (
            jnp.concatenate([grad_qkv_weight, proj_sums.total().astype(bf16)], axis=1),
            grad_in_mine,
        ),
    )
    grad_attn_mine = lax.psum_scatter(
        after(grad_attn_slab, grad_in_mine), "dp", scatter_dimension=0, tiled=True
    ).astype(f32)
    patch_grad, sums_one = back_one(
        one_line.terms(), patches, grad_x_one, modulation, segment_mine
    )
    grad_modulation = jnp.concatenate([sums_one, sums_two, sums_gate], axis=1)
    payload = jnp.concatenate(
        [
            grad_modulation.reshape(item_count, devices, ada_cols)
            .transpose(1, 0, 2)
            .reshape(devices, item_count * ada_cols),
            grad_router.reshape(devices, router_cols),
        ],
        axis=1,
    )
    received = lax.all_to_all(payload, ("dp", "mp"), 0, 0, tiled=True)
    router_grad = jnp.sum(received[:, item_count * ada_cols :], axis=0)
    columns = jnp.sum(
        received[:, : item_count * ada_cols].reshape(n_dp, width, item_count, ada_cols), axis=1
    ).reshape(n_dp * item_count, ada_cols)
    ada_grad = jnp.einsum("id,ic->dc", cond_act.astype(f32), columns, precision=highest)
    grad_out_mine, grad_in_mine = grad_out_mine.astype(f32), grad_in_mine.astype(f32)

    qkv_cols = qkv_weight.shape[1]
    gradients = (
        ada_grad,
        router_grad,
        grad_attn_mine[:, :qkv_cols],
        grad_attn_mine[:, qkv_cols:].T,
        grad_in_mine[E],
        grad_out_mine[E].T,
        grad_in_mine[:E],
        jnp.swapaxes(grad_out_mine[:E], 1, 2),
    )
    states_of = (
        (ada_weight, ada_first, ada_second),
        (router_weight, router_first, router_second),
        (qkv_weight, qkv_first, qkv_second),
        (proj_weight, proj_first, proj_second),
        (shared_in_weight, shared_in_first, shared_in_second),
        (shared_out_weight, shared_out_first, shared_out_second),
        (expert_in_weight, expert_in_first, expert_in_second),
        (expert_out_weight, expert_out_first, expert_out_second),
    )
    total_hidden = float(hidden * width)
    fan_ins = (D, D, D, 8.0 * D / group, D, total_hidden, D, total_hidden)
    updates = []
    for (master, first, second), gradient, fan_in in zip(states_of, gradients, fan_ins):
        updates.extend(adamw_update(master, first, second, gradient, float(fan_in)))
    return tuple([result, patch_grad] + updates)


def solution(mesh):
    tokens, data = P(("dp", "mp"), None), P("dp", None)
    ada, router = P(None, ("dp", "mp")), P(("dp", "mp"))
    deep, wide = P("dp", "mp"), P("mp", "dp")
    deep_experts, wide_experts = P(None, "dp", "mp"), P(None, "mp", "dp")
    kinds = (ada, router, deep, wide, deep, wide, deep_experts, wide_experts)
    in_specs = (tokens, tokens, data, data, data) + tuple(k for k in kinds for _ in range(3))
    out_specs = (tokens, tokens) + tuple(k for k in kinds for _ in range(4))
    return jax.shard_map(body, mesh=mesh, in_specs=in_specs, out_specs=out_specs, check_vma=False)
```

```python
import functools
import math

import jax
import jax.numpy as jnp
import numpy as np
from jax import lax
from jax.experimental import pallas as pl
from jax.experimental.pallas import tpu as pltpu
from jax.sharding import PartitionSpec as P

H = 12
HD = 64
E = 8
STEP = 10

beta_one = 0.9
beta_two = 0.95
epsilon = 1e-08
weight_decay = 0.1
norm_floor = 1e-06
highest = lax.Precision.HIGHEST
f32 = jnp.float32
bf16 = jnp.bfloat16


def norm_parts(values):
    centred = values - jnp.mean(values, axis=1, keepdims=True)
    inverse = lax.rsqrt(jnp.mean(centred * centred, axis=1, keepdims=True) + norm_floor)
    return centred * inverse, inverse


def norm_back(normed, inverse, gradient):
    first = jnp.mean(gradient, axis=1, keepdims=True)
    second = jnp.mean(gradient * normed, axis=1, keepdims=True)
    return inverse * (gradient - first - normed * second)


def after(values, *earlier):
    return lax.optimization_barrier((values, earlier))[0]


class Gather:
    def __init__(self, block):
        self.ups, self.downs = [block], [block]

    def send(self):
        width, step = lax.axis_size("mp"), len(self.ups)
        up_pairs = [(i, i + 1) for i in range(step - 1, width - 1)]
        down_pairs = [(i + 1, i) for i in range(width - step)]
        return (
            lax.ppermute(self.ups[-1], "mp", up_pairs),
            lax.ppermute(self.downs[-1], "mp", down_pairs),
        )

    def take(self, pair):
        self.ups.append(pair[0])
        self.downs.append(pair[1])

    def arrays(self):
        return self.ups + self.downs[1:]

    def ring(self, part):
        width, rank = lax.axis_size("mp"), lax.axis_index("mp")
        pairs = zip(range(1, width), self.ups[1:], reversed(self.downs[1:]))
        return [self.ups[0][part]] + [jnp.where(rank >= i, u[part], d[part]) for i, u, d in pairs]


class Scatter:
    def __init__(self, partial):
        self.partial, self.step = partial, 1
        self.up, self.down = None, None

    def part(self, index):
        extent = self.partial.shape[0] // lax.axis_size("mp")
        return self.partial[index * extent : (index + 1) * extent]

    def send(self):
        width, step = lax.axis_size("mp"), self.step
        up, down = self.part(step), self.part(width - step)
        if self.up is not None:
            up = (up.astype(f32) + self.up.astype(f32)).astype(bf16)
            down = (down.astype(f32) + self.down.astype(f32)).astype(bf16)
        return (
            lax.ppermute(up, "mp", [(i, i + 1) for i in range(step)]),
            lax.ppermute(down, "mp", [(i, i - 1) for i in range(width - step, width)]),
        )

    def take(self, pair):
        self.up, self.down = pair
        self.step += 1

    def terms(self):
        return self.part(0), self.up, self.down


def phase(transfers, work):
    pairs, work = lax.optimization_barrier(([t.send() for t in transfers], work))
    for transfer, pair in zip(transfers, pairs):
        transfer.take(pair)
    return work


LANES = 128
VMEM = 60 * 2**20
Q_BLOCK = 256
FAR = 2.0**50
NT = (((1,), (1,)), ((), ()))
TN = (((0,), (0,)), ((), ()))
NN = (((1,), (0,)), ((), ()))


def dot(a, b, dims=NN):
    return lax.dot_general(a, b, dims, preferred_element_type=f32)


def key_widths(group):
    return sorted({min(w, group) for w in (512, 768, 1024, group)})


def key_windows(lengths, group):
    ends = jnp.cumsum(lengths)
    begins = ends - lengths
    first = jnp.arange(group // Q_BLOCK, dtype=jnp.int32) * Q_BLOCK
    last = first + Q_BLOCK - 1
    low = jnp.max(jnp.where(begins[None, :] <= first[:, None], begins[None, :], 0), axis=1)
    high = jnp.min(jnp.where(ends[None, :] > last[:, None], ends[None, :], group), axis=1)
    low = low // LANES * LANES
    widths = jnp.array(key_widths(group), jnp.int32)
    kind = jnp.sum((high - low)[:, None] > widths[None, :], axis=1).astype(jnp.int32)
    return jnp.minimum(low, group - widths[kind]).astype(jnp.int32), kind


def attend_kernel(start_ref, kind_ref, qkv_ref, mixed_ref, log_ref, *, group):
    block = pl.program_id(1)
    rows = pl.ds(pl.multiple_of(block * Q_BLOCK, Q_BLOCK), Q_BLOCK)
    query = qkv_ref[rows, 0:LANES] * jnp.asarray(HD**-0.5, bf16)
    for index, extent in enumerate(key_widths(group)):

        @pl.when(kind_ref[block] == index)
        def _():
            keys = pl.ds(pl.multiple_of(start_ref[block], LANES), extent)
            scores = dot(qkv_ref[keys, LANES : 2 * LANES], query, NT)
            peak = jnp.max(scores, axis=0, keepdims=True)
            exps = jnp.exp(scores - peak)
            total = jnp.sum(exps, axis=0, keepdims=True)
            probs = (exps * (1.0 / total)).astype(bf16)
            mixed = dot(qkv_ref[keys, 2 * LANES : 3 * LANES], probs, TN)
            mixed_ref[...] = mixed[:HD].astype(bf16)
            log_ref[...] = (peak + jnp.log(total))[None]


def attend(qkv, start, kind):
    group = qkv.shape[0]
    heads = qkv.shape[1] // (3 * LANES)
    blocks = group // Q_BLOCK
    return pl.pallas_call(
        functools.partial(attend_kernel, group=group),
        out_shape=(
            jax.ShapeDtypeStruct((heads * HD, group), bf16),
            jax.ShapeDtypeStruct((heads, 1, group), f32),
        ),
        grid_spec=pltpu.PrefetchScalarGridSpec(
            num_scalar_prefetch=2,
            grid=(heads, blocks),
            in_specs=[pl.BlockSpec((group, 3 * LANES), lambda h, i, *_: (0, h))],
            out_specs=(
                pl.BlockSpec((HD, Q_BLOCK), lambda h, i, *_: (h, i)),
                pl.BlockSpec((1, 1, Q_BLOCK), lambda h, i, *_: (h, 0, i)),
            ),
        ),
        compiler_params=pltpu.CompilerParams(vmem_limit_bytes=VMEM),
        cost_estimate=pl.CostEstimate(
            flops=16 * heads * group * group * HD, bytes_accessed=6 * 2**20, transcendentals=heads * group * group
        ),
        name="attend",
    )(start, kind, qkv)


def attend_back_kernel(
    start_ref, kind_ref, qkv_ref, grad_ref, log_ref, out_ref, key_total, value_total, *, group
):
    block = pl.program_id(1)

    @pl.when(block == 0)
    def _():
        key_total[...] = jnp.zeros_like(key_total)
        value_total[...] = jnp.zeros_like(value_total)

    rows = pl.ds(pl.multiple_of(block * Q_BLOCK, Q_BLOCK), Q_BLOCK)
    scaling = HD**-0.5
    query = qkv_ref[rows, 0:LANES] * jnp.asarray(scaling, bf16)
    grad = grad_ref[...]
    kept = lax.broadcasted_iota(jnp.int32, (1, LANES), 1) < HD
    for index, extent in enumerate(key_widths(group)):

        @pl.when(kind_ref[block] == index)
        def _():
            keys = pl.ds(pl.multiple_of(start_ref[block], LANES), extent)
            key_rows = qkv_ref[keys, LANES : 2 * LANES]
            value_rows = qkv_ref[keys, 2 * LANES : 3 * LANES]
            probs = jnp.exp(dot(key_rows, query, NT) - log_ref[0])
            grad_probs = dot(value_rows[:, :HD], grad)
            middle = jnp.sum(probs * grad_probs, axis=0, keepdims=True)
            grad_scores = (probs * (grad_probs - middle)).astype(bf16)
            value_total[keys, :HD] += dot(probs.astype(bf16), grad, NT)
            key_total[keys, :] += dot(grad_scores, query)
            grad_query = dot(key_rows, grad_scores, TN).T * scaling
            out_ref[rows, 0:LANES] = jnp.where(kept, grad_query, 0.0).astype(bf16)

    @pl.when(block == pl.num_programs(1) - 1)
    def _():
        out_ref[:, LANES : 2 * LANES] = jnp.where(kept, key_total[...], 0.0).astype(bf16)
        out_ref[:, 2 * LANES : 3 * LANES] = value_total[...].astype(bf16)


def attend_back(qkv, grad_mixed, logs, start, kind):
    group = qkv.shape[0]
    heads = qkv.shape[1] // (3 * LANES)
    blocks = group // Q_BLOCK
    return pl.pallas_call(
        functools.partial(attend_back_kernel, group=group),
        out_shape=jax.ShapeDtypeStruct(qkv.shape, bf16),
        grid_spec=pltpu.PrefetchScalarGridSpec(
            num_scalar_prefetch=2,
            grid=(heads, blocks),
            in_specs=[
                pl.BlockSpec((group, 3 * LANES), lambda h, i, *_: (0, h)),
                pl.BlockSpec((HD, Q_BLOCK), lambda h, i, *_: (h, i)),
                pl.BlockSpec((1, 1, Q_BLOCK), lambda h, i, *_: (h, 0, i)),
            ],
            out_specs=pl.BlockSpec((group, 3 * LANES), lambda h, i, *_: (0, h)),
            scratch_shapes=[pltpu.VMEM((group, LANES), f32), pltpu.VMEM((group, LANES), f32)],
        ),
        compiler_params=pltpu.CompilerParams(vmem_limit_bytes=VMEM),
        cost_estimate=pl.CostEstimate(
            flops=40 * heads * group * group * HD, bytes_accessed=12 * 2**20, transcendentals=heads * group * group
        ),
        name="attend_back",
    )(start, kind, qkv, grad_mixed, logs)


def item_rows(table_ref, term, width, segment, items):
    columns = slice(term * width, (term + 1) * width)
    rows = table_ref[0:1, columns]
    for item in range(1, items):
        rows = jnp.where(segment >= item, table_ref[item : item + 1, columns], rows)
    return rows


def item_sums(values, segment, items):
    return jnp.concatenate(
        [jnp.sum(jnp.where(segment == item, values, 0.0), axis=0, keepdims=True) for item in range(items)], axis=0
    )


def chosen_block(refs, place, width_mp, rank):
    if place == 0:
        return refs[0][...]
    return jnp.where(rank >= place, refs[place][...], refs[2 * width_mp - 1 - place][...])


def placed(width_mp):
    return lambda i, rank: (lax.rem(rank[0] - i + width_mp, width_mp), 0)


def plain(*shape):
    return pl.BlockSpec(shape, lambda i, rank: (0,) * len(shape))


def image_marks(heads, items):
    marks = np.zeros((items, heads, 3, LANES), np.float32)
    for image in range(items):
        for item in range(items):
            if image == item:
                marks[image, :, 0, HD + item] = FAR
            else:
                marks[image, :, 1, HD + item] = -FAR
    return marks.reshape(items, heads * 3 * LANES)


def norm_one_kernel(*refs, width_mp, items):
    rank_ref, segment_ref, table_ref, marks_ref, weight_ref = refs[:5]
    block_refs, (rows_ref, h_ref, qkv_ref, wide_ref) = refs[5:-4], refs[-4:]
    segment = segment_ref[...]
    width = rows_ref.shape[1]

    @pl.when(pl.program_id(0) == 0)
    def _():
        wide_ref[...] = jnp.zeros_like(wide_ref)
        for part in range(weight_ref.shape[1] // HD):
            wide_ref[:, part * LANES : part * LANES + HD] = weight_ref[:, part * HD : (part + 1) * HD]

    for place in range(width_mp):

        @pl.when(pl.program_id(0) == place)
        def _():
            rows_ref[...] = chosen_block(block_refs, place, width_mp, rank_ref[0])

    normed, _ = norm_parts(rows_ref[...].astype(f32))
    shift = item_rows(table_ref, 0, width, segment, items)
    scale = item_rows(table_ref, 1, width, segment, items)
    h_one = (normed * (1.0 + scale) + shift).astype(bf16)
    h_ref[...] = h_one
    marks = item_rows(marks_ref, 0, qkv_ref.shape[1], segment, items)
    qkv_ref[...] = (dot(h_one, wide_ref[...]) + marks).astype(bf16)


def norm_one(line, rows, table, segment, weight):
    arrays = line.arrays()
    width_mp, width, items = (len(arrays) + 1) // 2, arrays[0].shape[1], table.shape[0]
    heads = weight.shape[1] // (3 * HD)
    wide = heads * 3 * LANES
    marks = jnp.asarray(image_marks(heads, items))
    order = placed(width_mp)
    return pl.pallas_call(
        functools.partial(norm_one_kernel, width_mp=width_mp, items=items),
        out_shape=(
            jax.ShapeDtypeStruct((rows * width_mp, width), bf16),
            jax.ShapeDtypeStruct((rows * width_mp, width), bf16),
            jax.ShapeDtypeStruct((rows * width_mp, wide), bf16),
            jax.ShapeDtypeStruct((width, wide), bf16),
        ),
        grid_spec=pltpu.PrefetchScalarGridSpec(
            num_scalar_prefetch=1,
            grid=(width_mp,),
            in_specs=[pl.BlockSpec((rows, 1), order), plain(*table.shape), plain(*marks.shape), plain(*weight.shape)]
            + [plain(rows, width)] * len(arrays),
            out_specs=(
                pl.BlockSpec((rows, width), order),
                pl.BlockSpec((rows, width), order),
                pl.BlockSpec((rows, wide), order),
                plain(width, wide),
            ),
        ),
        compiler_params=pltpu.CompilerParams(vmem_limit_bytes=VMEM),
        cost_estimate=pl.CostEstimate(flops=3 * 10**9, bytes_accessed=15 * 2**20, transcendentals=0),
        name="norm_one",
    )(lax.axis_index("mp").reshape(1), segment, table, marks, weight, *arrays)


def gated_kernel(*refs, width_mp, items):
    rank_ref, segment_ref, table_ref = refs[:3]
    block_refs, out_ref = refs[3:-1], refs[-1]
    segment = segment_ref[...]
    width = out_ref.shape[1]
    for place in range(width_mp):

        @pl.when(pl.program_id(0) == place)
        def _():
            rows = chosen_block(block_refs, place, width_mp, rank_ref[0]).astype(f32)
            out_ref[...] = (item_rows(table_ref, 5, width, segment, items) * rows).astype(bf16)


def by_rows(kernel, outputs, line, rows, table, segment, name):
    arrays = line.arrays()
    width_mp, width, items = (len(arrays) + 1) // 2, arrays[0].shape[1], table.shape[0]
    order = placed(width_mp)
    return pl.pallas_call(
        functools.partial(kernel, width_mp=width_mp, items=items),
        out_shape=(jax.ShapeDtypeStruct((rows * width_mp, width), bf16),) * outputs,
        grid_spec=pltpu.PrefetchScalarGridSpec(
            num_scalar_prefetch=1,
            grid=(width_mp,),
            in_specs=[pl.BlockSpec((rows, 1), order), plain(*table.shape)]
            + [plain(rows, width)] * len(arrays),
            out_specs=(pl.BlockSpec((rows, width), order),) * outputs,
        ),
        compiler_params=pltpu.CompilerParams(vmem_limit_bytes=VMEM),
        cost_estimate=pl.CostEstimate(flops=2 * 10**7, bytes_accessed=8 * 2**20, transcendentals=0),
        name=name,
    )(lax.axis_index("mp").reshape(1), segment, table, *arrays)


def norm_two_kernel(*refs, width_mp, items):
    rank_ref, segment_ref, table_ref, rows_ref, turned_ref = refs[:5]
    mixed_refs = refs[5:-6]
    h_ref, x_mine_ref, attn_mine_ref, mixed_mine_ref, proj_ref, proj_scratch = refs[-6:]
    step = pl.program_id(0)
    rank = rank_ref[0]
    segment = segment_ref[...]
    width = rows_ref.shape[1]
    heads = mixed_refs[0].shape[0]

    @pl.when(step == 0)
    def _():
        proj_scratch[...] = turned_ref[...].T
        proj_ref[...] = proj_scratch[...]

    attn = jnp.zeros(rows_ref.shape, f32)
    for place in range(width_mp):
        here = slice(place * heads, (place + 1) * heads)
        mixed = chosen_block(mixed_refs, place, width_mp, rank)
        attn += dot(mixed, proj_scratch[here, :], TN)

        @pl.when(step == rank)
        def _():
            mixed_mine_ref[here, :] = mixed

    x_one = rows_ref[...].astype(f32) + item_rows(table_ref, 2, width, segment, items) * attn

    @pl.when(step == rank)
    def _():
        x_mine_ref[...] = x_one
        attn_mine_ref[...] = attn

    normed, _ = norm_parts(x_one)
    shift = item_rows(table_ref, 3, width, segment, items)
    scale = item_rows(table_ref, 4, width, segment, items)
    h_ref[...] = (normed * (1.0 + scale) + shift).astype(bf16)


def norm_two(line, patches, proj_t, table, segment):
    arrays = line.arrays()
    width_mp, (heads, group) = (len(arrays) + 1) // 2, arrays[0].shape
    rows, width, items = group // width_mp, patches.shape[1], table.shape[0]
    every = heads * width_mp
    return pl.pallas_call(
        functools.partial(norm_two_kernel, width_mp=width_mp, items=items),
        out_shape=(
            jax.ShapeDtypeStruct((group, width), bf16),
            jax.ShapeDtypeStruct((rows, width), f32),
            jax.ShapeDtypeStruct((rows, width), f32),
            jax.ShapeDtypeStruct((every, rows), bf16),
            jax.ShapeDtypeStruct((every, width), bf16),
        ),
        grid_spec=pltpu.PrefetchScalarGridSpec(
            num_scalar_prefetch=1,
            grid=(width_mp,),
            in_specs=[
                pl.BlockSpec((rows, 1), lambda i, rank: (i, 0)),
                plain(*table.shape),
                pl.BlockSpec((rows, width), lambda i, rank: (i, 0)),
                plain(*proj_t.shape),
            ]
            + [pl.BlockSpec((heads, rows), lambda i, rank: (0, i))] * len(arrays),
            out_specs=(
                pl.BlockSpec((rows, width), lambda i, rank: (i, 0)),
                plain(rows, width),
                plain(rows, width),
                plain(every, rows),
                plain(every, width),
            ),
            scratch_shapes=[pltpu.VMEM((every, width), bf16)],
        ),
        compiler_params=pltpu.CompilerParams(vmem_limit_bytes=VMEM),
        cost_estimate=pl.CostEstimate(flops=2 * 10**9, bytes_accessed=13 * 2**20, transcendentals=0),
        name="norm_two",
    )(lax.axis_index("mp").reshape(1), segment, table, patches, proj_t, *arrays)


def product_kernel(rank_ref, a_ref, b_ref, part_ref, out_ref):
    rows = a_ref.shape[0]
    out_ref[0:rows, :] = dot(a_ref[...], b_ref[...], NT).astype(bf16)
    out_ref[rows:, :] = part_ref[0]


def ring_product(a, b, parts):
    width_mp, extra, width = parts.shape
    rows = a.shape[0] // width_mp
    return pl.pallas_call(
        product_kernel,
        out_shape=jax.ShapeDtypeStruct((a.shape[0] + width_mp * extra, width), bf16),
        grid_spec=pltpu.PrefetchScalarGridSpec(
            num_scalar_prefetch=1,
            grid=(width_mp,),
            in_specs=[
                pl.BlockSpec((rows, a.shape[1]), placed(width_mp)),
                plain(*b.shape),
                pl.BlockSpec((1, extra, width), lambda i, rank: (i, 0, 0)),
            ],
            out_specs=pl.BlockSpec((rows + extra, width), lambda i, rank: (i, 0)),
        ),
        compiler_params=pltpu.CompilerParams(vmem_limit_bytes=VMEM),
        cost_estimate=pl.CostEstimate(flops=3 * 10**9, bytes_accessed=8 * 2**20, transcendentals=0),
        name="grad_h_one",
    )(lax.axis_index("mp").reshape(1), a, b, parts)


def back_two_kernel(
    rank_ref,
    segment_ref,
    table_ref,
    own_ref,
    up_ref,
    down_ref,
    x_ref,
    attn_ref,
    cot_ref,
    proj_ref,
    grad_x_ref,
    grad_attn_ref,
    grad_mixed_ref,
    sums_ref,
    *,
    width_mp,
    items,
):
    segment = segment_ref[...]
    width = x_ref.shape[1]
    heads = proj_ref.shape[0] // width_mp
    grad = own_ref[...].astype(f32) + up_ref[...].astype(f32) + down_ref[...].astype(f32)
    normed, inverse = norm_parts(x_ref[...])
    scale = item_rows(table_ref, 4, width, segment, items)
    grad_x = cot_ref[...].astype(f32) + norm_back(normed, inverse, grad * (1.0 + scale))
    grad_x_ref[...] = grad_x
    grad_attn = (item_rows(table_ref, 2, width, segment, items) * grad_x).astype(bf16)
    grad_attn_ref[...] = grad_attn
    for place in range(width_mp):
        owner = lax.rem(rank_ref[0] - place + width_mp, width_mp)
        part = dot(proj_ref[place * heads : (place + 1) * heads, :], grad_attn, NT)
        grad_mixed_ref[owner] = part.astype(bf16)
    sums_ref[:, 0:width] = item_sums(grad_x * attn_ref[...], segment, items)
    sums_ref[:, width : 2 * width] = item_sums(grad, segment, items)
    sums_ref[:, 2 * width :] = item_sums(grad * normed, segment, items)


def back_two(terms, x_one, attn, cotangent, proj, table, segment):
    rows, width = x_one.shape
    items, width_mp = table.shape[0], lax.axis_size("mp")
    shapes = (
        jax.ShapeDtypeStruct((rows, width), f32),
        jax.ShapeDtypeStruct((rows, width), bf16),
        jax.ShapeDtypeStruct((width_mp, proj.shape[0] // width_mp, rows), bf16),
        jax.ShapeDtypeStruct((items, 3 * width), f32),
    )
    operands = (segment, table, *(t for t in terms), x_one, attn, cotangent, proj)
    return pl.pallas_call(
        functools.partial(back_two_kernel, width_mp=width_mp, items=items),
        out_shape=shapes,
        grid_spec=pltpu.PrefetchScalarGridSpec(
            num_scalar_prefetch=1,
            grid=(1,),
            in_specs=[plain(*o.shape) for o in operands],
            out_specs=tuple(plain(*o.shape) for o in shapes),
        ),
        compiler_params=pltpu.CompilerParams(vmem_limit_bytes=VMEM),
        cost_estimate=pl.CostEstimate(flops=10**9, bytes_accessed=9 * 2**20, transcendentals=0),
        name="back_two",
    )(lax.axis_index("mp").reshape(1), *operands)


def back_one_kernel(
    segment_ref,
    table_ref,
    own_ref,
    up_ref,
    down_ref,
    patches_ref,
    grad_x_ref,
    grad_ref,
    sums_ref,
    *,
    items,
):
    segment = segment_ref[...]
    width = patches_ref.shape[1]
    grad = own_ref[...].astype(f32) + up_ref[...].astype(f32) + down_ref[...].astype(f32)
    normed, inverse = norm_parts(patches_ref[...].astype(f32))
    scale = item_rows(table_ref, 1, width, segment, items)
    grad_ref[...] = (grad_x_ref[...] + norm_back(normed, inverse, grad * (1.0 + scale))).astype(bf16)
    sums_ref[:, 0:width] = item_sums(grad, segment, items)
    sums_ref[:, width:] = item_sums(grad * normed, segment, items)


def back_one(terms, patches, grad_x, table, segment):
    rows, width = patches.shape
    items = table.shape[0]
    shapes = (
        jax.ShapeDtypeStruct((rows, width), bf16),
        jax.ShapeDtypeStruct((items, 2 * width), f32),
    )

    def single(*shape):
        return pl.BlockSpec(shape, lambda i: (0,) * len(shape))

    return pl.pallas_call(
        functools.partial(back_one_kernel, items=items),
        out_shape=shapes,
        grid=(1,),
        in_specs=[single(*segment.shape), single(*table.shape)] + [single(rows, width)] * 5,
        out_specs=tuple(single(*o.shape) for o in shapes),
        compiler_params=pltpu.CompilerParams(vmem_limit_bytes=VMEM),
        cost_estimate=pl.CostEstimate(flops=10**7, bytes_accessed=5 * 2**20, transcendentals=0),
        name="back_one",
    )(segment, table, *terms, patches, grad_x)


def outcome_kernel(
    segment_ref, table_ref, own_ref, up_ref, down_ref, x_ref, cot_ref, out_ref, sums_ref, *, items
):
    segment = segment_ref[...]
    width = x_ref.shape[1]
    branch = own_ref[...].astype(f32) + up_ref[...].astype(f32) + down_ref[...].astype(f32)
    gate = item_rows(table_ref, 5, width, segment, items)
    out_ref[...] = (x_ref[...] + gate * branch).astype(bf16)
    sums_ref[...] = item_sums(cot_ref[...].astype(f32) * branch, segment, items)


def outcome(terms, x_one, cotangent, table, segment):
    rows, width = x_one.shape
    items = table.shape[0]
    return pl.pallas_call(
        functools.partial(outcome_kernel, items=items),
        out_shape=(
            jax.ShapeDtypeStruct((rows, width), bf16),
            jax.ShapeDtypeStruct((items, width), f32),
        ),
        compiler_params=pltpu.CompilerParams(vmem_limit_bytes=VMEM),
        cost_estimate=pl.CostEstimate(flops=10**7, bytes_accessed=5 * 2**20, transcendentals=0),
        name="outcome",
    )(segment, table, *terms, x_one, cotangent)


def gelu_terms(before):
    slope = (2.0 / math.pi) ** 0.5
    square = before * before
    curve = jnp.tanh(slope * before * (1.0 + 0.044715 * square))
    half = 0.5 * (1.0 + curve)
    value = before * half
    derivative = half + (0.5 * slope) * before * (1.0 - curve * curve) * (1.0 + 0.134145 * square)
    return value, derivative


def slot_picks(place_row, capacity):
    slots = lax.broadcasted_iota(jnp.int32, (capacity, place_row.shape[1]), 0)
    return slots == place_row


def row_chunks(group):
    return [slice(first, first + 512) for first in range(0, group, 512)]


def before_kernel(
    place_ref, named_ref, branch_ref, weight_ref, *refs, count, shared
):
    slots_ref, named_slots_ref, back_ref = refs[-4:-1] if shared else refs[-3:]
    step = pl.program_id(0)

    @pl.when(step < count)
    def _():
        picks = slot_picks(place_ref[0], slots_ref.shape[1]).astype(bf16)
        slots = dot(picks, branch_ref[...]).astype(bf16)
        slots_ref[0] = slots
        named_slots_ref[0] = dot(picks, named_ref[...]).astype(bf16)
        back_ref[0] = dot(slots, weight_ref[0]).astype(bf16)

    if shared:

        @pl.when(step == count)
        def _():
            for chunk in row_chunks(branch_ref.shape[0]):
                refs[-1][chunk, :] = dot(branch_ref[chunk, :], weight_ref[0]).astype(bf16)


def whole(*shape):
    return pl.BlockSpec(shape, lambda *_: (0,) * len(shape), pipeline_mode=pl.Buffered(1))


def per_expert(experts, *shape):
    return pl.BlockSpec(
        (1,) + shape, lambda e, *_: (jnp.minimum(e, experts - 1),) + (0,) * len(shape)
    )


def per_slab(experts, *shape):
    return pl.BlockSpec((1,) + shape, lambda e, *_: (jnp.minimum(e, experts),) + (0,) * len(shape))


def experts_before(places, named, branch, out_t, capacity, first, held=None):
    group, width = branch.shape
    experts, hidden = out_t.shape[0] - 1, out_t.shape[2]
    base, count = (0, first) if held is None else (first, experts - first)
    shapes = (
        jax.ShapeDtypeStruct((experts, capacity, width), bf16),
        jax.ShapeDtypeStruct((experts, capacity, LANES), bf16),
        jax.ShapeDtypeStruct((experts, capacity, hidden), bf16),
    )

    def mine(*shape):
        return pl.BlockSpec(
            (1,) + shape, lambda e: (base + jnp.minimum(e, count - 1),) + (0,) * len(shape)
        )

    shared = held is not None
    return pl.pallas_call(
        functools.partial(before_kernel, count=count, shared=shared),
        out_shape=shapes + (jax.ShapeDtypeStruct((group, hidden), bf16),) * shared,
        grid=(count + shared,),
        in_specs=[
            mine(1, group),
            whole(group, LANES),
            whole(group, width),
            pl.BlockSpec((1, width, hidden), lambda e: (base + e, 0, 0)),
        ]
        + [pl.BlockSpec(memory_space=pl.ANY)] * (3 * shared),
        out_specs=(mine(capacity, width), mine(capacity, LANES), mine(capacity, hidden))
        + (whole(group, hidden),) * shared,
        input_output_aliases={4: 0, 5: 1, 6: 2} if shared else {},
        compiler_params=pltpu.CompilerParams(vmem_limit_bytes=VMEM),
        cost_estimate=pl.CostEstimate(
            flops=8 * 10**9, bytes_accessed=15 * 2**20, transcendentals=0
        ),
        name="experts_before",
    )(places.reshape(experts, 1, group), named, branch, out_t, *(held or ()))


def experts_kernel(
    rank_ref,
    place_ref,
    places_ref,
    picked_ref,
    rows_ref,
    weight_ref,
    router_ref,
    router_wide_ref,
    slots_ref,
    named_ref,
    back_ref,
    shared_back_ref,
    dispatched_ref,
    act_ref,
    grad_pre_ref,
    grad_res_ref,
    gate_ref,
    shared_act_ref,
    shared_grad_ref,
    grad_logits_ref,
    grad_rows_ref,
    grad_gates_ref,
    grad_slots_ref,
    high_ref,
    rest_ref,
    *,
    experts,
):
    step = pl.program_id(0)
    group = rows_ref.shape[0]
    capacity = slots_ref.shape[1]

    @pl.when(step < experts)
    def _():
        picks = slot_picks(place_ref[0], capacity)
        dispatched = dot(picks.astype(bf16), rows_ref[...]).astype(bf16)
        dispatched_ref[0] = dispatched
        pre = dot(dispatched, weight_ref[0])
        logits = dot(dispatched, router_wide_ref[...])
        lane = lax.broadcasted_iota(jnp.int32, logits.shape, 1)
        named = named_ref[0].astype(f32) > 0.0
        peak = jnp.max(jnp.where(named, logits, -jnp.inf), axis=1, keepdims=True)
        shares = jnp.where(named, jnp.exp(logits - peak), 0.0)
        total = jnp.sum(shares, axis=1, keepdims=True)
        own = jnp.sum(jnp.where(lane == step, shares, 0.0), axis=1, keepdims=True)
        gate = jnp.where(total > 0.0, own / jnp.maximum(total, 1.0), 0.0)
        gate_ref[0] = gate
        value, slope = gelu_terms(pre)
        act = value.astype(bf16)
        act_ref[0] = act
        back = back_ref[0].astype(f32)
        grad_pre = (gate * back * slope).astype(bf16)
        grad_pre_ref[0] = grad_pre
        grad_res_ref[0] = (gate * slots_ref[0].astype(f32)).astype(bf16)
        grad_gate = jnp.sum(back * act.astype(f32), axis=1, keepdims=True)
        grad_gates_ref[step] = jnp.sum(jnp.where(picks, grad_gate, 0.0), axis=0, keepdims=True)
        here = pl.ds(pl.multiple_of(step * capacity, capacity), capacity)
        grad_slots_ref[here, :] = dot(grad_pre, weight_ref[0], NT).astype(bf16)

    @pl.when(step == experts)
    def _():
        logits = dot(router_ref[...], rows_ref[...], NT)
        named = places_ref[...] >= 0
        peak = jnp.max(jnp.where(named, logits, -jnp.inf), axis=0, keepdims=True)
        shares = jnp.where(named, jnp.exp(logits - peak), 0.0)
        gates = shares / jnp.sum(shares, axis=0, keepdims=True)
        grad_gates = jnp.concatenate([grad_gates_ref[e] for e in range(experts)], axis=0)
        grad_logits = gates * (grad_gates - jnp.sum(gates * grad_gates, axis=0, keepdims=True))
        grad_logits_ref[...] = grad_logits
        high = grad_logits.astype(bf16)
        high_ref[...] = high
        rest_ref[...] = (grad_logits - high.astype(f32)).astype(bf16)

    @pl.when(step >= experts)
    def _():
        size = shared_act_ref.shape[0]
        here = pl.ds(pl.multiple_of((step - experts) * size, size), size)
        value, slope = gelu_terms(dot(rows_ref[here, :], weight_ref[0]))
        shared_act_ref[...] = value.astype(bf16)
        grad_pre = (shared_back_ref[...].astype(f32) * slope).astype(bf16)
        shared_grad_ref[...] = grad_pre
        total = dot(picked_ref[...], grad_slots_ref[...])
        total += dot(grad_pre, weight_ref[0], NT)
        total += dot(high_ref[:, here], router_ref[...], TN)
        total += dot(rest_ref[:, here], router_ref[...], TN)
        grad_rows_ref[...] = total.astype(bf16)


def row_block(experts, *shape):
    return pl.BlockSpec(shape, lambda e, *_: (jnp.maximum(e - experts, 0), 0))


def ring_block(experts, width_mp, *shape):
    def index(e, rank):
        return (lax.rem(rank[0] - jnp.maximum(e - experts, 0) + width_mp, width_mp), 0)

    return pl.BlockSpec(shape, index)


def experts_main(places, picked, h_two, in_w, router, slots, named, back, shared_back):
    group, width = h_two.shape
    experts, capacity, hidden = back.shape
    width_mp = lax.axis_size("mp")
    rows = group // width_mp
    slot_shape = jax.ShapeDtypeStruct((experts, capacity, width), bf16)
    unit_shape = jax.ShapeDtypeStruct((experts, capacity, hidden), bf16)
    return pl.pallas_call(
        functools.partial(experts_kernel, experts=experts),
        out_shape=(
            slot_shape,
            unit_shape,
            unit_shape,
            slot_shape,
            jax.ShapeDtypeStruct((experts, capacity, 1), f32),
            jax.ShapeDtypeStruct((group, hidden), bf16),
            jax.ShapeDtypeStruct((group, hidden), bf16),
            jax.ShapeDtypeStruct((experts, group), f32),
            jax.ShapeDtypeStruct((group, width), bf16),
        ),
        grid_spec=pltpu.PrefetchScalarGridSpec(
            num_scalar_prefetch=1,
            grid=(experts + width_mp,),
            in_specs=[
                per_expert(experts, 1, group),
                whole(experts, group),
                row_block(experts, rows, experts * capacity),
                whole(group, width),
                per_slab(experts, width, hidden),
                whole(experts, width),
                whole(width, LANES),
                per_expert(experts, capacity, width),
                per_expert(experts, capacity, LANES),
                per_expert(experts, capacity, hidden),
                row_block(experts, rows, hidden),
            ],
            out_specs=(
                per_expert(experts, capacity, width),
                per_expert(experts, capacity, hidden),
                per_expert(experts, capacity, hidden),
                per_expert(experts, capacity, width),
                per_expert(experts, capacity, 1),
                row_block(experts, rows, hidden),
                row_block(experts, rows, hidden),
                whole(experts, group),
                ring_block(experts, width_mp, rows, width),
            ),
            scratch_shapes=[
                pltpu.VMEM((experts, 1, group), f32),
                pltpu.VMEM((experts * capacity, width), bf16),
                pltpu.VMEM((experts, group), bf16),
                pltpu.VMEM((experts, group), bf16),
            ],
        ),
        compiler_params=pltpu.CompilerParams(vmem_limit_bytes=VMEM),
        cost_estimate=pl.CostEstimate(
            flops=32 * 10**9, bytes_accessed=50 * 2**20, transcendentals=5 * 10**6
        ),
        name="experts_main",
    )(
        lax.axis_index("mp").reshape(1),
        places.reshape(experts, 1, group),
        places,
        picked,
        h_two,
        in_w,
        router.T,
        jnp.pad(router, ((0, 0), (0, LANES - experts))),
        slots,
        named,
        back,
        shared_back,
    )


def slab_kernel(a_ref, b_ref, a_shared_ref, b_shared_ref, out_ref, *, experts):
    step = pl.program_id(0)

    @pl.when(step < experts)
    def _():
        out_ref[0] = dot(a_ref[0], b_ref[0], TN).astype(bf16)

    @pl.when(step == experts)
    def _():
        out_ref[0] = dot(a_shared_ref[...], b_shared_ref[...], TN).astype(bf16)


def slab_product(a, b, a_shared, b_shared, name):
    experts, capacity, width = a.shape
    hidden = b.shape[2]
    group = a_shared.shape[0]
    return pl.pallas_call(
        functools.partial(slab_kernel, experts=experts),
        out_shape=jax.ShapeDtypeStruct((experts + 1, width, hidden), bf16),
        grid=(experts + 1,),
        in_specs=[
            per_expert(experts, capacity, width),
            per_expert(experts, capacity, hidden),
            whole(group, width),
            whole(group, hidden),
        ],
        out_specs=per_slab(experts, width, hidden),
        compiler_params=pltpu.CompilerParams(vmem_limit_bytes=VMEM),
        cost_estimate=pl.CostEstimate(
            flops=7 * 10**9, bytes_accessed=28 * 2**20, transcendentals=0
        ),
        name=name,
    )(a, b, a_shared, b_shared)


def branch_kernel(
    rank_ref, picked_ref, gate_ref, act_ref, weight_ref, shared_ref, out_ref, res_ref, *, experts
):
    step = pl.program_id(0)
    capacity = act_ref.shape[1]

    @pl.when(step < experts)
    def _():
        here = pl.ds(pl.multiple_of(step * capacity, capacity), capacity)
        res_ref[here, :] = (gate_ref[0] * dot(act_ref[0], weight_ref[0], NT)).astype(bf16)

    @pl.when(step >= experts)
    def _():
        total = dot(picked_ref[...], res_ref[...])
        out_ref[...] = (total + dot(shared_ref[...], weight_ref[0], NT)).astype(bf16)


def experts_out(picked, gates, act, out_t, shared_act):
    experts, capacity, hidden = act.shape
    group, width, width_mp = shared_act.shape[0], out_t.shape[1], lax.axis_size("mp")
    rows = group // width_mp
    return pl.pallas_call(
        functools.partial(branch_kernel, experts=experts),
        out_shape=jax.ShapeDtypeStruct((group, width), bf16),
        grid_spec=pltpu.PrefetchScalarGridSpec(
            num_scalar_prefetch=1,
            grid=(experts + width_mp,),
            in_specs=[
                row_block(experts, rows, experts * capacity),
                per_expert(experts, capacity, 1),
                per_expert(experts, capacity, hidden),
                per_slab(experts, width, hidden),
                row_block(experts, rows, hidden),
            ],
            out_specs=ring_block(experts, width_mp, rows, width),
            scratch_shapes=[pltpu.VMEM((experts * capacity, width), bf16)],
        ),
        compiler_params=pltpu.CompilerParams(vmem_limit_bytes=VMEM),
        cost_estimate=pl.CostEstimate(
            flops=16 * 10**9, bytes_accessed=22 * 2**20, transcendentals=0
        ),
        name="experts_out",
    )(lax.axis_index("mp").reshape(1), picked, gates, act, out_t, shared_act)


def adamw_update(master, first, second, gradient, fan_in):
    step_rate = 0.5 * fan_in ** (-0.5)
    first_new = beta_one * first + (1.0 - beta_one) * gradient
    second_new = beta_two * second + (1.0 - beta_two) * gradient * gradient
    first_hat = first_new / (1.0 - beta_one**STEP)
    second_hat = second_new / (1.0 - beta_two**STEP)
    master_new = master - step_rate * (
        first_hat / (jnp.sqrt(second_hat) + epsilon) + weight_decay * master
    )
    return (master_new, first_new, second_new, master_new.astype(bf16))


def body(
    patches,
    cotangent,
    conditioning,
    lengths,
    routes,
    ada_weight,
    ada_first,
    ada_second,
    router_weight,
    router_first,
    router_second,
    qkv_weight,
    qkv_first,
    qkv_second,
    proj_weight,
    proj_first,
    proj_second,
    shared_in_weight,
    shared_in_first,
    shared_in_second,
    shared_out_weight,
    shared_out_first,
    shared_out_second,
    expert_in_weight,
    expert_in_first,
    expert_in_second,
    expert_out_weight,
    expert_out_first,
    expert_out_second,
):
    rows, D = patches.shape
    width = lax.axis_size("mp")
    n_dp = lax.axis_size("dp")
    devices = width * n_dp
    group = rows * width
    capacity = 5 * group // 16
    heads_here = H // width
    model_rank = lax.axis_index("mp")
    item_count = lengths.shape[1]
    hidden = shared_in_weight.shape[1]
    ada_cols = ada_weight.shape[1]
    router_cols = router_weight.shape[0]

    out_slab = jnp.concatenate(
        [
            jnp.swapaxes(expert_out_weight.astype(bf16), 1, 2),
            shared_out_weight.astype(bf16).T[None],
        ],
        axis=0,
    )
    in_slab = jnp.concatenate(
        [expert_in_weight.astype(bf16), shared_in_weight.astype(bf16)[None]], axis=0
    )
    out_t = lax.all_gather(out_slab, "dp", axis=1, tiled=True)
    proj_block = proj_weight.astype(bf16).T
    proj_shape = proj_block.shape
    proj_rows = proj_block.size // D
    fill = -proj_rows % 32

    def riding(blocks):
        return jnp.pad(blocks, ((0, 0),) * (blocks.ndim - 2) + ((0, fill), (0, 0)))

    patches_line = Gather(
        after(jnp.concatenate([patches, riding(proj_block.reshape(-1, D))], axis=0), out_slab)
    )

    def over_dp(values):
        parts = lax.all_to_all(
            values.reshape((n_dp, values.shape[0] // n_dp) + values.shape[1:]), "dp", 0, 0, tiled=True
        )
        return jnp.sum(parts.astype(f32), axis=0)

    def from_dp(values):
        parts = jnp.broadcast_to(values[None], (n_dp,) + values.shape)
        return lax.all_to_all(parts, "dp", 0, 0, tiled=True).reshape((-1,) + values.shape[1:])

    cond_all = lax.all_gather(conditioning, "dp", axis=0, tiled=True)
    cond_all = phase([patches_line], cond_all)
    cond_act = jax.nn.silu(cond_all.astype(f32)).astype(bf16)
    columns = jnp.dot(cond_act, ada_weight.astype(bf16), preferred_element_type=f32)
    columns = jnp.repeat(columns.reshape(n_dp, item_count * ada_cols), width, axis=0)
    router_low = router_weight.astype(bf16).astype(f32)
    payload = jnp.concatenate(
        [columns, jnp.broadcast_to(router_low[None], (devices, router_cols))], axis=1
    )
    received = phase(
        [patches_line], lax.all_to_all(payload, ("dp", "mp"), 0, 0, tiled=True)
    )
    qkv_here = lax.all_gather(
        after(qkv_weight.astype(bf16), received), "dp", axis=0, tiled=True
    )
    modulation = (
        received[:, : item_count * ada_cols]
        .reshape(devices, item_count, ada_cols)
        .transpose(1, 0, 2)
        .reshape(item_count, devices * ada_cols)
    )
    router_matrix = received[:, item_count * ada_cols :].reshape(D, E).astype(bf16)
    bounds = jnp.cumsum(lengths[0])
    places = jnp.arange(group, dtype=jnp.int32)
    segment = jnp.sum((places[:, None] >= bounds[None, :]).astype(jnp.int32), axis=1)
    segment_column = segment[:, None]
    segment_mine = lax.dynamic_slice_in_dim(segment_column, model_rank * rows, rows, 0)
    start, kind = key_windows(lengths[0], group)

    chosen = routes[:, :, None] == jnp.arange(E, dtype=jnp.int32)[None, None, :]
    names = chosen.any(axis=1)
    below = (places[:, None] > places[None, :]).astype(bf16)
    earlier = jnp.dot(below, names.astype(bf16), preferred_element_type=f32).astype(jnp.int32)
    place_of = jnp.where(names, earlier, -1).T
    picked = routes * capacity + jnp.sum(jnp.where(chosen, earlier[:, None, :], 0), axis=2)
    names_low = jnp.pad(names.astype(bf16), ((0, 0), (0, LANES - E)))
    modulation, router_matrix, qkv_here, place_of, picked = phase(
        [patches_line], (modulation, router_matrix, qkv_here, place_of, picked)
    )

    proj_here = jnp.concatenate(
        [
            p.reshape(proj_shape)
            for p in patches_line.ring(slice(rows, rows + proj_rows))
        ],
        axis=1,
    )
    cot_line = Gather(after(cotangent, patches_line.ups[-1]))
    patches_all, h_one_all, qkv, qkv_wide = phase(
        [cot_line], norm_one(patches_line, rows, modulation, segment_column, qkv_here)
    )
    (mixed_here, logs), out_t = phase([cot_line], (attend(qkv, start, kind), out_t))
    in_w = lax.all_gather(after(in_slab, out_t), "dp", axis=1, tiled=True)
    mixed_line = Gather(mixed_here)
    proj_t = from_dp(after(proj_here, mixed_here))
    slots = jnp.arange(E * capacity, dtype=jnp.int32)[None, :]
    picked = after(picked, mixed_here)
    picked = phase(
        [cot_line, mixed_line],
        ((slots == picked[:, 0:1]) | (slots == picked[:, 1:2])).astype(bf16),
    )
    (grad_branch,) = by_rows(
        gated_kernel, 1, cot_line, rows, modulation, segment_column, "grad_branch"
    )
    grad_branch, held = phase(
        [mixed_line],
        (grad_branch, experts_before(place_of, names_low, grad_branch, out_t, capacity, E // 2)),
    )
    (branch_slots, named_slots, back_slots, back_shared), proj_t = phase(
        [mixed_line],
        (experts_before(place_of, names_low, grad_branch, out_t, capacity, E // 2, held), proj_t),
    )
    h_two, x_one_mine, attn_mine, mixed_mine, proj = norm_two(
        mixed_line, patches_all, proj_t, modulation, segment_column
    )

    (
        dispatched,
        expert_act,
        grad_expert_pre,
        grad_res,
        gates,
        shared_act,
        grad_shared_pre,
        grad_logits,
        grad_h_two,
    ) = experts_main(
        place_of,
        picked,
        h_two,
        in_w,
        router_matrix,
        branch_slots,
        named_slots,
        back_slots,
        back_shared,
    )
    two_line = Scatter(grad_h_two)
    grad_out_slab = phase(
        [two_line], slab_product(grad_res, expert_act, grad_branch, shared_act, "grad_out")
    )
    grad_out_mine = lax.psum_scatter(grad_out_slab, "dp", scatter_dimension=1, tiled=True)
    grad_in_slab = phase(
        [two_line], slab_product(dispatched, grad_expert_pre, h_two, grad_shared_pre, "grad_in")
    )
    grad_router = phase(
        [two_line],
        jnp.einsum("gd,eg->de", h_two.astype(f32), grad_logits, precision=highest),
    )
    grad_x_one, grad_attn, grad_mixed_mine, sums_two = back_two(
        two_line.terms(), x_one_mine, attn_mine, cotangent, proj, modulation, segment_mine
    )
    grad_mixed, mlp_part = phase(
        [],
        (
            lax.all_to_all(grad_mixed_mine, "mp", 0, 0, tiled=True),
            experts_out(picked, after(gates, grad_mixed_mine), expert_act, out_t, shared_act),
        ),
    )
    grad_mixed = grad_mixed.transpose(1, 0, 2).reshape(heads_here * HD, group)
    mlp_line = Scatter(mlp_part)

    grad_proj_t = jnp.einsum(
        "gd,cg->dc", after(grad_attn, grad_mixed), mixed_mine, preferred_element_type=f32
    )
    grad_qkv, grad_out_mine, grad_proj_t = phase(
        [mlp_line],
        (
            attend_back(qkv, grad_mixed, logs, start, kind),
            grad_out_mine,
            over_dp(grad_proj_t.astype(bf16)).astype(bf16),
        ),
    )
    grad_in_mine = lax.psum_scatter(
        after(grad_in_slab, grad_out_mine), "dp", scatter_dimension=1, tiled=True
    )
    proj_parts = grad_proj_t.reshape(proj_shape[0], width, proj_shape[1]).transpose(1, 0, 2)
    partial = ring_product(grad_qkv, qkv_wide, riding(proj_parts.reshape(width, -1, D)))
    one_line = Scatter(partial)
    mlp_line.take(after((mlp_line.up, mlp_line.down), partial))
    mlp_line.step -= 1
    grad_qkv_weight = jnp.einsum("gd,gc->dc", h_one_all, grad_qkv, preferred_element_type=f32)
    grad_qkv_weight = grad_qkv_weight.reshape(D, heads_here * 3, LANES)[:, :, :HD]
    grad_qkv_weight = phase(
        [one_line, mlp_line], grad_qkv_weight.reshape(D, heads_here * 3 * HD).astype(bf16)
    )
    grad_qkv_mine = phase([one_line, mlp_line], over_dp(grad_qkv_weight))
    result, sums_gate = phase(
        [one_line], outcome(mlp_line.terms(), x_one_mine, cotangent, modulation, segment_mine)
    )
    patch_grad, sums_one = back_one(
        one_line.terms(), patches, grad_x_one, modulation, segment_mine
    )
    grad_proj_mine = sum(
        t[rows : rows + proj_rows].astype(f32) for t in one_line.terms()
    ).reshape(proj_shape)
    grad_modulation = jnp.concatenate([sums_one, sums_two, sums_gate], axis=1)
    payload = jnp.concatenate(
        [
            grad_modulation.reshape(item_count, devices, ada_cols)
            .transpose(1, 0, 2)
            .reshape(devices, item_count * ada_cols),
            grad_router.reshape(devices, router_cols),
        ],
        axis=1,
    )
    received = lax.all_to_all(payload, ("dp", "mp"), 0, 0, tiled=True)
    received, grad_in_mine = lax.optimization_barrier((received, grad_in_mine))
    router_grad = jnp.sum(received[:, item_count * ada_cols :], axis=0)
    columns = jnp.sum(
        received[:, : item_count * ada_cols].reshape(n_dp, width, item_count, ada_cols), axis=1
    ).reshape(n_dp * item_count, ada_cols)
    ada_grad = jnp.einsum("id,ic->dc", cond_act.astype(f32), columns, precision=highest)
    grad_out_mine, grad_in_mine = grad_out_mine.astype(f32), grad_in_mine.astype(f32)

    gradients = (
        ada_grad,
        router_grad,
        grad_qkv_mine,
        grad_proj_mine.T,
        grad_in_mine[E],
        grad_out_mine[E].T,
        grad_in_mine[:E],
        jnp.swapaxes(grad_out_mine[:E], 1, 2),
    )
    states_of = (
        (ada_weight, ada_first, ada_second),
        (router_weight, router_first, router_second),
        (qkv_weight, qkv_first, qkv_second),
        (proj_weight, proj_first, proj_second),
        (shared_in_weight, shared_in_first, shared_in_second),
        (shared_out_weight, shared_out_first, shared_out_second),
        (expert_in_weight, expert_in_first, expert_in_second),
        (expert_out_weight, expert_out_first, expert_out_second),
    )
    total_hidden = float(hidden * width)
    fan_ins = (D, D, D, 8.0 * D / group, D, total_hidden, D, total_hidden)
    updates = []
    for (master, first, second), gradient, fan_in in zip(states_of, gradients, fan_ins):
        updates.extend(adamw_update(master, first, second, gradient, float(fan_in)))
    return tuple([result, patch_grad] + updates)


def solution(mesh):
    tokens, data = P(("dp", "mp"), None), P("dp", None)
    ada, router = P(None, ("dp", "mp")), P(("dp", "mp"))
    deep, wide = P("dp", "mp"), P("mp", "dp")
    deep_experts, wide_experts = P(None, "dp", "mp"), P(None, "mp", "dp")
    kinds = (ada, router, deep, wide, deep, wide, deep_experts, wide_experts)
    in_specs = (tokens, tokens, data, data, data) + tuple(k for k in kinds for _ in range(3))
    out_specs = (tokens, tokens) + tuple(k for k in kinds for _ in range(4))
    return jax.shard_map(body, mesh=mesh, in_specs=in_specs, out_specs=out_specs, check_vma=False)
```

```python
import functools
import math

import jax
import jax.numpy as jnp
import numpy as np
from jax import lax
from jax.experimental import pallas as pl
from jax.experimental.pallas import tpu as pltpu
from jax.sharding import PartitionSpec as P

H = 12
HD = 64
E = 8
STEP = 10

beta_one = 0.9
beta_two = 0.95
epsilon = 1e-08
weight_decay = 0.1
norm_floor = 1e-06
highest = lax.Precision.HIGHEST
f32 = jnp.float32
bf16 = jnp.bfloat16


def norm_parts(values):
    centred = values - jnp.mean(values, axis=1, keepdims=True)
    inverse = lax.rsqrt(jnp.mean(centred * centred, axis=1, keepdims=True) + norm_floor)
    return centred * inverse, inverse


def norm_back(normed, inverse, gradient):
    first = jnp.mean(gradient, axis=1, keepdims=True)
    second = jnp.mean(gradient * normed, axis=1, keepdims=True)
    return inverse * (gradient - first - normed * second)


def after(values, *earlier):
    return lax.optimization_barrier((values, earlier))[0]


def ring_gather(block):
    width = lax.axis_size("mp")
    return [block] + [
        lax.ppermute(block, "mp", [(i, (i + shift) % width) for i in range(width)])
        for shift in range(1, width)
    ]


def sent_beside(terms, near, far):
    width = len(terms)
    first = [i for i in range(1, width) if i in (1, width - 1)]
    later = [i for i in range(1, width) if i not in first]
    got, near = lax.optimization_barrier(([terms[i] for i in first], near))
    rest, far = lax.optimization_barrier(([terms[i] for i in later], far(near)))
    found = dict(zip(first + later, got + rest))
    return [terms[0]] + [found[i] for i in range(1, width)], near, far


def ring_scatter(partial):
    width = lax.axis_size("mp")
    extent = partial.shape[0] // width
    parts = [partial[i * extent : (i + 1) * extent] for i in range(width)]
    return parts[:1] + [
        lax.ppermute(parts[shift], "mp", [(i, (i - shift) % width) for i in range(width)])
        for shift in range(1, width)
    ]


LANES = 128
VMEM = 60 * 2**20
SMALL = pl.CostEstimate(flops=10**6, bytes_accessed=10**5, transcendentals=0)
Q_BLOCK = 256
FAR = 2.0**50
NT = (((1,), (1,)), ((), ()))
TN = (((0,), (0,)), ((), ()))
NN = (((1,), (0,)), ((), ()))


def dot(a, b, dims=NN):
    return lax.dot_general(a, b, dims, preferred_element_type=f32)


def key_widths(group):
    return sorted({min(w, group) for w in (512, 768, 1024, group)})


def key_windows(lengths, group):
    ends = jnp.cumsum(lengths)
    begins = ends - lengths
    first = jnp.arange(group // Q_BLOCK, dtype=jnp.int32) * Q_BLOCK
    last = first + Q_BLOCK - 1
    low = jnp.max(jnp.where(begins[None, :] <= first[:, None], begins[None, :], 0), axis=1)
    high = jnp.min(jnp.where(ends[None, :] > last[:, None], ends[None, :], group), axis=1)
    low = low // LANES * LANES
    widths = jnp.array(key_widths(group), jnp.int32)
    kind = jnp.sum((high - low)[:, None] > widths[None, :], axis=1).astype(jnp.int32)
    return jnp.minimum(low, group - widths[kind]).astype(jnp.int32), kind


def attend_kernel(start_ref, kind_ref, qkv_ref, mixed_ref, log_ref, *, group):
    block = pl.program_id(1)
    rows = pl.ds(pl.multiple_of(block * Q_BLOCK, Q_BLOCK), Q_BLOCK)
    query = qkv_ref[rows, 0:LANES] * jnp.asarray(HD**-0.5, bf16)
    for index, extent in enumerate(key_widths(group)):

        @pl.when(kind_ref[block] == index)
        def _():
            keys = pl.ds(pl.multiple_of(start_ref[block], LANES), extent)
            scores = dot(qkv_ref[keys, LANES : 2 * LANES], query, NT)
            peak = jnp.max(scores, axis=0, keepdims=True)
            exps = jnp.exp(scores - peak)
            total = jnp.sum(exps, axis=0, keepdims=True)
            probs = (exps * (1.0 / total)).astype(bf16)
            mixed = dot(qkv_ref[keys, 2 * LANES : 3 * LANES], probs, TN)
            mixed_ref[...] = mixed[:HD].astype(bf16)
            log_ref[...] = (peak + jnp.log(total))[None]


def attend(qkv, start, kind):
    group = qkv.shape[0]
    heads = qkv.shape[1] // (3 * LANES)
    blocks = group // Q_BLOCK
    return pl.pallas_call(
        functools.partial(attend_kernel, group=group),
        out_shape=(
            jax.ShapeDtypeStruct((heads * HD, group), bf16),
            jax.ShapeDtypeStruct((heads, 1, group), f32),
        ),
        grid_spec=pltpu.PrefetchScalarGridSpec(
            num_scalar_prefetch=2,
            grid=(heads, blocks),
            in_specs=[pl.BlockSpec((group, 3 * LANES), lambda h, i, *_: (0, h))],
            out_specs=(
                pl.BlockSpec((HD, Q_BLOCK), lambda h, i, *_: (h, i)),
                pl.BlockSpec((1, 1, Q_BLOCK), lambda h, i, *_: (h, 0, i)),
            ),
        ),
        compiler_params=pltpu.CompilerParams(vmem_limit_bytes=VMEM),
        cost_estimate=SMALL,
        name="attend",
    )(start, kind, qkv)


def attend_back_kernel(
    start_ref, kind_ref, qkv_ref, grad_ref, log_ref, out_ref, key_total, value_total, *, group
):
    block = pl.program_id(1)

    @pl.when(block == 0)
    def _():
        key_total[...] = jnp.zeros_like(key_total)
        value_total[...] = jnp.zeros_like(value_total)

    rows = pl.ds(pl.multiple_of(block * Q_BLOCK, Q_BLOCK), Q_BLOCK)
    scaling = HD**-0.5
    query = qkv_ref[rows, 0:LANES] * jnp.asarray(scaling, bf16)
    grad = grad_ref[...]
    kept = lax.broadcasted_iota(jnp.int32, (1, LANES), 1) < HD
    for index, extent in enumerate(key_widths(group)):

        @pl.when(kind_ref[block] == index)
        def _():
            keys = pl.ds(pl.multiple_of(start_ref[block], LANES), extent)
            key_rows = qkv_ref[keys, LANES : 2 * LANES]
            value_rows = qkv_ref[keys, 2 * LANES : 3 * LANES]
            probs = jnp.exp(dot(key_rows, query, NT) - log_ref[0])
            grad_probs = dot(value_rows[:, :HD], grad)
            middle = jnp.sum(probs * grad_probs, axis=0, keepdims=True)
            grad_scores = (probs * (grad_probs - middle)).astype(bf16)
            value_total[keys, :HD] += dot(probs.astype(bf16), grad, NT)
            key_total[keys, :] += dot(grad_scores, query)
            grad_query = dot(key_rows, grad_scores, TN).T * scaling
            out_ref[rows, 0:LANES] = jnp.where(kept, grad_query, 0.0).astype(bf16)

    @pl.when(block == pl.num_programs(1) - 1)
    def _():
        out_ref[:, LANES : 2 * LANES] = jnp.where(kept, key_total[...], 0.0).astype(bf16)
        out_ref[:, 2 * LANES : 3 * LANES] = value_total[...].astype(bf16)


def attend_back(qkv, grad_mixed, logs, start, kind):
    group = qkv.shape[0]
    heads = qkv.shape[1] // (3 * LANES)
    blocks = group // Q_BLOCK
    return pl.pallas_call(
        functools.partial(attend_back_kernel, group=group),
        out_shape=jax.ShapeDtypeStruct(qkv.shape, bf16),
        grid_spec=pltpu.PrefetchScalarGridSpec(
            num_scalar_prefetch=2,
            grid=(heads, blocks),
            in_specs=[
                pl.BlockSpec((group, 3 * LANES), lambda h, i, *_: (0, h)),
                pl.BlockSpec((HD, Q_BLOCK), lambda h, i, *_: (h, i)),
                pl.BlockSpec((1, 1, Q_BLOCK), lambda h, i, *_: (h, 0, i)),
            ],
            out_specs=pl.BlockSpec((group, 3 * LANES), lambda h, i, *_: (0, h)),
            scratch_shapes=[pltpu.VMEM((group, LANES), f32), pltpu.VMEM((group, LANES), f32)],
        ),
        compiler_params=pltpu.CompilerParams(vmem_limit_bytes=VMEM),
        cost_estimate=SMALL,
        name="attend_back",
    )(start, kind, qkv, grad_mixed, logs)


def item_rows(table_ref, term, width, segment, items):
    columns = slice(term * width, (term + 1) * width)
    rows = table_ref[0:1, columns]
    for item in range(1, items):
        rows = jnp.where(segment >= item, table_ref[item : item + 1, columns], rows)
    return rows


def item_sums(values, segment, items):
    return jnp.concatenate(
        [jnp.sum(jnp.where(segment == item, values, 0.0), axis=0, keepdims=True) for item in range(items)], axis=0
    )


def placed(width_mp):
    return lambda i, rank: (lax.rem(rank[0] - i + width_mp, width_mp), 0)


def plain(*shape):
    return pl.BlockSpec(shape, lambda i, rank: (0,) * len(shape))


def image_marks(heads, items):
    marks = np.zeros((items, heads, 3, LANES), np.float32)
    for image in range(items):
        for item in range(items):
            if image == item:
                marks[image, :, 0, HD + item] = FAR
            else:
                marks[image, :, 1, HD + item] = -FAR
    return marks.reshape(items, heads * 3 * LANES)


def norm_one_kernel(*refs, width_mp, items):
    rank_ref, segment_ref, table_ref, marks_ref, weight_ref = refs[:5]
    block_refs, (rows_ref, h_ref, qkv_ref, wide_ref) = refs[5:-4], refs[-4:]
    segment = segment_ref[...]
    width = rows_ref.shape[1]

    @pl.when(pl.program_id(0) == 0)
    def _():
        wide_ref[...] = jnp.zeros_like(wide_ref)
        for part in range(weight_ref.shape[1] // HD):
            wide_ref[:, part * LANES : part * LANES + HD] = weight_ref[:, part * HD : (part + 1) * HD]

    for place in range(width_mp):

        @pl.when(pl.program_id(0) == place)
        def _():
            rows_ref[...] = block_refs[place][...]

    normed, _ = norm_parts(rows_ref[...].astype(f32))
    shift = item_rows(table_ref, 0, width, segment, items)
    scale = item_rows(table_ref, 1, width, segment, items)
    h_one = (normed * (1.0 + scale) + shift).astype(bf16)
    h_ref[...] = h_one
    marks = item_rows(marks_ref, 0, qkv_ref.shape[1], segment, items)
    qkv_ref[...] = (dot(h_one, wide_ref[...]) + marks).astype(bf16)


def norm_one(arrays, rows, table, segment, weight):
    width_mp, width, items = len(arrays), arrays[0].shape[1], table.shape[0]
    heads = weight.shape[1] // (3 * HD)
    wide = heads * 3 * LANES
    marks = jnp.asarray(image_marks(heads, items))
    order = placed(width_mp)
    return pl.pallas_call(
        functools.partial(norm_one_kernel, width_mp=width_mp, items=items),
        out_shape=(
            jax.ShapeDtypeStruct((rows * width_mp, width), bf16),
            jax.ShapeDtypeStruct((rows * width_mp, width), bf16),
            jax.ShapeDtypeStruct((rows * width_mp, wide), bf16),
            jax.ShapeDtypeStruct((width, wide), bf16),
        ),
        grid_spec=pltpu.PrefetchScalarGridSpec(
            num_scalar_prefetch=1,
            grid=(width_mp,),
            in_specs=[pl.BlockSpec((rows, 1), order), plain(*table.shape), plain(*marks.shape), plain(*weight.shape)]
            + [plain(rows, width)] * len(arrays),
            out_specs=(
                pl.BlockSpec((rows, width), order),
                pl.BlockSpec((rows, width), order),
                pl.BlockSpec((rows, wide), order),
                plain(width, wide),
            ),
        ),
        compiler_params=pltpu.CompilerParams(vmem_limit_bytes=VMEM),
        cost_estimate=SMALL,
        name="norm_one",
    )(lax.axis_index("mp").reshape(1), segment, table, marks, weight, *arrays)


def gated_kernel(*refs, width_mp, items):
    rank_ref, segment_ref, table_ref = refs[:3]
    block_refs, out_ref = refs[3:-1], refs[-1]
    segment = segment_ref[...]
    width = out_ref.shape[1]
    for place in range(width_mp):

        @pl.when(pl.program_id(0) == place)
        def _():
            rows = block_refs[place][...].astype(f32)
            out_ref[...] = (item_rows(table_ref, 5, width, segment, items) * rows).astype(bf16)


def by_rows(kernel, outputs, arrays, rows, table, segment, name):
    width_mp, width, items = len(arrays), arrays[0].shape[1], table.shape[0]
    order = placed(width_mp)
    return pl.pallas_call(
        functools.partial(kernel, width_mp=width_mp, items=items),
        out_shape=(jax.ShapeDtypeStruct((rows * width_mp, width), bf16),) * outputs,
        grid_spec=pltpu.PrefetchScalarGridSpec(
            num_scalar_prefetch=1,
            grid=(width_mp,),
            in_specs=[pl.BlockSpec((rows, 1), order), plain(*table.shape)]
            + [plain(rows, width)] * len(arrays),
            out_specs=(pl.BlockSpec((rows, width), order),) * outputs,
        ),
        compiler_params=pltpu.CompilerParams(vmem_limit_bytes=VMEM),
        cost_estimate=SMALL,
        name=name,
    )(lax.axis_index("mp").reshape(1), segment, table, *arrays)


def norm_two_kernel(*refs, width_mp, items):
    rank_ref, segment_ref, table_ref, rows_ref, turned_ref = refs[:5]
    mixed_refs = refs[5:-6]
    h_ref, x_mine_ref, attn_mine_ref, mixed_mine_ref, proj_ref, proj_scratch = refs[-6:]
    step = pl.program_id(0)
    rank = rank_ref[0]
    segment = segment_ref[...]
    width = rows_ref.shape[1]
    heads = mixed_refs[0].shape[0]

    @pl.when(step == 0)
    def _():
        proj_scratch[...] = turned_ref[...].T
        proj_ref[...] = proj_scratch[...]

    attn = jnp.zeros(rows_ref.shape, f32)
    for place in range(width_mp):
        here = slice(place * heads, (place + 1) * heads)
        mixed = mixed_refs[place][...]
        attn += dot(mixed, proj_scratch[here, :], TN)

        @pl.when(step == rank)
        def _():
            mixed_mine_ref[here, :] = mixed

    x_one = rows_ref[...].astype(f32) + item_rows(table_ref, 2, width, segment, items) * attn

    @pl.when(step == rank)
    def _():
        x_mine_ref[...] = x_one
        attn_mine_ref[...] = attn

    normed, _ = norm_parts(x_one)
    shift = item_rows(table_ref, 3, width, segment, items)
    scale = item_rows(table_ref, 4, width, segment, items)
    h_ref[...] = (normed * (1.0 + scale) + shift).astype(bf16)


def norm_two(arrays, patches, proj_t, table, segment):
    width_mp, (heads, group) = len(arrays), arrays[0].shape
    rows, width, items = group // width_mp, patches.shape[1], table.shape[0]
    every = heads * width_mp
    return pl.pallas_call(
        functools.partial(norm_two_kernel, width_mp=width_mp, items=items),
        out_shape=(
            jax.ShapeDtypeStruct((group, width), bf16),
            jax.ShapeDtypeStruct((rows, width), f32),
            jax.ShapeDtypeStruct((rows, width), f32),
            jax.ShapeDtypeStruct((every, rows), bf16),
            jax.ShapeDtypeStruct((every, width), bf16),
        ),
        grid_spec=pltpu.PrefetchScalarGridSpec(
            num_scalar_prefetch=1,
            grid=(width_mp,),
            in_specs=[
                pl.BlockSpec((rows, 1), lambda i, rank: (i, 0)),
                plain(*table.shape),
                pl.BlockSpec((rows, width), lambda i, rank: (i, 0)),
                plain(*proj_t.shape),
            ]
            + [pl.BlockSpec((heads, rows), lambda i, rank: (0, i))] * len(arrays),
            out_specs=(
                pl.BlockSpec((rows, width), lambda i, rank: (i, 0)),
                plain(rows, width),
                plain(rows, width),
                plain(every, rows),
                plain(every, width),
            ),
            scratch_shapes=[pltpu.VMEM((every, width), bf16)],
        ),
        compiler_params=pltpu.CompilerParams(vmem_limit_bytes=VMEM),
        cost_estimate=SMALL,
        name="norm_two",
    )(lax.axis_index("mp").reshape(1), segment, table, patches, proj_t, *arrays)


def product_kernel(rank_ref, a_ref, b_ref, part_ref, out_ref):
    rows = a_ref.shape[0]
    out_ref[0:rows, :] = dot(a_ref[...], b_ref[...], NT).astype(bf16)
    out_ref[rows:, :] = part_ref[0]


def ring_product(a, b, parts):
    width_mp, extra, width = parts.shape
    rows = a.shape[0] // width_mp
    return pl.pallas_call(
        product_kernel,
        out_shape=jax.ShapeDtypeStruct((a.shape[0] + width_mp * extra, width), bf16),
        grid_spec=pltpu.PrefetchScalarGridSpec(
            num_scalar_prefetch=1,
            grid=(width_mp,),
            in_specs=[
                pl.BlockSpec((rows, a.shape[1]), placed(width_mp)),
                plain(*b.shape),
                pl.BlockSpec((1, extra, width), lambda i, rank: (i, 0, 0)),
            ],
            out_specs=pl.BlockSpec((rows + extra, width), lambda i, rank: (i, 0)),
        ),
        compiler_params=pltpu.CompilerParams(vmem_limit_bytes=VMEM),
        cost_estimate=SMALL,
        name="grad_h_one",
    )(lax.axis_index("mp").reshape(1), a, b, parts)


def term_sum(refs):
    return functools.reduce(lambda total, ref: total + ref[...].astype(f32), refs[1:], refs[0][...].astype(f32))


def back_two_kernel(rank_ref, segment_ref, table_ref, *refs, width_mp, items):
    term_refs, (x_ref, attn_ref, cot_ref, proj_ref) = refs[:width_mp], refs[width_mp:-4]
    grad_x_ref, grad_attn_ref, grad_mixed_ref, sums_ref = refs[-4:]
    segment = segment_ref[...]
    width = x_ref.shape[1]
    heads = proj_ref.shape[0] // width_mp
    grad = term_sum(term_refs)
    normed, inverse = norm_parts(x_ref[...])
    scale = item_rows(table_ref, 4, width, segment, items)
    grad_x = cot_ref[...].astype(f32) + norm_back(normed, inverse, grad * (1.0 + scale))
    grad_x_ref[...] = grad_x
    grad_attn = (item_rows(table_ref, 2, width, segment, items) * grad_x).astype(bf16)
    grad_attn_ref[...] = grad_attn
    for place in range(width_mp):
        owner = lax.rem(rank_ref[0] - place + width_mp, width_mp)
        part = dot(proj_ref[place * heads : (place + 1) * heads, :], grad_attn, NT)
        grad_mixed_ref[owner] = part.astype(bf16)
    sums_ref[:, 0:width] = item_sums(grad_x * attn_ref[...], segment, items)
    sums_ref[:, width : 2 * width] = item_sums(grad, segment, items)
    sums_ref[:, 2 * width :] = item_sums(grad * normed, segment, items)


def back_two(terms, x_one, attn, cotangent, proj, table, segment):
    rows, width = x_one.shape
    items, width_mp = table.shape[0], lax.axis_size("mp")
    shapes = (
        jax.ShapeDtypeStruct((rows, width), f32),
        jax.ShapeDtypeStruct((rows, width), bf16),
        jax.ShapeDtypeStruct((width_mp, proj.shape[0] // width_mp, rows), bf16),
        jax.ShapeDtypeStruct((items, 3 * width), f32),
    )
    operands = (segment, table, *(t for t in terms), x_one, attn, cotangent, proj)
    return pl.pallas_call(
        functools.partial(back_two_kernel, width_mp=width_mp, items=items),
        out_shape=shapes,
        grid_spec=pltpu.PrefetchScalarGridSpec(
            num_scalar_prefetch=1,
            grid=(1,),
            in_specs=[plain(*o.shape) for o in operands],
            out_specs=tuple(plain(*o.shape) for o in shapes),
        ),
        compiler_params=pltpu.CompilerParams(vmem_limit_bytes=VMEM),
        cost_estimate=SMALL,
        name="back_two",
    )(lax.axis_index("mp").reshape(1), *operands)


def back_one_kernel(segment_ref, table_ref, *refs, items):
    term_refs, (patches_ref, grad_x_ref, grad_ref, sums_ref) = refs[:-4], refs[-4:]
    segment = segment_ref[...]
    width = patches_ref.shape[1]
    grad = term_sum(term_refs)
    normed, inverse = norm_parts(patches_ref[...].astype(f32))
    scale = item_rows(table_ref, 1, width, segment, items)
    grad_ref[...] = (grad_x_ref[...] + norm_back(normed, inverse, grad * (1.0 + scale))).astype(bf16)
    sums_ref[:, 0:width] = item_sums(grad, segment, items)
    sums_ref[:, width:] = item_sums(grad * normed, segment, items)


def outcome_kernel(segment_ref, table_ref, *refs, items):
    term_refs, (x_ref, cot_ref, out_ref, sums_ref) = refs[:-4], refs[-4:]
    segment = segment_ref[...]
    width = x_ref.shape[1]
    branch = term_sum(term_refs)
    gate = item_rows(table_ref, 5, width, segment, items)
    out_ref[...] = (x_ref[...] + gate * branch).astype(bf16)
    sums_ref[...] = item_sums(cot_ref[...].astype(f32) * branch, segment, items)


def own_rows(kernel, terms, first, second, table, segment, sums, name):
    rows, width = first.shape
    items = table.shape[0]
    shapes = (
        jax.ShapeDtypeStruct((rows, width), bf16),
        jax.ShapeDtypeStruct((items, sums * width), f32),
    )

    def single(*shape):
        return pl.BlockSpec(shape, lambda i: (0,) * len(shape))

    return pl.pallas_call(
        functools.partial(kernel, items=items),
        out_shape=shapes,
        grid=(1,),
        in_specs=[single(*segment.shape), single(*table.shape)]
        + [single(rows, width)] * (len(terms) + 2),
        out_specs=tuple(single(*o.shape) for o in shapes),
        compiler_params=pltpu.CompilerParams(vmem_limit_bytes=VMEM),
        cost_estimate=SMALL,
        name=name,
    )(segment, table, *terms, first, second)


def gelu_terms(before):
    slope = (2.0 / math.pi) ** 0.5
    square = before * before
    curve = jnp.tanh(slope * before * (1.0 + 0.044715 * square))
    half = 0.5 * (1.0 + curve)
    value = before * half
    derivative = half + (0.5 * slope) * before * (1.0 - curve * curve) * (1.0 + 0.134145 * square)
    return value, derivative


def slot_picks(place_row, capacity):
    slots = lax.broadcasted_iota(jnp.int32, (capacity, place_row.shape[1]), 0)
    return slots == place_row


def row_chunks(group):
    return [slice(first, first + 512) for first in range(0, group, 512)]


def before_kernel(
    place_ref, named_ref, branch_ref, weight_ref, *refs, count, shared
):
    slots_ref, named_slots_ref, back_ref = refs[-4:-1] if shared else refs[-3:]
    step = pl.program_id(0)

    @pl.when(step < count)
    def _():
        picks = slot_picks(place_ref[0], slots_ref.shape[1]).astype(bf16)
        slots = dot(picks, branch_ref[...]).astype(bf16)
        slots_ref[0] = slots
        named_slots_ref[0] = dot(picks, named_ref[...]).astype(bf16)
        back_ref[0] = dot(slots, weight_ref[0]).astype(bf16)

    if shared:

        @pl.when(step == count)
        def _():
            for chunk in row_chunks(branch_ref.shape[0]):
                refs[-1][chunk, :] = dot(branch_ref[chunk, :], weight_ref[0]).astype(bf16)


def whole(*shape):
    return pl.BlockSpec(shape, lambda *_: (0,) * len(shape), pipeline_mode=pl.Buffered(1))


def per_expert(experts, *shape):
    return pl.BlockSpec(
        (1,) + shape, lambda e, *_: (jnp.minimum(e, experts - 1),) + (0,) * len(shape)
    )


def per_slab(experts, *shape):
    return pl.BlockSpec((1,) + shape, lambda e, *_: (jnp.minimum(e, experts),) + (0,) * len(shape))


def experts_before(places, named, branch, out_t, capacity, first, held=None):
    group, width = branch.shape
    experts, hidden = out_t.shape[0] - 1, out_t.shape[2]
    base, count = (0, first) if held is None else (first, experts - first)
    shapes = (
        jax.ShapeDtypeStruct((experts, capacity, width), bf16),
        jax.ShapeDtypeStruct((experts, capacity, LANES), bf16),
        jax.ShapeDtypeStruct((experts, capacity, hidden), bf16),
    )

    def mine(*shape):
        return pl.BlockSpec(
            (1,) + shape, lambda e: (base + jnp.minimum(e, count - 1),) + (0,) * len(shape)
        )

    shared = held is not None
    return pl.pallas_call(
        functools.partial(before_kernel, count=count, shared=shared),
        out_shape=shapes + (jax.ShapeDtypeStruct((group, hidden), bf16),) * shared,
        grid=(count + shared,),
        in_specs=[
            mine(1, group),
            whole(group, LANES),
            whole(group, width),
            pl.BlockSpec((1, width, hidden), lambda e: (base + e, 0, 0)),
        ]
        + [pl.BlockSpec(memory_space=pl.ANY)] * (3 * shared),
        out_specs=(mine(capacity, width), mine(capacity, LANES), mine(capacity, hidden))
        + (whole(group, hidden),) * shared,
        input_output_aliases={4: 0, 5: 1, 6: 2} if shared else {},
        compiler_params=pltpu.CompilerParams(vmem_limit_bytes=VMEM),
        cost_estimate=SMALL,
        name="experts_before",
    )(places.reshape(experts, 1, group), named, branch, out_t, *(held or ()))


def slots_of(picked, slots):
    index = lax.broadcasted_iota(jnp.int32, (picked.shape[0], slots), 1)
    return ((index == picked[:, 0:1]) | (index == picked[:, 1:2])).astype(bf16)


def experts_kernel(
    rank_ref,
    place_ref,
    places_ref,
    picked_ref,
    rows_ref,
    weight_ref,
    router_ref,
    router_wide_ref,
    slots_ref,
    named_ref,
    back_ref,
    shared_back_ref,
    dispatched_ref,
    act_ref,
    grad_pre_ref,
    grad_res_ref,
    gate_ref,
    shared_act_ref,
    shared_grad_ref,
    grad_logits_ref,
    grad_rows_ref,
    grad_gates_ref,
    grad_slots_ref,
    high_ref,
    rest_ref,
    *,
    experts,
):
    step = pl.program_id(0)
    group = rows_ref.shape[0]
    capacity = slots_ref.shape[1]

    @pl.when(step < experts)
    def _():
        picks = slot_picks(place_ref[0], capacity)
        dispatched = dot(picks.astype(bf16), rows_ref[...]).astype(bf16)
        dispatched_ref[0] = dispatched
        pre = dot(dispatched, weight_ref[0])
        logits = dot(dispatched, router_wide_ref[...])
        lane = lax.broadcasted_iota(jnp.int32, logits.shape, 1)
        named = named_ref[0].astype(f32) > 0.0
        peak = jnp.max(jnp.where(named, logits, -jnp.inf), axis=1, keepdims=True)
        shares = jnp.where(named, jnp.exp(logits - peak), 0.0)
        total = jnp.sum(shares, axis=1, keepdims=True)
        own = jnp.sum(jnp.where(lane == step, shares, 0.0), axis=1, keepdims=True)
        gate = jnp.where(total > 0.0, own / jnp.maximum(total, 1.0), 0.0)
        gate_ref[0] = gate
        value, slope = gelu_terms(pre)
        act = value.astype(bf16)
        act_ref[0] = act
        back = back_ref[0].astype(f32)
        grad_pre = (gate * back * slope).astype(bf16)
        grad_pre_ref[0] = grad_pre
        grad_res_ref[0] = (gate * slots_ref[0].astype(f32)).astype(bf16)
        grad_gate = jnp.sum(back * act.astype(f32), axis=1, keepdims=True)
        grad_gates_ref[step] = jnp.sum(jnp.where(picks, grad_gate, 0.0), axis=0, keepdims=True)
        here = pl.ds(pl.multiple_of(step * capacity, capacity), capacity)
        grad_slots_ref[here, :] = dot(grad_pre, weight_ref[0], NT).astype(bf16)

    @pl.when(step == experts)
    def _():
        logits = dot(router_ref[...], rows_ref[...], NT)
        named = places_ref[...] >= 0
        peak = jnp.max(jnp.where(named, logits, -jnp.inf), axis=0, keepdims=True)
        shares = jnp.where(named, jnp.exp(logits - peak), 0.0)
        gates = shares / jnp.sum(shares, axis=0, keepdims=True)
        grad_gates = jnp.concatenate([grad_gates_ref[e] for e in range(experts)], axis=0)
        grad_logits = gates * (grad_gates - jnp.sum(gates * grad_gates, axis=0, keepdims=True))
        grad_logits_ref[...] = grad_logits
        high = grad_logits.astype(bf16)
        high_ref[...] = high
        rest_ref[...] = (grad_logits - high.astype(f32)).astype(bf16)

    @pl.when(step >= experts)
    def _():
        size = shared_act_ref.shape[0]
        here = pl.ds(pl.multiple_of((step - experts) * size, size), size)
        value, slope = gelu_terms(dot(rows_ref[here, :], weight_ref[0]))
        shared_act_ref[...] = value.astype(bf16)
        grad_pre = (shared_back_ref[...].astype(f32) * slope).astype(bf16)
        shared_grad_ref[...] = grad_pre
        total = dot(slots_of(picked_ref[...], experts * capacity), grad_slots_ref[...])
        total += dot(grad_pre, weight_ref[0], NT)
        total += dot(high_ref[:, here], router_ref[...], TN)
        total += dot(rest_ref[:, here], router_ref[...], TN)
        grad_rows_ref[...] = total.astype(bf16)


def row_block(experts, *shape):
    return pl.BlockSpec(shape, lambda e, *_: (jnp.maximum(e - experts, 0), 0))


def ring_block(experts, width_mp, *shape):
    def index(e, rank):
        return (lax.rem(rank[0] - jnp.maximum(e - experts, 0) + width_mp, width_mp), 0)

    return pl.BlockSpec(shape, index)


def experts_main(places, picked, h_two, in_w, router, slots, named, back, shared_back):
    group, width = h_two.shape
    experts, capacity, hidden = back.shape
    width_mp = lax.axis_size("mp")
    rows = group // width_mp
    slot_shape = jax.ShapeDtypeStruct((experts, capacity, width), bf16)
    unit_shape = jax.ShapeDtypeStruct((experts, capacity, hidden), bf16)
    return pl.pallas_call(
        functools.partial(experts_kernel, experts=experts),
        out_shape=(
            slot_shape,
            unit_shape,
            unit_shape,
            slot_shape,
            jax.ShapeDtypeStruct((experts, capacity, 1), f32),
            jax.ShapeDtypeStruct((group, hidden), bf16),
            jax.ShapeDtypeStruct((group, hidden), bf16),
            jax.ShapeDtypeStruct((experts, group), f32),
            jax.ShapeDtypeStruct((group, width), bf16),
        ),
        grid_spec=pltpu.PrefetchScalarGridSpec(
            num_scalar_prefetch=1,
            grid=(experts + width_mp,),
            in_specs=[
                per_expert(experts, 1, group),
                whole(experts, group),
                row_block(experts, rows, 2),
                whole(group, width),
                per_slab(experts, width, hidden),
                whole(experts, width),
                whole(width, LANES),
                per_expert(experts, capacity, width),
                per_expert(experts, capacity, LANES),
                per_expert(experts, capacity, hidden),
                row_block(experts, rows, hidden),
            ],
            out_specs=(
                per_expert(experts, capacity, width),
                per_expert(experts, capacity, hidden),
                per_expert(experts, capacity, hidden),
                per_expert(experts, capacity, width),
                per_expert(experts, capacity, 1),
                row_block(experts, rows, hidden),
                row_block(experts, rows, hidden),
                whole(experts, group),
                ring_block(experts, width_mp, rows, width),
            ),
            scratch_shapes=[
                pltpu.VMEM((experts, 1, group), f32),
                pltpu.VMEM((experts * capacity, width), bf16),
                pltpu.VMEM((experts, group), bf16),
                pltpu.VMEM((experts, group), bf16),
            ],
        ),
        compiler_params=pltpu.CompilerParams(vmem_limit_bytes=VMEM),
        cost_estimate=SMALL,
        name="experts_main",
    )(
        lax.axis_index("mp").reshape(1),
        places.reshape(experts, 1, group),
        places,
        picked,
        h_two,
        in_w,
        router.T,
        jnp.pad(router, ((0, 0), (0, LANES - experts))),
        slots,
        named,
        back,
        shared_back,
    )


def slab_kernel(a_ref, b_ref, a_shared_ref, b_shared_ref, out_ref, *, experts):
    step = pl.program_id(0)

    @pl.when(step < experts)
    def _():
        out_ref[0] = dot(a_ref[0], b_ref[0], TN).astype(bf16)

    @pl.when(step == experts)
    def _():
        out_ref[0] = dot(a_shared_ref[...], b_shared_ref[...], TN).astype(bf16)


def slab_product(a, b, a_shared, b_shared, name):
    experts, capacity, width = a.shape
    hidden = b.shape[2]
    group = a_shared.shape[0]
    return pl.pallas_call(
        functools.partial(slab_kernel, experts=experts),
        out_shape=jax.ShapeDtypeStruct((experts + 1, width, hidden), bf16),
        grid=(experts + 1,),
        in_specs=[
            per_expert(experts, capacity, width),
            per_expert(experts, capacity, hidden),
            whole(group, width),
            whole(group, hidden),
        ],
        out_specs=per_slab(experts, width, hidden),
        compiler_params=pltpu.CompilerParams(vmem_limit_bytes=VMEM),
        cost_estimate=SMALL,
        name=name,
    )(a, b, a_shared, b_shared)


def branch_kernel(
    rank_ref, picked_ref, gate_ref, act_ref, weight_ref, shared_ref, out_ref, res_ref, *, experts
):
    step = pl.program_id(0)
    capacity = act_ref.shape[1]

    @pl.when(step < experts)
    def _():
        here = pl.ds(pl.multiple_of(step * capacity, capacity), capacity)
        res_ref[here, :] = (gate_ref[0] * dot(act_ref[0], weight_ref[0], NT)).astype(bf16)

    @pl.when(step >= experts)
    def _():
        total = dot(slots_of(picked_ref[...], experts * capacity), res_ref[...])
        out_ref[...] = (total + dot(shared_ref[...], weight_ref[0], NT)).astype(bf16)


def experts_out(picked, gates, act, out_t, shared_act):
    experts, capacity, hidden = act.shape
    group, width, width_mp = shared_act.shape[0], out_t.shape[1], lax.axis_size("mp")
    rows = group // width_mp
    return pl.pallas_call(
        functools.partial(branch_kernel, experts=experts),
        out_shape=jax.ShapeDtypeStruct((group, width), bf16),
        grid_spec=pltpu.PrefetchScalarGridSpec(
            num_scalar_prefetch=1,
            grid=(experts + width_mp,),
            in_specs=[
                row_block(experts, rows, 2),
                per_expert(experts, capacity, 1),
                per_expert(experts, capacity, hidden),
                per_slab(experts, width, hidden),
                row_block(experts, rows, hidden),
            ],
            out_specs=ring_block(experts, width_mp, rows, width),
            scratch_shapes=[pltpu.VMEM((experts * capacity, width), bf16)],
        ),
        compiler_params=pltpu.CompilerParams(vmem_limit_bytes=VMEM),
        cost_estimate=SMALL,
        name="experts_out",
    )(lax.axis_index("mp").reshape(1), picked, gates, act, out_t, shared_act)


def adamw_update(master, first, second, gradient, fan_in):
    step_rate = 0.5 * fan_in ** (-0.5)
    first_new = beta_one * first + (1.0 - beta_one) * gradient
    second_new = beta_two * second + (1.0 - beta_two) * gradient * gradient
    first_hat = first_new / (1.0 - beta_one**STEP)
    second_hat = second_new / (1.0 - beta_two**STEP)
    master_new = master - step_rate * (
        first_hat / (jnp.sqrt(second_hat) + epsilon) + weight_decay * master
    )
    return (master_new, first_new, second_new, master_new.astype(bf16))


def body(
    patches,
    cotangent,
    conditioning,
    lengths,
    routes,
    ada_weight,
    ada_first,
    ada_second,
    router_weight,
    router_first,
    router_second,
    qkv_weight,
    qkv_first,
    qkv_second,
    proj_weight,
    proj_first,
    proj_second,
    shared_in_weight,
    shared_in_first,
    shared_in_second,
    shared_out_weight,
    shared_out_first,
    shared_out_second,
    expert_in_weight,
    expert_in_first,
    expert_in_second,
    expert_out_weight,
    expert_out_first,
    expert_out_second,
):
    rows, D = patches.shape
    width = lax.axis_size("mp")
    n_dp = lax.axis_size("dp")
    devices = width * n_dp
    group = rows * width
    capacity = 5 * group // 16
    heads_here = H // width
    model_rank = lax.axis_index("mp")
    item_count = lengths.shape[1]
    hidden = shared_in_weight.shape[1]
    ada_cols = ada_weight.shape[1]
    router_cols = router_weight.shape[0]

    out_slab = jnp.concatenate(
        [
            jnp.swapaxes(expert_out_weight.astype(bf16), 1, 2),
            shared_out_weight.astype(bf16).T[None],
        ],
        axis=0,
    )
    in_slab = jnp.concatenate(
        [expert_in_weight.astype(bf16), shared_in_weight.astype(bf16)[None]], axis=0
    )
    out_t = lax.all_gather(out_slab, "dp", axis=1, tiled=True)
    proj_block = proj_weight.astype(bf16).T
    proj_shape = proj_block.shape
    proj_rows = proj_block.size // D
    fill = -proj_rows % 32

    def riding(blocks):
        return jnp.pad(blocks, ((0, 0),) * (blocks.ndim - 2) + ((0, fill), (0, 0)))

    patches_blocks = ring_gather(
        after(jnp.concatenate([patches, riding(proj_block.reshape(-1, D))], axis=0), out_slab)
    )

    def over_dp(values):
        parts = lax.all_to_all(
            values.reshape((n_dp, values.shape[0] // n_dp) + values.shape[1:]), "dp", 0, 0, tiled=True
        )
        return jnp.sum(parts.astype(f32), axis=0)

    def from_dp(values):
        parts = jnp.broadcast_to(values[None], (n_dp,) + values.shape)
        return lax.all_to_all(parts, "dp", 0, 0, tiled=True).reshape((-1,) + values.shape[1:])

    cond_all = lax.all_gather(conditioning, "dp", axis=0, tiled=True)
    cond_act = jax.nn.silu(cond_all.astype(f32)).astype(bf16)
    columns = jnp.dot(cond_act, ada_weight.astype(bf16), preferred_element_type=f32)
    columns = jnp.repeat(columns.reshape(n_dp, item_count * ada_cols), width, axis=0)
    router_low = router_weight.astype(bf16).astype(f32)
    payload = jnp.concatenate(
        [columns, jnp.broadcast_to(router_low[None], (devices, router_cols))], axis=1
    )
    received = lax.all_to_all(payload, ("dp", "mp"), 0, 0, tiled=True)
    qkv_here = lax.all_gather(
        after(qkv_weight.astype(bf16), cond_all), "dp", axis=0, tiled=True
    )
    modulation = (
        received[:, : item_count * ada_cols]
        .reshape(devices, item_count, ada_cols)
        .transpose(1, 0, 2)
        .reshape(item_count, devices * ada_cols)
    )
    router_matrix = received[:, item_count * ada_cols :].reshape(D, E).astype(bf16)
    bounds = jnp.cumsum(lengths[0])
    places = jnp.arange(group, dtype=jnp.int32)
    segment = jnp.sum((places[:, None] >= bounds[None, :]).astype(jnp.int32), axis=1)
    segment_column = segment[:, None]
    segment_mine = lax.dynamic_slice_in_dim(segment_column, model_rank * rows, rows, 0)
    start, kind = key_windows(lengths[0], group)

    chosen = routes[:, :, None] == jnp.arange(E, dtype=jnp.int32)[None, None, :]
    names = chosen.any(axis=1)
    below = (places[:, None] > places[None, :]).astype(bf16)
    earlier = jnp.dot(below, names.astype(bf16), preferred_element_type=f32).astype(jnp.int32)
    place_of = jnp.where(names, earlier, -1).T
    picked = routes * capacity + jnp.sum(jnp.where(chosen, earlier[:, None, :], 0), axis=2)
    names_low = jnp.pad(names.astype(bf16), ((0, 0), (0, LANES - E)))

    cot_blocks = ring_gather(after(cotangent, *patches_blocks))
    patches_all, h_one_all, qkv, qkv_wide = norm_one(
        patches_blocks, rows, modulation, segment_column, qkv_here
    )
    proj_here = jnp.concatenate(
        [b[rows : rows + proj_rows].reshape(proj_shape) for b in patches_blocks], axis=1
    )
    qkv, out_t = lax.optimization_barrier((qkv, out_t))
    in_w = lax.all_gather(after(in_slab, out_t), "dp", axis=1, tiled=True)
    proj_t = from_dp(after(proj_here, qkv))
    near, far = (1, width - 1), tuple(range(2, width - 1))
    mixed_here, logs, cot_near = lax.optimization_barrier(
        (*attend(qkv, start, kind), [cot_blocks[i] for i in near])
    )
    cot_near = dict(zip(near, cot_near))
    cot_blocks = [cot_near.get(i, block) for i, block in enumerate(cot_blocks)]
    mixed_blocks = ring_gather(mixed_here)
    (grad_branch,) = by_rows(
        gated_kernel,
        1,
        after(cot_blocks, mixed_here),
        rows,
        modulation,
        segment_column,
        "grad_branch",
    )
    held = experts_before(place_of, names_low, grad_branch, out_t, capacity, E // 2)
    held = experts_before(place_of, names_low, grad_branch, out_t, capacity, E // 2, held)
    mixed_blocks, held, proj_t = lax.optimization_barrier((mixed_blocks, held, proj_t))
    branch_slots, named_slots, back_slots, back_shared = held
    h_two, x_one_mine, attn_mine, mixed_mine, proj = norm_two(
        mixed_blocks, patches_all, proj_t, modulation, segment_column
    )

    (
        dispatched,
        expert_act,
        grad_expert_pre,
        grad_res,
        gates,
        shared_act,
        grad_shared_pre,
        grad_logits,
        grad_h_two,
    ) = experts_main(
        place_of,
        picked,
        h_two,
        in_w,
        router_matrix,
        branch_slots,
        named_slots,
        back_slots,
        back_shared,
    )
    two_terms = ring_scatter(grad_h_two)

    two_terms, grad_out_slab, mlp_part = sent_beside(
        two_terms,
        slab_product(grad_res, expert_act, grad_branch, shared_act, "grad_out"),
        lambda near: experts_out(picked, after(gates, near), expert_act, out_t, shared_act),
    )
    grad_out_mine = lax.psum_scatter(grad_out_slab, "dp", scatter_dimension=1, tiled=True)
    grad_x_one, grad_attn, grad_mixed_mine, sums_two = back_two(
        two_terms, x_one_mine, attn_mine, cotangent, proj, modulation, segment_mine
    )
    grad_mixed = lax.all_to_all(grad_mixed_mine, "mp", 0, 0, tiled=True)
    mlp_terms = ring_scatter(mlp_part)
    grad_in_slab = slab_product(
        after(dispatched, grad_mixed_mine), grad_expert_pre, h_two, grad_shared_pre, "grad_in"
    )
    grad_router = jnp.einsum(
        "gd,eg->de", h_two.astype(f32), after(grad_logits, grad_mixed_mine), precision=highest
    )
    grad_mixed, grad_router, grad_in_slab, mlp_near, grad_out_mine = lax.optimization_barrier(
        (grad_mixed, grad_router, grad_in_slab, [mlp_terms[i] for i in near], grad_out_mine)
    )
    grad_in_mine = lax.psum_scatter(
        after(grad_in_slab, grad_out_mine), "dp", scatter_dimension=1, tiled=True
    )
    grad_mixed = grad_mixed.transpose(1, 0, 2).reshape(heads_here * HD, group)
    grad_proj_t = jnp.einsum(
        "gd,cg->dc", after(grad_attn, grad_mixed), mixed_mine, preferred_element_type=f32
    )
    grad_proj_t = over_dp(grad_proj_t.astype(bf16)).astype(bf16)
    grad_qkv, grad_proj_t, mlp_far = lax.optimization_barrier(
        (
            attend_back(qkv, grad_mixed, logs, start, kind),
            grad_proj_t,
            [mlp_terms[i] for i in far],
        )
    )
    proj_parts = grad_proj_t.reshape(proj_shape[0], width, proj_shape[1]).transpose(1, 0, 2)
    partial = ring_product(grad_qkv, qkv_wide, riding(proj_parts.reshape(width, -1, D)))
    one_terms = ring_scatter(partial)
    grad_qkv = after(grad_qkv, partial)
    grad_qkv_weight = jnp.einsum("gd,gc->dc", h_one_all, grad_qkv, preferred_element_type=f32)
    grad_qkv_weight = grad_qkv_weight.reshape(D, heads_here * 3, LANES)[:, :, :HD]
    grad_qkv_weight = grad_qkv_weight.reshape(D, heads_here * 3 * HD).astype(bf16)
    one_terms, grad_qkv_weight, (result, sums_gate, grad_qkv_mine, grad_in_mine) = sent_beside(
        one_terms,
        grad_qkv_weight,
        lambda made: (
            *own_rows(
                outcome_kernel,
                after([mlp_terms[0], *mlp_near, *mlp_far], made),
                x_one_mine,
                cotangent,
                modulation,
                segment_mine,
                1,
                "outcome",
            ),
            over_dp(made),
            grad_in_mine,
        ),
    )
    patch_grad, sums_one = own_rows(
        back_one_kernel, one_terms, patches, grad_x_one, modulation, segment_mine, 2, "back_one"
    )
    grad_proj_mine = sum(
        t[rows : rows + proj_rows].astype(f32) for t in one_terms
    ).reshape(proj_shape)
    grad_modulation = jnp.concatenate([sums_one, sums_two, sums_gate], axis=1)
    payload = jnp.concatenate(
        [
            grad_modulation.reshape(item_count, devices, ada_cols)
            .transpose(1, 0, 2)
            .reshape(devices, item_count * ada_cols),
            grad_router.reshape(devices, router_cols),
        ],
        axis=1,
    )
    received = lax.all_to_all(payload, ("dp", "mp"), 0, 0, tiled=True)
    router_grad = jnp.sum(received[:, item_count * ada_cols :], axis=0)
    columns = jnp.sum(
        received[:, : item_count * ada_cols].reshape(n_dp, width, item_count, ada_cols), axis=1
    ).reshape(n_dp * item_count, ada_cols)
    ada_grad = jnp.einsum("id,ic->dc", cond_act.astype(f32), columns, precision=highest)
    grad_out_mine, grad_in_mine = grad_out_mine.astype(f32), grad_in_mine.astype(f32)

    gradients = (
        ada_grad,
        router_grad,
        grad_qkv_mine,
        grad_proj_mine.T,
        grad_in_mine[E],
        grad_out_mine[E].T,
        grad_in_mine[:E],
        jnp.swapaxes(grad_out_mine[:E], 1, 2),
    )
    states_of = (
        (ada_weight, ada_first, ada_second),
        (router_weight, router_first, router_second),
        (qkv_weight, qkv_first, qkv_second),
        (proj_weight, proj_first, proj_second),
        (shared_in_weight, shared_in_first, shared_in_second),
        (shared_out_weight, shared_out_first, shared_out_second),
        (expert_in_weight, expert_in_first, expert_in_second),
        (expert_out_weight, expert_out_first, expert_out_second),
    )
    total_hidden = float(hidden * width)
    fan_ins = (D, D, D, 8.0 * D / group, D, total_hidden, D, total_hidden)
    updates = []
    for (master, first, second), gradient, fan_in in zip(states_of, gradients, fan_ins):
        updates.extend(adamw_update(master, first, second, gradient, float(fan_in)))
    return tuple([result, patch_grad] + updates)


def solution(mesh):
    tokens, data = P(("dp", "mp"), None), P("dp", None)
    ada, router = P(None, ("dp", "mp")), P(("dp", "mp"))
    deep, wide = P("dp", "mp"), P("mp", "dp")
    deep_experts, wide_experts = P(None, "dp", "mp"), P(None, "mp", "dp")
    kinds = (ada, router, deep, wide, deep, wide, deep_experts, wide_experts)
    in_specs = (tokens, tokens, data, data, data) + tuple(k for k in kinds for _ in range(3))
    out_specs = (tokens, tokens) + tuple(k for k in kinds for _ in range(4))
    return jax.shard_map(body, mesh=mesh, in_specs=in_specs, out_specs=out_specs, check_vma=False)
```

```python
import functools
import math

import jax
import jax.numpy as jnp
import numpy as np
from jax import lax
from jax.experimental import pallas as pl
from jax.experimental.pallas import tpu as pltpu
from jax.sharding import PartitionSpec as P

H = 12
HD = 64
E = 8
STEP = 10

beta_one = 0.9
beta_two = 0.95
epsilon = 1e-08
weight_decay = 0.1
norm_floor = 1e-06
highest = lax.Precision.HIGHEST
f32 = jnp.float32
bf16 = jnp.bfloat16


def norm_parts(values):
    centred = values - jnp.mean(values, axis=1, keepdims=True)
    inverse = lax.rsqrt(jnp.mean(centred * centred, axis=1, keepdims=True) + norm_floor)
    return centred * inverse, inverse


def norm_back(normed, inverse, gradient):
    first = jnp.mean(gradient, axis=1, keepdims=True)
    second = jnp.mean(gradient * normed, axis=1, keepdims=True)
    return inverse * (gradient - first - normed * second)


def after(values, *earlier):
    return lax.optimization_barrier((values, earlier))[0]


def ring_gather(block):
    width = lax.axis_size("mp")
    return [block] + [
        lax.ppermute(block, "mp", [(i, (i + shift) % width) for i in range(width)])
        for shift in range(1, width)
    ]


def sent_beside(terms, near, far):
    width = len(terms)
    first = [i for i in range(1, width) if i in (1, width - 1)]
    later = [i for i in range(1, width) if i not in first]
    got, near = lax.optimization_barrier(([terms[i] for i in first], near))
    rest, far = lax.optimization_barrier(([terms[i] for i in later], far(near)))
    found = dict(zip(first + later, got + rest))
    return [terms[0]] + [found[i] for i in range(1, width)], near, far


def ring_scatter(parts):
    width = lax.axis_size("mp")
    return [parts[0]] + [
        lax.ppermute(parts[shift], "mp", [(i, (i - shift) % width) for i in range(width)])
        for shift in range(1, width)
    ]


LANES = 128
VMEM = 60 * 2**20
SMALL = pl.CostEstimate(flops=10**6, bytes_accessed=10**5, transcendentals=0)
Q_BLOCK = 256
FAR = 2.0**50
NT = (((1,), (1,)), ((), ()))
TN = (((0,), (0,)), ((), ()))
NN = (((1,), (0,)), ((), ()))


def dot(a, b, dims=NN):
    return lax.dot_general(a, b, dims, preferred_element_type=f32)


def key_widths(group):
    return sorted({min(w, group) for w in (512, 768, 1024, group)})


def key_windows(lengths, group):
    ends = jnp.cumsum(lengths)
    begins = ends - lengths
    first = jnp.arange(group // Q_BLOCK, dtype=jnp.int32) * Q_BLOCK
    last = first + Q_BLOCK - 1
    low = jnp.max(jnp.where(begins[None, :] <= first[:, None], begins[None, :], 0), axis=1)
    high = jnp.min(jnp.where(ends[None, :] > last[:, None], ends[None, :], group), axis=1)
    low = low // LANES * LANES
    widths = jnp.array(key_widths(group), jnp.int32)
    kind = jnp.sum((high - low)[:, None] > widths[None, :], axis=1).astype(jnp.int32)
    return jnp.minimum(low, group - widths[kind]).astype(jnp.int32), kind


def attend_kernel(start_ref, kind_ref, qkv_ref, mixed_ref, log_ref, *, group):
    block = pl.program_id(1)
    rows = pl.ds(pl.multiple_of(block * Q_BLOCK, Q_BLOCK), Q_BLOCK)
    query = qkv_ref[rows, 0:LANES] * jnp.asarray(HD**-0.5, bf16)
    for index, extent in enumerate(key_widths(group)):

        @pl.when(kind_ref[block] == index)
        def _():
            keys = pl.ds(pl.multiple_of(start_ref[block], LANES), extent)
            scores = dot(qkv_ref[keys, LANES : 2 * LANES], query, NT)
            peak = jnp.max(scores, axis=0, keepdims=True)
            exps = jnp.exp(scores - peak)
            total = jnp.sum(exps, axis=0, keepdims=True)
            probs = (exps * (1.0 / total)).astype(bf16)
            mixed = dot(qkv_ref[keys, 2 * LANES : 3 * LANES], probs, TN)
            mixed_ref[...] = mixed[:HD].astype(bf16)
            log_ref[...] = (peak + jnp.log(total))[None]


def attend(qkv, start, kind):
    group = qkv.shape[0]
    heads = qkv.shape[1] // (3 * LANES)
    blocks = group // Q_BLOCK
    return pl.pallas_call(
        functools.partial(attend_kernel, group=group),
        out_shape=(
            jax.ShapeDtypeStruct((heads * HD, group), bf16),
            jax.ShapeDtypeStruct((heads, 1, group), f32),
        ),
        grid_spec=pltpu.PrefetchScalarGridSpec(
            num_scalar_prefetch=2,
            grid=(heads, blocks),
            in_specs=[pl.BlockSpec((group, 3 * LANES), lambda h, i, *_: (0, h))],
            out_specs=(
                pl.BlockSpec((HD, Q_BLOCK), lambda h, i, *_: (h, i)),
                pl.BlockSpec((1, 1, Q_BLOCK), lambda h, i, *_: (h, 0, i)),
            ),
        ),
        compiler_params=pltpu.CompilerParams(vmem_limit_bytes=VMEM),
        cost_estimate=SMALL,
        name="attend",
    )(start, kind, qkv)


def attend_back_kernel(
    start_ref, kind_ref, qkv_ref, grad_ref, log_ref, out_ref, key_total, value_total, *, group
):
    block = pl.program_id(1)

    @pl.when(block == 0)
    def _():
        key_total[...] = jnp.zeros_like(key_total)
        value_total[...] = jnp.zeros_like(value_total)

    rows = pl.ds(pl.multiple_of(block * Q_BLOCK, Q_BLOCK), Q_BLOCK)
    scaling = HD**-0.5
    query = qkv_ref[rows, 0:LANES] * jnp.asarray(scaling, bf16)
    grad = grad_ref[...]
    kept = lax.broadcasted_iota(jnp.int32, (1, LANES), 1) < HD
    for index, extent in enumerate(key_widths(group)):

        @pl.when(kind_ref[block] == index)
        def _():
            keys = pl.ds(pl.multiple_of(start_ref[block], LANES), extent)
            key_rows = qkv_ref[keys, LANES : 2 * LANES]
            value_rows = qkv_ref[keys, 2 * LANES : 3 * LANES]
            probs = jnp.exp(dot(key_rows, query, NT) - log_ref[0])
            grad_probs = dot(value_rows[:, :HD], grad)
            middle = jnp.sum(probs * grad_probs, axis=0, keepdims=True)
            grad_scores = (probs * (grad_probs - middle)).astype(bf16)
            value_total[keys, :HD] += dot(probs.astype(bf16), grad, NT)
            key_total[keys, :] += dot(grad_scores, query)
            grad_query = dot(key_rows, grad_scores, TN).T * scaling
            out_ref[rows, 0:LANES] = jnp.where(kept, grad_query, 0.0).astype(bf16)

    @pl.when(block == pl.num_programs(1) - 1)
    def _():
        out_ref[:, LANES : 2 * LANES] = jnp.where(kept, key_total[...], 0.0).astype(bf16)
        out_ref[:, 2 * LANES : 3 * LANES] = value_total[...].astype(bf16)


def attend_back(qkv, grad_mixed, logs, start, kind):
    group = qkv.shape[0]
    heads = qkv.shape[1] // (3 * LANES)
    blocks = group // Q_BLOCK
    return pl.pallas_call(
        functools.partial(attend_back_kernel, group=group),
        out_shape=jax.ShapeDtypeStruct(qkv.shape, bf16),
        grid_spec=pltpu.PrefetchScalarGridSpec(
            num_scalar_prefetch=2,
            grid=(heads, blocks),
            in_specs=[
                pl.BlockSpec((group, 3 * LANES), lambda h, i, *_: (0, h)),
                pl.BlockSpec((HD, Q_BLOCK), lambda h, i, *_: (h, i)),
                pl.BlockSpec((1, 1, Q_BLOCK), lambda h, i, *_: (h, 0, i)),
            ],
            out_specs=pl.BlockSpec((group, 3 * LANES), lambda h, i, *_: (0, h)),
            scratch_shapes=[pltpu.VMEM((group, LANES), f32), pltpu.VMEM((group, LANES), f32)],
        ),
        compiler_params=pltpu.CompilerParams(vmem_limit_bytes=VMEM),
        cost_estimate=SMALL,
        name="attend_back",
    )(start, kind, qkv, grad_mixed, logs)


def item_rows(table_ref, term, width, segment, items):
    columns = slice(term * width, (term + 1) * width)
    rows = table_ref[0:1, columns]
    for item in range(1, items):
        rows = jnp.where(segment >= item, table_ref[item : item + 1, columns], rows)
    return rows


def item_sums(values, segment, items):
    return jnp.concatenate(
        [jnp.sum(jnp.where(segment == item, values, 0.0), axis=0, keepdims=True) for item in range(items)], axis=0
    )


def placed(width_mp):
    return lambda i, rank: (lax.rem(rank[0] - i + width_mp, width_mp), 0)


def plain(*shape):
    return pl.BlockSpec(shape, lambda i, rank: (0,) * len(shape))


def image_marks(heads, items):
    marks = np.zeros((items, heads, 3, LANES), np.float32)
    for image in range(items):
        for item in range(items):
            if image == item:
                marks[image, :, 0, HD + item] = FAR
            else:
                marks[image, :, 1, HD + item] = -FAR
    return marks.reshape(items, heads * 3 * LANES)


def norm_one_kernel(*refs, width_mp, items):
    rank_ref, segment_ref, table_ref, marks_ref, weight_ref = refs[:5]
    block_refs, (rows_ref, h_ref, qkv_ref, wide_ref) = refs[5:-4], refs[-4:]
    segment = segment_ref[...]
    width = rows_ref.shape[1]

    @pl.when(pl.program_id(0) == 0)
    def _():
        wide_ref[...] = jnp.zeros_like(wide_ref)
        for part in range(weight_ref.shape[1] // HD):
            wide_ref[:, part * LANES : part * LANES + HD] = weight_ref[:, part * HD : (part + 1) * HD]

    for place in range(width_mp):

        @pl.when(pl.program_id(0) == place)
        def _():
            rows_ref[...] = block_refs[place][...]

    normed, _ = norm_parts(rows_ref[...].astype(f32))
    shift = item_rows(table_ref, 0, width, segment, items)
    scale = item_rows(table_ref, 1, width, segment, items)
    h_one = (normed * (1.0 + scale) + shift).astype(bf16)
    h_ref[...] = h_one
    marks = item_rows(marks_ref, 0, qkv_ref.shape[1], segment, items)
    qkv_ref[...] = (dot(h_one, wide_ref[...]) + marks).astype(bf16)


def norm_one(arrays, rows, table, segment, weight):
    width_mp, width, items = len(arrays), arrays[0].shape[1], table.shape[0]
    heads = weight.shape[1] // (3 * HD)
    wide = heads * 3 * LANES
    marks = jnp.asarray(image_marks(heads, items))
    order = placed(width_mp)
    return pl.pallas_call(
        functools.partial(norm_one_kernel, width_mp=width_mp, items=items),
        out_shape=(
            jax.ShapeDtypeStruct((rows * width_mp, width), bf16),
            jax.ShapeDtypeStruct((rows * width_mp, width), bf16),
            jax.ShapeDtypeStruct((rows * width_mp, wide), bf16),
            jax.ShapeDtypeStruct((width, wide), bf16),
        ),
        grid_spec=pltpu.PrefetchScalarGridSpec(
            num_scalar_prefetch=1,
            grid=(width_mp,),
            in_specs=[pl.BlockSpec((rows, 1), order), plain(*table.shape), plain(*marks.shape), plain(*weight.shape)]
            + [plain(rows, width)] * len(arrays),
            out_specs=(
                pl.BlockSpec((rows, width), order),
                pl.BlockSpec((rows, width), order),
                pl.BlockSpec((rows, wide), order),
                plain(width, wide),
            ),
        ),
        compiler_params=pltpu.CompilerParams(vmem_limit_bytes=VMEM),
        cost_estimate=SMALL,
        name="norm_one",
    )(lax.axis_index("mp").reshape(1), segment, table, marks, weight, *arrays)


def gated_kernel(*refs, width_mp, items):
    rank_ref, segment_ref, table_ref = refs[:3]
    block_refs, out_ref = refs[3:-1], refs[-1]
    segment = segment_ref[...]
    width = out_ref.shape[1]
    for place in range(width_mp):

        @pl.when(pl.program_id(0) == place)
        def _():
            rows = block_refs[place][...].astype(f32)
            out_ref[...] = (item_rows(table_ref, 5, width, segment, items) * rows).astype(bf16)


def by_rows(kernel, outputs, arrays, rows, table, segment, name):
    width_mp, width, items = len(arrays), arrays[0].shape[1], table.shape[0]
    order = placed(width_mp)
    return pl.pallas_call(
        functools.partial(kernel, width_mp=width_mp, items=items),
        out_shape=(jax.ShapeDtypeStruct((rows * width_mp, width), bf16),) * outputs,
        grid_spec=pltpu.PrefetchScalarGridSpec(
            num_scalar_prefetch=1,
            grid=(width_mp,),
            in_specs=[pl.BlockSpec((rows, 1), order), plain(*table.shape)]
            + [plain(rows, width)] * len(arrays),
            out_specs=(pl.BlockSpec((rows, width), order),) * outputs,
        ),
        compiler_params=pltpu.CompilerParams(vmem_limit_bytes=VMEM),
        cost_estimate=SMALL,
        name=name,
    )(lax.axis_index("mp").reshape(1), segment, table, *arrays)


def norm_two_kernel(*refs, width_mp, items):
    rank_ref, segment_ref, table_ref, rows_ref, proj_ref = refs[:5]
    mixed_refs = refs[5:-4]
    h_ref, x_mine_ref, attn_mine_ref, mixed_mine_ref = refs[-4:]
    step = pl.program_id(0)
    rank = rank_ref[0]
    segment = segment_ref[...]
    width = rows_ref.shape[1]
    heads = mixed_refs[0].shape[0]

    attn = jnp.zeros(rows_ref.shape, f32)
    for place in range(width_mp):
        here = slice(place * heads, (place + 1) * heads)
        mixed = mixed_refs[place][...]
        attn += dot(mixed, proj_ref[here, :], TN)

        @pl.when(step == rank)
        def _():
            mixed_mine_ref[here, :] = mixed

    x_one = rows_ref[...].astype(f32) + item_rows(table_ref, 2, width, segment, items) * attn

    @pl.when(step == rank)
    def _():
        x_mine_ref[...] = x_one
        attn_mine_ref[...] = attn

    normed, _ = norm_parts(x_one)
    shift = item_rows(table_ref, 3, width, segment, items)
    scale = item_rows(table_ref, 4, width, segment, items)
    h_ref[...] = (normed * (1.0 + scale) + shift).astype(bf16)


def norm_two(arrays, patches, proj, table, segment):
    width_mp, (heads, group) = len(arrays), arrays[0].shape
    rows, width, items = group // width_mp, patches.shape[1], table.shape[0]
    every = heads * width_mp
    return pl.pallas_call(
        functools.partial(norm_two_kernel, width_mp=width_mp, items=items),
        out_shape=(
            jax.ShapeDtypeStruct((group, width), bf16),
            jax.ShapeDtypeStruct((rows, width), f32),
            jax.ShapeDtypeStruct((rows, width), f32),
            jax.ShapeDtypeStruct((every, rows), bf16),
        ),
        grid_spec=pltpu.PrefetchScalarGridSpec(
            num_scalar_prefetch=1,
            grid=(width_mp,),
            in_specs=[
                pl.BlockSpec((rows, 1), lambda i, rank: (i, 0)),
                plain(*table.shape),
                pl.BlockSpec((rows, width), lambda i, rank: (i, 0)),
                plain(*proj.shape),
            ]
            + [pl.BlockSpec((heads, rows), lambda i, rank: (0, i))] * len(arrays),
            out_specs=(
                pl.BlockSpec((rows, width), lambda i, rank: (i, 0)),
                plain(rows, width),
                plain(rows, width),
                plain(every, rows),
            ),
        ),
        compiler_params=pltpu.CompilerParams(vmem_limit_bytes=VMEM),
        cost_estimate=SMALL,
        name="norm_two",
    )(lax.axis_index("mp").reshape(1), segment, table, patches, proj, *arrays)


def product_kernel(rank_ref, a_ref, b_ref, part_ref, *out_refs):
    rows = a_ref.shape[0]
    for place, out_ref in enumerate(out_refs):

        @pl.when(pl.program_id(0) == place)
        def _():
            out_ref[0:rows, :] = dot(a_ref[...], b_ref[...], NT).astype(bf16)
            out_ref[rows:, :] = part_ref[0]


def ring_product(a, b, parts):
    width_mp, extra, width = parts.shape
    rows = a.shape[0] // width_mp
    return pl.pallas_call(
        product_kernel,
        out_shape=(jax.ShapeDtypeStruct((rows + extra, width), bf16),) * width_mp,
        grid_spec=pltpu.PrefetchScalarGridSpec(
            num_scalar_prefetch=1,
            grid=(width_mp,),
            in_specs=[
                pl.BlockSpec((rows, a.shape[1]), placed(width_mp)),
                plain(*b.shape),
                pl.BlockSpec((1, extra, width), lambda i, rank: (i, 0, 0)),
            ],
            out_specs=(plain(rows + extra, width),) * width_mp,
        ),
        compiler_params=pltpu.CompilerParams(vmem_limit_bytes=VMEM),
        cost_estimate=SMALL,
        name="grad_h_one",
    )(lax.axis_index("mp").reshape(1), a, b, parts)


def term_sum(refs):
    return functools.reduce(lambda total, ref: total + ref[...].astype(f32), refs[1:], refs[0][...].astype(f32))


def back_two_kernel(rank_ref, segment_ref, table_ref, *refs, width_mp, items):
    term_refs, (x_ref, attn_ref, cot_ref, proj_ref) = refs[:width_mp], refs[width_mp:-4]
    grad_x_ref, grad_attn_ref, grad_mixed_ref, sums_ref = refs[-4:]
    segment = segment_ref[...]
    width = x_ref.shape[1]
    heads = proj_ref.shape[0] // width_mp
    grad = term_sum(term_refs)
    normed, inverse = norm_parts(x_ref[...])
    scale = item_rows(table_ref, 4, width, segment, items)
    grad_x = cot_ref[...].astype(f32) + norm_back(normed, inverse, grad * (1.0 + scale))
    grad_x_ref[...] = grad_x
    grad_attn = (item_rows(table_ref, 2, width, segment, items) * grad_x).astype(bf16)
    grad_attn_ref[...] = grad_attn
    for place in range(width_mp):
        owner = lax.rem(rank_ref[0] - place + width_mp, width_mp)
        part = dot(proj_ref[place * heads : (place + 1) * heads, :], grad_attn, NT)
        grad_mixed_ref[owner] = part.astype(bf16)
    sums_ref[:, 0:width] = item_sums(grad_x * attn_ref[...], segment, items)
    sums_ref[:, width : 2 * width] = item_sums(grad, segment, items)
    sums_ref[:, 2 * width :] = item_sums(grad * normed, segment, items)


def back_two(terms, x_one, attn, cotangent, proj, table, segment):
    rows, width = x_one.shape
    items, width_mp = table.shape[0], lax.axis_size("mp")
    shapes = (
        jax.ShapeDtypeStruct((rows, width), f32),
        jax.ShapeDtypeStruct((rows, width), bf16),
        jax.ShapeDtypeStruct((width_mp, proj.shape[0] // width_mp, rows), bf16),
        jax.ShapeDtypeStruct((items, 3 * width), f32),
    )
    operands = (segment, table, *(t for t in terms), x_one, attn, cotangent, proj)
    return pl.pallas_call(
        functools.partial(back_two_kernel, width_mp=width_mp, items=items),
        out_shape=shapes,
        grid_spec=pltpu.PrefetchScalarGridSpec(
            num_scalar_prefetch=1,
            grid=(1,),
            in_specs=[plain(*o.shape) for o in operands],
            out_specs=tuple(plain(*o.shape) for o in shapes),
        ),
        compiler_params=pltpu.CompilerParams(vmem_limit_bytes=VMEM),
        cost_estimate=SMALL,
        name="back_two",
    )(lax.axis_index("mp").reshape(1), *operands)


def back_one_kernel(segment_ref, table_ref, *refs, items):
    term_refs, (patches_ref, grad_x_ref, grad_ref, sums_ref) = refs[:-4], refs[-4:]
    segment = segment_ref[...]
    width = patches_ref.shape[1]
    grad = term_sum(term_refs)
    normed, inverse = norm_parts(patches_ref[...].astype(f32))
    scale = item_rows(table_ref, 1, width, segment, items)
    grad_ref[...] = (grad_x_ref[...] + norm_back(normed, inverse, grad * (1.0 + scale))).astype(bf16)
    sums_ref[:, 0:width] = item_sums(grad, segment, items)
    sums_ref[:, width:] = item_sums(grad * normed, segment, items)


def outcome_kernel(segment_ref, table_ref, *refs, items):
    term_refs, (x_ref, cot_ref, out_ref, sums_ref) = refs[:-4], refs[-4:]
    segment = segment_ref[...]
    width = x_ref.shape[1]
    branch = term_sum(term_refs)
    gate = item_rows(table_ref, 5, width, segment, items)
    out_ref[...] = (x_ref[...] + gate * branch).astype(bf16)
    sums_ref[...] = item_sums(cot_ref[...].astype(f32) * branch, segment, items)


def own_rows(kernel, terms, first, second, table, segment, sums, name):
    rows, width = first.shape
    items = table.shape[0]
    shapes = (
        jax.ShapeDtypeStruct((rows, width), bf16),
        jax.ShapeDtypeStruct((items, sums * width), f32),
    )

    def single(*shape):
        return pl.BlockSpec(shape, lambda i: (0,) * len(shape))

    return pl.pallas_call(
        functools.partial(kernel, items=items),
        out_shape=shapes,
        grid=(1,),
        in_specs=[single(*segment.shape), single(*table.shape)]
        + [single(rows, width)] * (len(terms) + 2),
        out_specs=tuple(single(*o.shape) for o in shapes),
        compiler_params=pltpu.CompilerParams(vmem_limit_bytes=VMEM),
        cost_estimate=SMALL,
        name=name,
    )(segment, table, *terms, first, second)


def gelu_terms(before):
    slope = (2.0 / math.pi) ** 0.5
    square = before * before
    curve = jnp.tanh(slope * before * (1.0 + 0.044715 * square))
    half = 0.5 * (1.0 + curve)
    value = before * half
    derivative = half + (0.5 * slope) * before * (1.0 - curve * curve) * (1.0 + 0.134145 * square)
    return value, derivative


def slot_picks(place_row, capacity):
    slots = lax.broadcasted_iota(jnp.int32, (capacity, place_row.shape[1]), 0)
    return slots == place_row


def row_chunks(group):
    return [slice(first, first + 512) for first in range(0, group, 512)]


def before_kernel(
    place_ref, named_ref, branch_ref, weight_ref, *refs, count, shared
):
    slots_ref, named_slots_ref, back_ref = refs[-4:-1] if shared else refs[-3:]
    step = pl.program_id(0)

    @pl.when(step < count)
    def _():
        picks = slot_picks(place_ref[0], slots_ref.shape[1]).astype(bf16)
        slots = dot(picks, branch_ref[...]).astype(bf16)
        slots_ref[0] = slots
        named_slots_ref[0] = dot(picks, named_ref[...]).astype(bf16)
        back_ref[0] = dot(slots, weight_ref[0]).astype(bf16)

    if shared:

        @pl.when(step == count)
        def _():
            for chunk in row_chunks(branch_ref.shape[0]):
                refs[-1][chunk, :] = dot(branch_ref[chunk, :], weight_ref[0]).astype(bf16)


def whole(*shape):
    return pl.BlockSpec(shape, lambda *_: (0,) * len(shape), pipeline_mode=pl.Buffered(1))


def per_expert(experts, *shape):
    return pl.BlockSpec(
        (1,) + shape, lambda e, *_: (jnp.minimum(e, experts - 1),) + (0,) * len(shape)
    )


def per_slab(experts, *shape):
    return pl.BlockSpec((1,) + shape, lambda e, *_: (jnp.minimum(e, experts),) + (0,) * len(shape))


def experts_before(places, named, branch, out_t, capacity, first, held=None):
    group, width = branch.shape
    experts, hidden = out_t.shape[0] - 1, out_t.shape[2]
    base, count = (0, first) if held is None else (first, experts - first)
    shapes = (
        jax.ShapeDtypeStruct((experts, capacity, width), bf16),
        jax.ShapeDtypeStruct((experts, capacity, LANES), bf16),
        jax.ShapeDtypeStruct((experts, capacity, hidden), bf16),
    )

    def mine(*shape):
        return pl.BlockSpec(
            (1,) + shape, lambda e: (base + jnp.minimum(e, count - 1),) + (0,) * len(shape)
        )

    shared = held is not None
    return pl.pallas_call(
        functools.partial(before_kernel, count=count, shared=shared),
        out_shape=shapes + (jax.ShapeDtypeStruct((group, hidden), bf16),) * shared,
        grid=(count + shared,),
        in_specs=[
            mine(1, group),
            whole(group, LANES),
            whole(group, width),
            pl.BlockSpec((1, width, hidden), lambda e: (base + e, 0, 0)),
        ]
        + [pl.BlockSpec(memory_space=pl.ANY)] * (3 * shared),
        out_specs=(mine(capacity, width), mine(capacity, LANES), mine(capacity, hidden))
        + (whole(group, hidden),) * shared,
        input_output_aliases={4: 0, 5: 1, 6: 2} if shared else {},
        compiler_params=pltpu.CompilerParams(vmem_limit_bytes=VMEM),
        cost_estimate=SMALL,
        name="experts_before",
    )(places.reshape(experts, 1, group), named, branch, out_t, *(held or ()))


def slots_of(picked, slots):
    index = lax.broadcasted_iota(jnp.int32, (picked.shape[0], slots), 1)
    return ((index == picked[:, 0:1]) | (index == picked[:, 1:2])).astype(bf16)


def ring_store(out_refs, rank, owner, block):
    width_mp = len(out_refs)
    for place, out_ref in enumerate(out_refs):

        @pl.when(lax.rem(rank - owner + width_mp, width_mp) == place)
        def _():
            out_ref[...] = block


def experts_kernel(*refs, experts):
    rank_ref, place_ref, places_ref, picked_ref, rows_ref, weight_ref = refs[:6]
    router_ref, router_wide_ref, named_ref, back_ref, shared_back_ref = refs[6:11]
    dispatched_ref, act_ref, grad_pre_ref, gate_ref = refs[11:15]
    shared_act_ref, shared_grad_ref, grad_logits_ref = refs[15:18]
    grad_rows_refs = refs[18:-4]
    grad_gates_ref, grad_slots_ref, high_ref, rest_ref = refs[-4:]
    step = pl.program_id(0)
    group = rows_ref.shape[0]
    capacity = back_ref.shape[1]

    @pl.when(step < experts)
    def _():
        picks = slot_picks(place_ref[0], capacity)
        dispatched = dot(picks.astype(bf16), rows_ref[...]).astype(bf16)
        dispatched_ref[0] = dispatched
        pre = dot(dispatched, weight_ref[0])
        logits = dot(dispatched, router_wide_ref[...])
        lane = lax.broadcasted_iota(jnp.int32, logits.shape, 1)
        named = named_ref[0].astype(f32) > 0.0
        peak = jnp.max(jnp.where(named, logits, -jnp.inf), axis=1, keepdims=True)
        shares = jnp.where(named, jnp.exp(logits - peak), 0.0)
        total = jnp.sum(shares, axis=1, keepdims=True)
        own = jnp.sum(jnp.where(lane == step, shares, 0.0), axis=1, keepdims=True)
        gate = jnp.where(total > 0.0, own / jnp.maximum(total, 1.0), 0.0)
        gate_ref[0] = gate
        value, slope = gelu_terms(pre)
        act = value.astype(bf16)
        act_ref[0] = act
        back = back_ref[0].astype(f32)
        grad_pre = (gate * back * slope).astype(bf16)
        grad_pre_ref[0] = grad_pre
        grad_gate = jnp.sum(back * act.astype(f32), axis=1, keepdims=True)
        grad_gates_ref[step] = jnp.sum(jnp.where(picks, grad_gate, 0.0), axis=0, keepdims=True)
        here = pl.ds(pl.multiple_of(step * capacity, capacity), capacity)
        grad_slots_ref[here, :] = dot(grad_pre, weight_ref[0], NT).astype(bf16)

    @pl.when(step == experts)
    def _():
        logits = dot(router_ref[...], rows_ref[...], NT)
        named = places_ref[...] >= 0
        peak = jnp.max(jnp.where(named, logits, -jnp.inf), axis=0, keepdims=True)
        shares = jnp.where(named, jnp.exp(logits - peak), 0.0)
        gates = shares / jnp.sum(shares, axis=0, keepdims=True)
        grad_gates = jnp.concatenate([grad_gates_ref[e] for e in range(experts)], axis=0)
        grad_logits = gates * (grad_gates - jnp.sum(gates * grad_gates, axis=0, keepdims=True))
        grad_logits_ref[...] = grad_logits
        high = grad_logits.astype(bf16)
        high_ref[...] = high
        rest_ref[...] = (grad_logits - high.astype(f32)).astype(bf16)

    @pl.when(step >= experts)
    def _():
        size = shared_act_ref.shape[0]
        here = pl.ds(pl.multiple_of((step - experts) * size, size), size)
        value, slope = gelu_terms(dot(rows_ref[here, :], weight_ref[0]))
        shared_act_ref[...] = value.astype(bf16)
        grad_pre = (shared_back_ref[...].astype(f32) * slope).astype(bf16)
        shared_grad_ref[...] = grad_pre
        total = dot(slots_of(picked_ref[...], experts * capacity), grad_slots_ref[...])
        total += dot(grad_pre, weight_ref[0], NT)
        total += dot(high_ref[:, here], router_ref[...], TN)
        total += dot(rest_ref[:, here], router_ref[...], TN)
        ring_store(grad_rows_refs, rank_ref[0], step - experts, total.astype(bf16))


def row_block(experts, *shape):
    return pl.BlockSpec(shape, lambda e, *_: (jnp.maximum(e - experts, 0), 0))


def experts_main(places, picked, h_two, in_w, router, named, back, shared_back):
    group, width = h_two.shape
    experts, capacity, hidden = back.shape
    width_mp = lax.axis_size("mp")
    rows = group // width_mp
    unit_shape = jax.ShapeDtypeStruct((experts, capacity, hidden), bf16)
    return pl.pallas_call(
        functools.partial(experts_kernel, experts=experts),
        out_shape=(
            jax.ShapeDtypeStruct((experts, capacity, width), bf16),
            unit_shape,
            unit_shape,
            jax.ShapeDtypeStruct((experts, capacity, 1), f32),
            jax.ShapeDtypeStruct((group, hidden), bf16),
            jax.ShapeDtypeStruct((group, hidden), bf16),
            jax.ShapeDtypeStruct((experts, group), f32),
        )
        + (jax.ShapeDtypeStruct((rows, width), bf16),) * width_mp,
        grid_spec=pltpu.PrefetchScalarGridSpec(
            num_scalar_prefetch=1,
            grid=(experts + width_mp,),
            in_specs=[
                per_expert(experts, 1, group),
                whole(experts, group),
                row_block(experts, rows, 2),
                whole(group, width),
                per_slab(experts, width, hidden),
                whole(experts, width),
                whole(width, LANES),
                per_expert(experts, capacity, LANES),
                per_expert(experts, capacity, hidden),
                row_block(experts, rows, hidden),
            ],
            out_specs=(
                per_expert(experts, capacity, width),
                per_expert(experts, capacity, hidden),
                per_expert(experts, capacity, hidden),
                per_expert(experts, capacity, 1),
                row_block(experts, rows, hidden),
                row_block(experts, rows, hidden),
                whole(experts, group),
            )
            + (whole(rows, width),) * width_mp,
            scratch_shapes=[
                pltpu.VMEM((experts, 1, group), f32),
                pltpu.VMEM((experts * capacity, width), bf16),
                pltpu.VMEM((experts, group), bf16),
                pltpu.VMEM((experts, group), bf16),
            ],
        ),
        compiler_params=pltpu.CompilerParams(vmem_limit_bytes=VMEM),
        cost_estimate=SMALL,
        name="experts_main",
    )(
        lax.axis_index("mp").reshape(1),
        places.reshape(experts, 1, group),
        places,
        picked,
        h_two,
        in_w,
        router.T,
        jnp.pad(router, ((0, 0), (0, LANES - experts))),
        named,
        back,
        shared_back,
    )


def slab_kernel(a_ref, b_ref, a_shared_ref, b_shared_ref, *refs, experts):
    step = pl.program_id(0)
    out_ref = refs[-1]

    @pl.when(step < experts)
    def _():
        a = a_ref[0]
        if len(refs) > 1:
            a = (refs[0][0] * a.astype(f32)).astype(bf16)
        out_ref[0] = dot(a, b_ref[0], TN).astype(bf16)

    @pl.when(step == experts)
    def _():
        out_ref[0] = dot(a_shared_ref[...], b_shared_ref[...], TN).astype(bf16)


def slab_product(a, b, a_shared, b_shared, name, gates=None):
    experts, capacity, width = a.shape
    hidden = b.shape[2]
    group = a_shared.shape[0]
    scaled = gates is not None
    return pl.pallas_call(
        functools.partial(slab_kernel, experts=experts),
        out_shape=jax.ShapeDtypeStruct((experts + 1, width, hidden), bf16),
        grid=(experts + 1,),
        in_specs=[
            per_expert(experts, capacity, width),
            per_expert(experts, capacity, hidden),
            whole(group, width),
            whole(group, hidden),
        ]
        + [per_expert(experts, capacity, 1)] * scaled,
        out_specs=per_slab(experts, width, hidden),
        compiler_params=pltpu.CompilerParams(vmem_limit_bytes=VMEM),
        cost_estimate=SMALL,
        name=name,
    )(a, b, a_shared, b_shared, *((gates,) * scaled))


def branch_kernel(
    rank_ref, picked_ref, gate_ref, act_ref, weight_ref, shared_ref, *refs, experts
):
    out_refs, res_ref = refs[:-1], refs[-1]
    step = pl.program_id(0)
    capacity = act_ref.shape[1]

    @pl.when(step < experts)
    def _():
        here = pl.ds(pl.multiple_of(step * capacity, capacity), capacity)
        res_ref[here, :] = (gate_ref[0] * dot(act_ref[0], weight_ref[0], NT)).astype(bf16)

    @pl.when(step >= experts)
    def _():
        total = dot(slots_of(picked_ref[...], experts * capacity), res_ref[...])
        total += dot(shared_ref[...], weight_ref[0], NT)
        ring_store(out_refs, rank_ref[0], step - experts, total.astype(bf16))


def experts_out(picked, gates, act, out_t, shared_act):
    experts, capacity, hidden = act.shape
    group, width, width_mp = shared_act.shape[0], out_t.shape[1], lax.axis_size("mp")
    rows = group // width_mp
    return pl.pallas_call(
        functools.partial(branch_kernel, experts=experts),
        out_shape=(jax.ShapeDtypeStruct((rows, width), bf16),) * width_mp,
        grid_spec=pltpu.PrefetchScalarGridSpec(
            num_scalar_prefetch=1,
            grid=(experts + width_mp,),
            in_specs=[
                row_block(experts, rows, 2),
                per_expert(experts, capacity, 1),
                per_expert(experts, capacity, hidden),
                per_slab(experts, width, hidden),
                row_block(experts, rows, hidden),
            ],
            out_specs=(whole(rows, width),) * width_mp,
            scratch_shapes=[pltpu.VMEM((experts * capacity, width), bf16)],
        ),
        compiler_params=pltpu.CompilerParams(vmem_limit_bytes=VMEM),
        cost_estimate=SMALL,
        name="experts_out",
    )(lax.axis_index("mp").reshape(1), picked, gates, act, out_t, shared_act)


def adamw_update(master, first, second, gradient, fan_in):
    step_rate = 0.5 * fan_in ** (-0.5)
    first_new = beta_one * first + (1.0 - beta_one) * gradient
    second_new = beta_two * second + (1.0 - beta_two) * gradient * gradient
    first_hat = first_new / (1.0 - beta_one**STEP)
    second_hat = second_new / (1.0 - beta_two**STEP)
    master_new = master - step_rate * (
        first_hat / (jnp.sqrt(second_hat) + epsilon) + weight_decay * master
    )
    return (master_new, first_new, second_new, master_new.astype(bf16))


def body(
    patches,
    cotangent,
    conditioning,
    lengths,
    routes,
    ada_weight,
    ada_first,
    ada_second,
    router_weight,
    router_first,
    router_second,
    qkv_weight,
    qkv_first,
    qkv_second,
    proj_weight,
    proj_first,
    proj_second,
    shared_in_weight,
    shared_in_first,
    shared_in_second,
    shared_out_weight,
    shared_out_first,
    shared_out_second,
    expert_in_weight,
    expert_in_first,
    expert_in_second,
    expert_out_weight,
    expert_out_first,
    expert_out_second,
):
    rows, D = patches.shape
    width = lax.axis_size("mp")
    n_dp = lax.axis_size("dp")
    devices = width * n_dp
    group = rows * width
    capacity = 5 * group // 16
    heads_here = H // width
    model_rank = lax.axis_index("mp")
    item_count = lengths.shape[1]
    hidden = shared_in_weight.shape[1]
    ada_cols = ada_weight.shape[1]
    router_cols = router_weight.shape[0]

    out_slab = jnp.concatenate(
        [
            jnp.swapaxes(expert_out_weight.astype(bf16), 1, 2),
            shared_out_weight.astype(bf16).T[None],
        ],
        axis=0,
    )
    in_slab = jnp.concatenate(
        [expert_in_weight.astype(bf16), shared_in_weight.astype(bf16)[None]], axis=0
    )
    out_t = lax.all_gather(out_slab, "dp", axis=1, tiled=True)
    proj_block = proj_weight.astype(bf16).T
    proj_shape = proj_block.shape
    proj_rows = proj_block.size // D
    fill = -proj_rows % 32

    def riding(blocks):
        return jnp.pad(blocks, ((0, 0),) * (blocks.ndim - 2) + ((0, fill), (0, 0)))

    patches_blocks = ring_gather(
        after(jnp.concatenate([patches, riding(proj_block.reshape(-1, D))], axis=0), out_slab)
    )

    def over_dp(values):
        parts = lax.all_to_all(
            values.reshape((n_dp, values.shape[0] // n_dp) + values.shape[1:]), "dp", 0, 0, tiled=True
        )
        return jnp.sum(parts.astype(f32), axis=0)

    def from_dp(values):
        parts = jnp.broadcast_to(values[None], (n_dp,) + values.shape)
        return lax.all_to_all(parts, "dp", 0, 0, tiled=True).reshape((-1,) + values.shape[1:])

    cond_all = lax.all_gather(conditioning, "dp", axis=0, tiled=True)
    cond_act = jax.nn.silu(cond_all.astype(f32)).astype(bf16)
    columns = jnp.dot(cond_act, ada_weight.astype(bf16), preferred_element_type=f32)
    columns = jnp.repeat(columns.reshape(n_dp, item_count * ada_cols), width, axis=0)
    router_low = router_weight.astype(bf16).astype(f32)
    payload = jnp.concatenate(
        [columns, jnp.broadcast_to(router_low[None], (devices, router_cols))], axis=1
    )
    received = lax.all_to_all(payload, ("dp", "mp"), 0, 0, tiled=True)
    qkv_here = lax.all_gather(
        after(qkv_weight.astype(bf16), cond_all), "dp", axis=0, tiled=True
    )
    modulation = (
        received[:, : item_count * ada_cols]
        .reshape(devices, item_count, ada_cols)
        .transpose(1, 0, 2)
        .reshape(item_count, devices * ada_cols)
    )
    router_matrix = received[:, item_count * ada_cols :].reshape(D, E).astype(bf16)
    bounds = jnp.cumsum(lengths[0])
    places = jnp.arange(group, dtype=jnp.int32)
    segment = jnp.sum((places[:, None] >= bounds[None, :]).astype(jnp.int32), axis=1)
    segment_column = segment[:, None]
    segment_mine = lax.dynamic_slice_in_dim(segment_column, model_rank * rows, rows, 0)
    start, kind = key_windows(lengths[0], group)

    chosen = routes[:, :, None] == jnp.arange(E, dtype=jnp.int32)[None, None, :]
    names = chosen.any(axis=1)
    below = (places[:, None] > places[None, :]).astype(bf16)
    earlier = jnp.dot(below, names.astype(bf16), preferred_element_type=f32).astype(jnp.int32)
    place_of = jnp.where(names, earlier, -1).T
    picked = routes * capacity + jnp.sum(jnp.where(chosen, earlier[:, None, :], 0), axis=2)
    names_low = jnp.pad(names.astype(bf16), ((0, 0), (0, LANES - E)))

    cot_blocks = ring_gather(after(cotangent, *patches_blocks))
    patches_all, h_one_all, qkv, qkv_wide = norm_one(
        patches_blocks, rows, modulation, segment_column, qkv_here
    )
    proj_here = jnp.concatenate(
        [b[rows : rows + proj_rows].reshape(proj_shape) for b in patches_blocks], axis=1
    )
    qkv, out_t = lax.optimization_barrier((qkv, out_t))
    in_w = lax.all_gather(after(in_slab, out_t), "dp", axis=1, tiled=True)
    proj_t = from_dp(after(proj_here, qkv))
    near, far = (1, width - 1), tuple(range(2, width - 1))
    mixed_here, logs, cot_near = lax.optimization_barrier(
        (*attend(qkv, start, kind), [cot_blocks[i] for i in near])
    )
    cot_near = dict(zip(near, cot_near))
    cot_blocks = [cot_near.get(i, block) for i, block in enumerate(cot_blocks)]
    mixed_blocks = ring_gather(mixed_here)
    proj = after(proj_t, mixed_here).T
    proj, cot_blocks = lax.optimization_barrier((proj, cot_blocks))
    (grad_branch,) = by_rows(
        gated_kernel,
        1,
        after(cot_blocks, mixed_here),
        rows,
        modulation,
        segment_column,
        "grad_branch",
    )
    held = experts_before(place_of, names_low, grad_branch, out_t, capacity, E // 2)
    held = experts_before(place_of, names_low, grad_branch, out_t, capacity, E // 2, held)
    mixed_blocks, held = lax.optimization_barrier((mixed_blocks, held))
    branch_slots, named_slots, back_slots, back_shared = held
    h_two, x_one_mine, attn_mine, mixed_mine = norm_two(
        mixed_blocks, patches_all, proj, modulation, segment_column
    )

    (
        dispatched,
        expert_act,
        grad_expert_pre,
        gates,
        shared_act,
        grad_shared_pre,
        grad_logits,
        *grad_h_two,
    ) = experts_main(
        place_of,
        picked,
        h_two,
        in_w,
        router_matrix,
        named_slots,
        back_slots,
        back_shared,
    )
    two_terms = ring_scatter(grad_h_two)

    two_terms, grad_out_slab, mlp_part = sent_beside(
        two_terms,
        slab_product(branch_slots, expert_act, grad_branch, shared_act, "grad_out", gates),
        lambda near: experts_out(picked, after(gates, near), expert_act, out_t, shared_act),
    )
    grad_out_mine = lax.psum_scatter(grad_out_slab, "dp", scatter_dimension=1, tiled=True)
    grad_x_one, grad_attn, grad_mixed_mine, sums_two = back_two(
        two_terms, x_one_mine, attn_mine, cotangent, proj, modulation, segment_mine
    )
    grad_mixed = lax.all_to_all(grad_mixed_mine, "mp", 0, 0, tiled=True)
    mlp_terms = ring_scatter(mlp_part)
    grad_in_slab = slab_product(
        after(dispatched, grad_mixed_mine), grad_expert_pre, h_two, grad_shared_pre, "grad_in"
    )
    grad_router = jnp.einsum(
        "gd,eg->de", h_two.astype(f32), after(grad_logits, grad_mixed_mine), precision=highest
    )
    grad_mixed, grad_router, grad_in_slab, mlp_near, grad_out_mine = lax.optimization_barrier(
        (grad_mixed, grad_router, grad_in_slab, [mlp_terms[i] for i in near], grad_out_mine)
    )
    grad_in_mine = lax.psum_scatter(
        after(grad_in_slab, grad_out_mine), "dp", scatter_dimension=1, tiled=True
    )
    grad_mixed = grad_mixed.transpose(1, 0, 2).reshape(heads_here * HD, group)
    grad_proj_t = jnp.einsum(
        "gd,cg->dc", after(grad_attn, grad_mixed), mixed_mine, preferred_element_type=f32
    )
    grad_proj_t = over_dp(grad_proj_t.astype(bf16)).astype(bf16)
    grad_qkv, grad_proj_t, mlp_far = lax.optimization_barrier(
        (
            attend_back(qkv, grad_mixed, logs, start, kind),
            grad_proj_t,
            [mlp_terms[i] for i in far],
        )
    )
    proj_parts = grad_proj_t.reshape(proj_shape[0], width, proj_shape[1]).transpose(1, 0, 2)
    partial = ring_product(grad_qkv, qkv_wide, riding(proj_parts.reshape(width, -1, D)))
    one_terms = ring_scatter(partial)
    grad_qkv = after(grad_qkv, partial)
    grad_qkv_weight = jnp.einsum("gd,gc->dc", h_one_all, grad_qkv, preferred_element_type=f32)
    grad_qkv_weight = grad_qkv_weight.reshape(D, heads_here * 3, LANES)[:, :, :HD]
    grad_qkv_weight = grad_qkv_weight.reshape(D, heads_here * 3 * HD).astype(bf16)
    one_terms, grad_qkv_weight, (result, sums_gate, grad_qkv_mine, grad_in_mine) = sent_beside(
        one_terms,
        grad_qkv_weight,
        lambda made: (
            *own_rows(
                outcome_kernel,
                after([mlp_terms[0], *mlp_near, *mlp_far], made),
                x_one_mine,
                cotangent,
                modulation,
                segment_mine,
                1,
                "outcome",
            ),
            over_dp(made),
            grad_in_mine,
        ),
    )
    patch_grad, sums_one = own_rows(
        back_one_kernel, one_terms, patches, grad_x_one, modulation, segment_mine, 2, "back_one"
    )
    grad_proj_mine = sum(
        t[rows : rows + proj_rows].astype(f32) for t in one_terms
    ).reshape(proj_shape)
    grad_modulation = jnp.concatenate([sums_one, sums_two, sums_gate], axis=1)
    payload = jnp.concatenate(
        [
            grad_modulation.reshape(item_count, devices, ada_cols)
            .transpose(1, 0, 2)
            .reshape(devices, item_count * ada_cols),
            grad_router.reshape(devices, router_cols),
        ],
        axis=1,
    )
    received = lax.all_to_all(payload, ("dp", "mp"), 0, 0, tiled=True)
    router_grad = jnp.sum(received[:, item_count * ada_cols :], axis=0)
    columns = jnp.sum(
        received[:, : item_count * ada_cols].reshape(n_dp, width, item_count, ada_cols), axis=1
    ).reshape(n_dp * item_count, ada_cols)
    ada_grad = jnp.einsum("id,ic->dc", cond_act.astype(f32), columns, precision=highest)
    grad_out_mine, grad_in_mine = grad_out_mine.astype(f32), grad_in_mine.astype(f32)

    gradients = (
        ada_grad,
        router_grad,
        grad_qkv_mine,
        grad_proj_mine.T,
        grad_in_mine[E],
        grad_out_mine[E].T,
        grad_in_mine[:E],
        jnp.swapaxes(grad_out_mine[:E], 1, 2),
    )
    states_of = (
        (ada_weight, ada_first, ada_second),
        (router_weight, router_first, router_second),
        (qkv_weight, qkv_first, qkv_second),
        (proj_weight, proj_first, proj_second),
        (shared_in_weight, shared_in_first, shared_in_second),
        (shared_out_weight, shared_out_first, shared_out_second),
        (expert_in_weight, expert_in_first, expert_in_second),
        (expert_out_weight, expert_out_first, expert_out_second),
    )
    total_hidden = float(hidden * width)
    fan_ins = (D, D, D, 8.0 * D / group, D, total_hidden, D, total_hidden)
    updates = []
    for (master, first, second), gradient, fan_in in zip(states_of, gradients, fan_ins):
        updates.extend(adamw_update(master, first, second, gradient, float(fan_in)))
    return tuple([result, patch_grad] + updates)


def solution(mesh):
    tokens, data = P(("dp", "mp"), None), P("dp", None)
    ada, router = P(None, ("dp", "mp")), P(("dp", "mp"))
    deep, wide = P("dp", "mp"), P("mp", "dp")
    deep_experts, wide_experts = P(None, "dp", "mp"), P(None, "mp", "dp")
    kinds = (ada, router, deep, wide, deep, wide, deep_experts, wide_experts)
    in_specs = (tokens, tokens, data, data, data) + tuple(k for k in kinds for _ in range(3))
    out_specs = (tokens, tokens) + tuple(k for k in kinds for _ in range(4))
    return jax.shard_map(body, mesh=mesh, in_specs=in_specs, out_specs=out_specs, check_vma=False)
```

```python
import functools
import math

import jax
import jax.numpy as jnp
import numpy as np
from jax import lax
from jax.experimental import pallas as pl
from jax.experimental.pallas import tpu as pltpu
from jax.sharding import PartitionSpec as P

H = 12
HD = 64
E = 8
STEP = 10

beta_one = 0.9
beta_two = 0.95
epsilon = 1e-08
weight_decay = 0.1
norm_floor = 1e-06
highest = lax.Precision.HIGHEST
f32 = jnp.float32
bf16 = jnp.bfloat16


def norm_parts(values):
    centred = values - jnp.mean(values, axis=1, keepdims=True)
    inverse = lax.rsqrt(jnp.mean(centred * centred, axis=1, keepdims=True) + norm_floor)
    return centred * inverse, inverse


def norm_back(normed, inverse, gradient):
    first = jnp.mean(gradient, axis=1, keepdims=True)
    second = jnp.mean(gradient * normed, axis=1, keepdims=True)
    return inverse * (gradient - first - normed * second)


def after(values, *earlier):
    return lax.optimization_barrier((values, earlier))[0]


def ring_gather(block):
    width = lax.axis_size("mp")
    return [block] + [
        lax.ppermute(block, "mp", [(i, (i + shift) % width) for i in range(width)])
        for shift in range(1, width)
    ]


def sent_beside(terms, near, far):
    width = len(terms)
    first = [i for i in range(1, width) if i in (1, width - 1)]
    later = [i for i in range(1, width) if i not in first]
    got, near = lax.optimization_barrier(([terms[i] for i in first], near))
    rest, far = lax.optimization_barrier(([terms[i] for i in later], far(near)))
    found = dict(zip(first + later, got + rest))
    return [terms[0]] + [found[i] for i in range(1, width)], near, far


def ring_scatter(parts):
    width = lax.axis_size("mp")
    return [parts[0]] + [
        lax.ppermute(parts[shift], "mp", [(i, (i - shift) % width) for i in range(width)])
        for shift in range(1, width)
    ]


LANES = 128
VMEM = 60 * 2**20
SMALL = pl.CostEstimate(flops=10**6, bytes_accessed=10**5, transcendentals=0)
Q_BLOCK = 256
FAR = 2.0**50
NT = (((1,), (1,)), ((), ()))
TN = (((0,), (0,)), ((), ()))
NN = (((1,), (0,)), ((), ()))


def dot(a, b, dims=NN):
    return lax.dot_general(a, b, dims, preferred_element_type=f32)


def key_widths(group):
    return sorted({min(w, group) for w in (512, 768, 1024, group)})


def key_windows(lengths, group):
    ends = jnp.cumsum(lengths)
    begins = ends - lengths
    first = jnp.arange(group // Q_BLOCK, dtype=jnp.int32) * Q_BLOCK
    last = first + Q_BLOCK - 1
    low = jnp.max(jnp.where(begins[None, :] <= first[:, None], begins[None, :], 0), axis=1)
    high = jnp.min(jnp.where(ends[None, :] > last[:, None], ends[None, :], group), axis=1)
    low = low // LANES * LANES
    widths = jnp.array(key_widths(group), jnp.int32)
    kind = jnp.sum((high - low)[:, None] > widths[None, :], axis=1).astype(jnp.int32)
    return jnp.minimum(low, group - widths[kind]).astype(jnp.int32), kind


def attend_kernel(start_ref, kind_ref, qkv_ref, mixed_ref, log_ref, *, group):
    block = pl.program_id(1)
    rows = pl.ds(pl.multiple_of(block * Q_BLOCK, Q_BLOCK), Q_BLOCK)
    query = qkv_ref[rows, 0:LANES] * jnp.asarray(HD**-0.5, bf16)
    for index, extent in enumerate(key_widths(group)):

        @pl.when(kind_ref[block] == index)
        def _():
            keys = pl.ds(pl.multiple_of(start_ref[block], LANES), extent)
            scores = dot(qkv_ref[keys, LANES : 2 * LANES], query, NT)
            peak = jnp.max(scores, axis=0, keepdims=True)
            exps = jnp.exp(scores - peak)
            total = jnp.sum(exps, axis=0, keepdims=True)
            probs = (exps * (1.0 / total)).astype(bf16)
            mixed = dot(qkv_ref[keys, 2 * LANES : 3 * LANES], probs, TN)
            mixed_ref[...] = mixed[:HD].astype(bf16)
            log_ref[...] = (peak + jnp.log(total))[None]


def attend(qkv, start, kind):
    group = qkv.shape[0]
    heads = qkv.shape[1] // (3 * LANES)
    blocks = group // Q_BLOCK
    return pl.pallas_call(
        functools.partial(attend_kernel, group=group),
        out_shape=(
            jax.ShapeDtypeStruct((heads * HD, group), bf16),
            jax.ShapeDtypeStruct((heads, 1, group), f32),
        ),
        grid_spec=pltpu.PrefetchScalarGridSpec(
            num_scalar_prefetch=2,
            grid=(heads, blocks),
            in_specs=[pl.BlockSpec((group, 3 * LANES), lambda h, i, *_: (0, h))],
            out_specs=(
                pl.BlockSpec((HD, Q_BLOCK), lambda h, i, *_: (h, i)),
                pl.BlockSpec((1, 1, Q_BLOCK), lambda h, i, *_: (h, 0, i)),
            ),
        ),
        compiler_params=pltpu.CompilerParams(vmem_limit_bytes=VMEM),
        cost_estimate=SMALL,
        name="attend",
    )(start, kind, qkv)


def attend_back_kernel(
    start_ref, kind_ref, qkv_ref, grad_ref, log_ref, out_ref, key_total, value_total, *, group
):
    block = pl.program_id(1)

    @pl.when(block == 0)
    def _():
        key_total[...] = jnp.zeros_like(key_total)
        value_total[...] = jnp.zeros_like(value_total)

    rows = pl.ds(pl.multiple_of(block * Q_BLOCK, Q_BLOCK), Q_BLOCK)
    scaling = HD**-0.5
    query = qkv_ref[rows, 0:LANES] * jnp.asarray(scaling, bf16)
    grad = grad_ref[...]
    kept = lax.broadcasted_iota(jnp.int32, (1, LANES), 1) < HD
    for index, extent in enumerate(key_widths(group)):

        @pl.when(kind_ref[block] == index)
        def _():
            keys = pl.ds(pl.multiple_of(start_ref[block], LANES), extent)
            key_rows = qkv_ref[keys, LANES : 2 * LANES]
            value_rows = qkv_ref[keys, 2 * LANES : 3 * LANES]
            probs = jnp.exp(dot(key_rows, query, NT) - log_ref[0])
            grad_probs = dot(value_rows[:, :HD], grad)
            middle = jnp.sum(probs * grad_probs, axis=0, keepdims=True)
            grad_scores = (probs * (grad_probs - middle)).astype(bf16)
            value_total[keys, :HD] += dot(probs.astype(bf16), grad, NT)
            key_total[keys, :] += dot(grad_scores, query)
            grad_query = dot(key_rows, grad_scores, TN).T * scaling
            out_ref[rows, 0:LANES] = jnp.where(kept, grad_query, 0.0).astype(bf16)

    @pl.when(block == pl.num_programs(1) - 1)
    def _():
        out_ref[:, LANES : 2 * LANES] = jnp.where(kept, key_total[...], 0.0).astype(bf16)
        out_ref[:, 2 * LANES : 3 * LANES] = value_total[...].astype(bf16)


def attend_back(qkv, grad_mixed, logs, start, kind):
    group = qkv.shape[0]
    heads = qkv.shape[1] // (3 * LANES)
    blocks = group // Q_BLOCK
    return pl.pallas_call(
        functools.partial(attend_back_kernel, group=group),
        out_shape=jax.ShapeDtypeStruct(qkv.shape, bf16),
        grid_spec=pltpu.PrefetchScalarGridSpec(
            num_scalar_prefetch=2,
            grid=(heads, blocks),
            in_specs=[
                pl.BlockSpec((group, 3 * LANES), lambda h, i, *_: (0, h)),
                pl.BlockSpec((HD, Q_BLOCK), lambda h, i, *_: (h, i)),
                pl.BlockSpec((1, 1, Q_BLOCK), lambda h, i, *_: (h, 0, i)),
            ],
            out_specs=pl.BlockSpec((group, 3 * LANES), lambda h, i, *_: (0, h)),
            scratch_shapes=[pltpu.VMEM((group, LANES), f32), pltpu.VMEM((group, LANES), f32)],
        ),
        compiler_params=pltpu.CompilerParams(vmem_limit_bytes=VMEM),
        cost_estimate=SMALL,
        name="attend_back",
    )(start, kind, qkv, grad_mixed, logs)


def item_rows(table_ref, term, width, segment, items):
    columns = slice(term * width, (term + 1) * width)
    rows = table_ref[0:1, columns]
    for item in range(1, items):
        rows = jnp.where(segment >= item, table_ref[item : item + 1, columns], rows)
    return rows


def item_sums(values, segment, items):
    return jnp.concatenate(
        [jnp.sum(jnp.where(segment == item, values, 0.0), axis=0, keepdims=True) for item in range(items)], axis=0
    )


def placed(width_mp):
    return lambda i, rank: (lax.rem(rank[0] - i + width_mp, width_mp), 0)


def plain(*shape):
    return pl.BlockSpec(shape, lambda i, rank: (0,) * len(shape))


def image_marks(heads, items):
    marks = np.zeros((items, heads, 3, LANES), np.float32)
    for image in range(items):
        for item in range(items):
            if image == item:
                marks[image, :, 0, HD + item] = FAR
            else:
                marks[image, :, 1, HD + item] = -FAR
    return marks.reshape(items, heads * 3 * LANES)


def norm_one_kernel(*refs, width_mp, items):
    rank_ref, segment_ref, table_ref, marks_ref, weight_ref = refs[:5]
    block_refs, (rows_ref, h_ref, qkv_ref, wide_ref) = refs[5:-4], refs[-4:]
    segment = segment_ref[...]
    width = rows_ref.shape[1]

    @pl.when(pl.program_id(0) == 0)
    def _():
        wide_ref[...] = jnp.zeros_like(wide_ref)
        for part in range(weight_ref.shape[1] // HD):
            wide_ref[:, part * LANES : part * LANES + HD] = weight_ref[:, part * HD : (part + 1) * HD]

    for place in range(width_mp):

        @pl.when(pl.program_id(0) == place)
        def _():
            rows_ref[...] = block_refs[place][...]

    normed, _ = norm_parts(rows_ref[...].astype(f32))
    shift = item_rows(table_ref, 0, width, segment, items)
    scale = item_rows(table_ref, 1, width, segment, items)
    h_one = (normed * (1.0 + scale) + shift).astype(bf16)
    h_ref[...] = h_one
    marks = item_rows(marks_ref, 0, qkv_ref.shape[1], segment, items)
    qkv_ref[...] = (dot(h_one, wide_ref[...]) + marks).astype(bf16)


def norm_one(arrays, rows, table, segment, weight):
    width_mp, width, items = len(arrays), arrays[0].shape[1], table.shape[0]
    heads = weight.shape[1] // (3 * HD)
    wide = heads * 3 * LANES
    marks = jnp.asarray(image_marks(heads, items))
    order = placed(width_mp)
    return pl.pallas_call(
        functools.partial(norm_one_kernel, width_mp=width_mp, items=items),
        out_shape=(
            jax.ShapeDtypeStruct((rows * width_mp, width), bf16),
            jax.ShapeDtypeStruct((rows * width_mp, width), bf16),
            jax.ShapeDtypeStruct((rows * width_mp, wide), bf16),
            jax.ShapeDtypeStruct((width, wide), bf16),
        ),
        grid_spec=pltpu.PrefetchScalarGridSpec(
            num_scalar_prefetch=1,
            grid=(width_mp,),
            in_specs=[pl.BlockSpec((rows, 1), order), plain(*table.shape), plain(*marks.shape), plain(*weight.shape)]
            + [plain(rows, width)] * len(arrays),
            out_specs=(
                pl.BlockSpec((rows, width), order),
                pl.BlockSpec((rows, width), order),
                pl.BlockSpec((rows, wide), order),
                plain(width, wide),
            ),
        ),
        compiler_params=pltpu.CompilerParams(vmem_limit_bytes=VMEM),
        cost_estimate=SMALL,
        name="norm_one",
    )(lax.axis_index("mp").reshape(1), segment, table, marks, weight, *arrays)


def gated_kernel(*refs, width_mp, items):
    rank_ref, segment_ref, table_ref = refs[:3]
    block_refs, out_ref = refs[3:-1], refs[-1]
    segment = segment_ref[...]
    width = out_ref.shape[1]
    for place in range(width_mp):

        @pl.when(pl.program_id(0) == place)
        def _():
            rows = block_refs[place][...].astype(f32)
            out_ref[...] = (item_rows(table_ref, 5, width, segment, items) * rows).astype(bf16)


def by_rows(kernel, outputs, arrays, rows, table, segment, name):
    width_mp, width, items = len(arrays), arrays[0].shape[1], table.shape[0]
    order = placed(width_mp)
    return pl.pallas_call(
        functools.partial(kernel, width_mp=width_mp, items=items),
        out_shape=(jax.ShapeDtypeStruct((rows * width_mp, width), bf16),) * outputs,
        grid_spec=pltpu.PrefetchScalarGridSpec(
            num_scalar_prefetch=1,
            grid=(width_mp,),
            in_specs=[pl.BlockSpec((rows, 1), order), plain(*table.shape)]
            + [plain(rows, width)] * len(arrays),
            out_specs=(pl.BlockSpec((rows, width), order),) * outputs,
        ),
        compiler_params=pltpu.CompilerParams(vmem_limit_bytes=VMEM),
        cost_estimate=SMALL,
        name=name,
    )(lax.axis_index("mp").reshape(1), segment, table, *arrays)


def norm_two_kernel(*refs, width_mp, items):
    rank_ref, segment_ref, table_ref, rows_ref, proj_ref = refs[:5]
    mixed_refs = refs[5:-4]
    h_ref, x_mine_ref, attn_mine_ref, mixed_mine_ref = refs[-4:]
    step = pl.program_id(0)
    rank = rank_ref[0]
    segment = segment_ref[...]
    width = rows_ref.shape[1]
    heads = mixed_refs[0].shape[0]

    attn = jnp.zeros(rows_ref.shape, f32)
    for place in range(width_mp):
        here = slice(place * heads, (place + 1) * heads)
        mixed = mixed_refs[place][...]
        attn += dot(mixed, proj_ref[here, :], TN)

        @pl.when(step == rank)
        def _():
            mixed_mine_ref[here, :] = mixed

    x_one = rows_ref[...].astype(f32) + item_rows(table_ref, 2, width, segment, items) * attn

    @pl.when(step == rank)
    def _():
        x_mine_ref[...] = x_one
        attn_mine_ref[...] = attn

    normed, _ = norm_parts(x_one)
    shift = item_rows(table_ref, 3, width, segment, items)
    scale = item_rows(table_ref, 4, width, segment, items)
    h_ref[...] = (normed * (1.0 + scale) + shift).astype(bf16)


def norm_two(arrays, patches, proj, table, segment):
    width_mp, (heads, group) = len(arrays), arrays[0].shape
    rows, width, items = group // width_mp, patches.shape[1], table.shape[0]
    every = heads * width_mp
    return pl.pallas_call(
        functools.partial(norm_two_kernel, width_mp=width_mp, items=items),
        out_shape=(
            jax.ShapeDtypeStruct((group, width), bf16),
            jax.ShapeDtypeStruct((rows, width), f32),
            jax.ShapeDtypeStruct((rows, width), f32),
            jax.ShapeDtypeStruct((every, rows), bf16),
        ),
        grid_spec=pltpu.PrefetchScalarGridSpec(
            num_scalar_prefetch=1,
            grid=(width_mp,),
            in_specs=[
                pl.BlockSpec((rows, 1), lambda i, rank: (i, 0)),
                plain(*table.shape),
                pl.BlockSpec((rows, width), lambda i, rank: (i, 0)),
                plain(*proj.shape),
            ]
            + [pl.BlockSpec((heads, rows), lambda i, rank: (0, i))] * len(arrays),
            out_specs=(
                pl.BlockSpec((rows, width), lambda i, rank: (i, 0)),
                plain(rows, width),
                plain(rows, width),
                plain(every, rows),
            ),
        ),
        compiler_params=pltpu.CompilerParams(vmem_limit_bytes=VMEM),
        cost_estimate=SMALL,
        name="norm_two",
    )(lax.axis_index("mp").reshape(1), segment, table, patches, proj, *arrays)


def product_kernel(rank_ref, a_ref, b_ref, part_ref, *out_refs):
    rows = a_ref.shape[0]
    for place, out_ref in enumerate(out_refs):

        @pl.when(pl.program_id(0) == place)
        def _():
            out_ref[0:rows, :] = dot(a_ref[...], b_ref[...], NT).astype(bf16)
            out_ref[rows:, :] = part_ref[0]


def ring_product(a, b, parts):
    width_mp, extra, width = parts.shape
    rows = a.shape[0] // width_mp
    return pl.pallas_call(
        product_kernel,
        out_shape=(jax.ShapeDtypeStruct((rows + extra, width), bf16),) * width_mp,
        grid_spec=pltpu.PrefetchScalarGridSpec(
            num_scalar_prefetch=1,
            grid=(width_mp,),
            in_specs=[
                pl.BlockSpec((rows, a.shape[1]), placed(width_mp)),
                plain(*b.shape),
                pl.BlockSpec((1, extra, width), lambda i, rank: (i, 0, 0)),
            ],
            out_specs=(plain(rows + extra, width),) * width_mp,
        ),
        compiler_params=pltpu.CompilerParams(vmem_limit_bytes=VMEM),
        cost_estimate=SMALL,
        name="grad_h_one",
    )(lax.axis_index("mp").reshape(1), a, b, parts)


def term_sum(refs):
    return functools.reduce(lambda total, ref: total + ref[...].astype(f32), refs[1:], refs[0][...].astype(f32))


def back_two_kernel(rank_ref, segment_ref, table_ref, *refs, width_mp, items):
    term_refs, (x_ref, attn_ref, cot_ref, proj_ref) = refs[:width_mp], refs[width_mp:-4]
    grad_x_ref, grad_attn_ref, grad_mixed_ref, sums_ref = refs[-4:]
    segment = segment_ref[...]
    width = x_ref.shape[1]
    heads = proj_ref.shape[0] // width_mp
    grad = term_sum(term_refs)
    normed, inverse = norm_parts(x_ref[...])
    scale = item_rows(table_ref, 4, width, segment, items)
    grad_x = cot_ref[...].astype(f32) + norm_back(normed, inverse, grad * (1.0 + scale))
    grad_x_ref[...] = grad_x
    grad_attn = (item_rows(table_ref, 2, width, segment, items) * grad_x).astype(bf16)
    grad_attn_ref[...] = grad_attn
    for place in range(width_mp):
        owner = lax.rem(rank_ref[0] - place + width_mp, width_mp)
        part = dot(proj_ref[place * heads : (place + 1) * heads, :], grad_attn, NT)
        grad_mixed_ref[owner] = part.astype(bf16)
    sums_ref[:, 0:width] = item_sums(grad_x * attn_ref[...], segment, items)
    sums_ref[:, width : 2 * width] = item_sums(grad, segment, items)
    sums_ref[:, 2 * width :] = item_sums(grad * normed, segment, items)


def back_two(terms, x_one, attn, cotangent, proj, table, segment):
    rows, width = x_one.shape
    items, width_mp = table.shape[0], lax.axis_size("mp")
    shapes = (
        jax.ShapeDtypeStruct((rows, width), f32),
        jax.ShapeDtypeStruct((rows, width), bf16),
        jax.ShapeDtypeStruct((width_mp, proj.shape[0] // width_mp, rows), bf16),
        jax.ShapeDtypeStruct((items, 3 * width), f32),
    )
    operands = (segment, table, *(t for t in terms), x_one, attn, cotangent, proj)
    return pl.pallas_call(
        functools.partial(back_two_kernel, width_mp=width_mp, items=items),
        out_shape=shapes,
        grid_spec=pltpu.PrefetchScalarGridSpec(
            num_scalar_prefetch=1,
            grid=(1,),
            in_specs=[plain(*o.shape) for o in operands],
            out_specs=tuple(plain(*o.shape) for o in shapes),
        ),
        compiler_params=pltpu.CompilerParams(vmem_limit_bytes=VMEM),
        cost_estimate=SMALL,
        name="back_two",
    )(lax.axis_index("mp").reshape(1), *operands)


def back_one_kernel(segment_ref, table_ref, *refs, items):
    term_refs, (patches_ref, grad_x_ref, grad_ref, sums_ref) = refs[:-4], refs[-4:]
    segment = segment_ref[...]
    width = patches_ref.shape[1]
    grad = term_sum(term_refs)
    normed, inverse = norm_parts(patches_ref[...].astype(f32))
    scale = item_rows(table_ref, 1, width, segment, items)
    grad_ref[...] = (grad_x_ref[...] + norm_back(normed, inverse, grad * (1.0 + scale))).astype(bf16)
    sums_ref[:, 0:width] = item_sums(grad, segment, items)
    sums_ref[:, width:] = item_sums(grad * normed, segment, items)


def outcome_kernel(segment_ref, table_ref, *refs, items):
    term_refs, (x_ref, cot_ref, out_ref, sums_ref) = refs[:-4], refs[-4:]
    segment = segment_ref[...]
    width = x_ref.shape[1]
    branch = term_sum(term_refs)
    gate = item_rows(table_ref, 5, width, segment, items)
    out_ref[...] = (x_ref[...] + gate * branch).astype(bf16)
    sums_ref[...] = item_sums(cot_ref[...].astype(f32) * branch, segment, items)


def own_rows(kernel, terms, first, second, table, segment, sums, name):
    rows, width = first.shape
    items = table.shape[0]
    shapes = (
        jax.ShapeDtypeStruct((rows, width), bf16),
        jax.ShapeDtypeStruct((items, sums * width), f32),
    )

    def single(*shape):
        return pl.BlockSpec(shape, lambda i: (0,) * len(shape))

    return pl.pallas_call(
        functools.partial(kernel, items=items),
        out_shape=shapes,
        grid=(1,),
        in_specs=[single(*segment.shape), single(*table.shape)]
        + [single(rows, width)] * (len(terms) + 2),
        out_specs=tuple(single(*o.shape) for o in shapes),
        compiler_params=pltpu.CompilerParams(vmem_limit_bytes=VMEM),
        cost_estimate=SMALL,
        name=name,
    )(segment, table, *terms, first, second)


def gelu_terms(before):
    slope = (2.0 / math.pi) ** 0.5
    square = before * before
    curve = jnp.tanh(slope * before * (1.0 + 0.044715 * square))
    half = 0.5 * (1.0 + curve)
    value = before * half
    derivative = half + (0.5 * slope) * before * (1.0 - curve * curve) * (1.0 + 0.134145 * square)
    return value, derivative


def slot_picks(place_row, capacity):
    slots = lax.broadcasted_iota(jnp.int32, (capacity, place_row.shape[1]), 0)
    return slots == place_row


def row_chunks(group):
    return [slice(first, first + 512) for first in range(0, group, 512)]


def before_kernel(
    place_ref, named_ref, branch_ref, weight_ref, *refs, count, shared
):
    slots_ref, named_slots_ref, back_ref = refs[-4:-1] if shared else refs[-3:]
    step = pl.program_id(0)

    @pl.when(step < count)
    def _():
        picks = slot_picks(place_ref[0], slots_ref.shape[1]).astype(bf16)
        slots = dot(picks, branch_ref[...]).astype(bf16)
        slots_ref[0] = slots
        named_slots_ref[0] = dot(picks, named_ref[...]).astype(bf16)
        back_ref[0] = dot(slots, weight_ref[0]).astype(bf16)

    if shared:

        @pl.when(step == count)
        def _():
            for chunk in row_chunks(branch_ref.shape[0]):
                refs[-1][chunk, :] = dot(branch_ref[chunk, :], weight_ref[0]).astype(bf16)


def whole(*shape):
    return pl.BlockSpec(shape, lambda *_: (0,) * len(shape), pipeline_mode=pl.Buffered(1))


def per_expert(experts, *shape):
    return pl.BlockSpec(
        (1,) + shape, lambda e, *_: (jnp.minimum(e, experts - 1),) + (0,) * len(shape)
    )


def per_slab(experts, *shape):
    return pl.BlockSpec((1,) + shape, lambda e, *_: (jnp.minimum(e, experts),) + (0,) * len(shape))


def experts_before(places, named, branch, out_t, capacity, first, held=None):
    group, width = branch.shape
    experts, hidden = out_t.shape[0] - 1, out_t.shape[2]
    base, count = (0, first) if held is None else (first, experts - first)
    shapes = (
        jax.ShapeDtypeStruct((experts, capacity, width), bf16),
        jax.ShapeDtypeStruct((experts, capacity, LANES), bf16),
        jax.ShapeDtypeStruct((experts, capacity, hidden), bf16),
    )

    def mine(*shape):
        return pl.BlockSpec(
            (1,) + shape, lambda e: (base + jnp.minimum(e, count - 1),) + (0,) * len(shape)
        )

    shared = held is not None
    return pl.pallas_call(
        functools.partial(before_kernel, count=count, shared=shared),
        out_shape=shapes + (jax.ShapeDtypeStruct((group, hidden), bf16),) * shared,
        grid=(count + shared,),
        in_specs=[
            mine(1, group),
            whole(group, LANES),
            whole(group, width),
            pl.BlockSpec((1, width, hidden), lambda e: (base + e, 0, 0)),
        ]
        + [pl.BlockSpec(memory_space=pl.ANY)] * (3 * shared),
        out_specs=(mine(capacity, width), mine(capacity, LANES), mine(capacity, hidden))
        + (whole(group, hidden),) * shared,
        input_output_aliases={4: 0, 5: 1, 6: 2} if shared else {},
        compiler_params=pltpu.CompilerParams(vmem_limit_bytes=VMEM),
        cost_estimate=SMALL,
        name="experts_before",
    )(places.reshape(experts, 1, group), named, branch, out_t, *(held or ()))


def slots_of(picked, slots):
    index = lax.broadcasted_iota(jnp.int32, (picked.shape[0], slots), 1)
    return ((index == picked[:, 0:1]) | (index == picked[:, 1:2])).astype(bf16)


def ring_store(out_refs, rank, owner, block):
    width_mp = len(out_refs)
    for place, out_ref in enumerate(out_refs):

        @pl.when(lax.rem(rank - owner + width_mp, width_mp) == place)
        def _():
            out_ref[...] = block


def experts_kernel(*refs, experts):
    rank_ref, place_ref, places_ref, picked_ref, rows_ref, weight_ref = refs[:6]
    router_ref, router_wide_ref, named_ref, back_ref, shared_back_ref = refs[6:11]
    dispatched_ref, act_ref, grad_pre_ref, gate_ref = refs[11:15]
    shared_act_ref, shared_grad_ref, grad_logits_ref = refs[15:18]
    grad_rows_refs = refs[18:-4]
    grad_gates_ref, grad_slots_ref, high_ref, rest_ref = refs[-4:]
    step = pl.program_id(0)
    group = rows_ref.shape[0]
    capacity = back_ref.shape[1]

    @pl.when(step < experts)
    def _():
        picks = slot_picks(place_ref[0], capacity)
        dispatched = dot(picks.astype(bf16), rows_ref[...]).astype(bf16)
        dispatched_ref[0] = dispatched
        pre = dot(dispatched, weight_ref[0])
        logits = dot(dispatched, router_wide_ref[...])
        lane = lax.broadcasted_iota(jnp.int32, logits.shape, 1)
        named = named_ref[0].astype(f32) > 0.0
        peak = jnp.max(jnp.where(named, logits, -jnp.inf), axis=1, keepdims=True)
        shares = jnp.where(named, jnp.exp(logits - peak), 0.0)
        total = jnp.sum(shares, axis=1, keepdims=True)
        own = jnp.sum(jnp.where(lane == step, shares, 0.0), axis=1, keepdims=True)
        gate = jnp.where(total > 0.0, own / jnp.maximum(total, 1.0), 0.0)
        gate_ref[0] = gate
        value, slope = gelu_terms(pre)
        act = value.astype(bf16)
        act_ref[0] = act
        back = back_ref[0].astype(f32)
        grad_pre = (gate * back * slope).astype(bf16)
        grad_pre_ref[0] = grad_pre
        grad_gate = jnp.sum(back * act.astype(f32), axis=1, keepdims=True)
        grad_gates_ref[step] = jnp.sum(jnp.where(picks, grad_gate, 0.0), axis=0, keepdims=True)
        here = pl.ds(pl.multiple_of(step * capacity, capacity), capacity)
        grad_slots_ref[here, :] = dot(grad_pre, weight_ref[0], NT).astype(bf16)

    @pl.when(step == experts)
    def _():
        logits = dot(router_ref[...], rows_ref[...], NT)
        named = places_ref[...] >= 0
        peak = jnp.max(jnp.where(named, logits, -jnp.inf), axis=0, keepdims=True)
        shares = jnp.where(named, jnp.exp(logits - peak), 0.0)
        gates = shares / jnp.sum(shares, axis=0, keepdims=True)
        grad_gates = jnp.concatenate([grad_gates_ref[e] for e in range(experts)], axis=0)
        grad_logits = gates * (grad_gates - jnp.sum(gates * grad_gates, axis=0, keepdims=True))
        grad_logits_ref[...] = grad_logits
        high = grad_logits.astype(bf16)
        high_ref[...] = high
        rest_ref[...] = (grad_logits - high.astype(f32)).astype(bf16)

    @pl.when(step >= experts)
    def _():
        size = shared_act_ref.shape[0]
        here = pl.ds(pl.multiple_of((step - experts) * size, size), size)
        value, slope = gelu_terms(dot(rows_ref[here, :], weight_ref[0]))
        shared_act_ref[...] = value.astype(bf16)
        grad_pre = (shared_back_ref[...].astype(f32) * slope).astype(bf16)
        shared_grad_ref[...] = grad_pre
        total = dot(slots_of(picked_ref[...], experts * capacity), grad_slots_ref[...])
        total += dot(grad_pre, weight_ref[0], NT)
        total += dot(high_ref[:, here], router_ref[...], TN)
        total += dot(rest_ref[:, here], router_ref[...], TN)
        ring_store(grad_rows_refs, rank_ref[0], step - experts, total.astype(bf16))


def row_block(experts, *shape):
    return pl.BlockSpec(shape, lambda e, *_: (jnp.maximum(e - experts, 0), 0))


def experts_main(places, picked, h_two, in_w, router, named, back, shared_back):
    group, width = h_two.shape
    experts, capacity, hidden = back.shape
    width_mp = lax.axis_size("mp")
    rows = group // width_mp
    unit_shape = jax.ShapeDtypeStruct((experts, capacity, hidden), bf16)
    return pl.pallas_call(
        functools.partial(experts_kernel, experts=experts),
        out_shape=(
            jax.ShapeDtypeStruct((experts, capacity, width), bf16),
            unit_shape,
            unit_shape,
            jax.ShapeDtypeStruct((experts, capacity, 1), f32),
            jax.ShapeDtypeStruct((group, hidden), bf16),
            jax.ShapeDtypeStruct((group, hidden), bf16),
            jax.ShapeDtypeStruct((experts, group), f32),
        )
        + (jax.ShapeDtypeStruct((rows, width), bf16),) * width_mp,
        grid_spec=pltpu.PrefetchScalarGridSpec(
            num_scalar_prefetch=1,
            grid=(experts + width_mp,),
            in_specs=[
                per_expert(experts, 1, group),
                whole(experts, group),
                row_block(experts, rows, 2),
                whole(group, width),
                per_slab(experts, width, hidden),
                whole(experts, width),
                whole(width, LANES),
                per_expert(experts, capacity, LANES),
                per_expert(experts, capacity, hidden),
                row_block(experts, rows, hidden),
            ],
            out_specs=(
                per_expert(experts, capacity, width),
                per_expert(experts, capacity, hidden),
                per_expert(experts, capacity, hidden),
                per_expert(experts, capacity, 1),
                row_block(experts, rows, hidden),
                row_block(experts, rows, hidden),
                whole(experts, group),
            )
            + (whole(rows, width),) * width_mp,
            scratch_shapes=[
                pltpu.VMEM((experts, 1, group), f32),
                pltpu.VMEM((experts * capacity, width), bf16),
                pltpu.VMEM((experts, group), bf16),
                pltpu.VMEM((experts, group), bf16),
            ],
        ),
        compiler_params=pltpu.CompilerParams(vmem_limit_bytes=VMEM),
        cost_estimate=SMALL,
        name="experts_main",
    )(
        lax.axis_index("mp").reshape(1),
        places.reshape(experts, 1, group),
        places,
        picked,
        h_two,
        in_w,
        router.T,
        jnp.pad(router, ((0, 0), (0, LANES - experts))),
        named,
        back,
        shared_back,
    )


def slab_kernel(a_ref, b_ref, a_shared_ref, b_shared_ref, *refs, experts):
    step = pl.program_id(0)
    out_ref = refs[-1]

    @pl.when(step < experts)
    def _():
        a = a_ref[0]
        if len(refs) > 1:
            a = (refs[0][0] * a.astype(f32)).astype(bf16)
        out_ref[0] = dot(a, b_ref[0], TN).astype(bf16)

    @pl.when(step == experts)
    def _():
        out_ref[0] = dot(a_shared_ref[...], b_shared_ref[...], TN).astype(bf16)


def slab_product(a, b, a_shared, b_shared, name, gates=None):
    experts, capacity, width = a.shape
    hidden = b.shape[2]
    group = a_shared.shape[0]
    scaled = gates is not None
    return pl.pallas_call(
        functools.partial(slab_kernel, experts=experts),
        out_shape=jax.ShapeDtypeStruct((experts + 1, width, hidden), bf16),
        grid=(experts + 1,),
        in_specs=[
            per_expert(experts, capacity, width),
            per_expert(experts, capacity, hidden),
            whole(group, width),
            whole(group, hidden),
        ]
        + [per_expert(experts, capacity, 1)] * scaled,
        out_specs=per_slab(experts, width, hidden),
        compiler_params=pltpu.CompilerParams(vmem_limit_bytes=VMEM),
        cost_estimate=SMALL,
        name=name,
    )(a, b, a_shared, b_shared, *((gates,) * scaled))


def branch_kernel(
    rank_ref, picked_ref, gate_ref, act_ref, weight_ref, shared_ref, *refs, experts
):
    out_refs, res_ref = refs[:-1], refs[-1]
    step = pl.program_id(0)
    capacity = act_ref.shape[1]

    @pl.when(step < experts)
    def _():
        here = pl.ds(pl.multiple_of(step * capacity, capacity), capacity)
        res_ref[here, :] = (gate_ref[0] * dot(act_ref[0], weight_ref[0], NT)).astype(bf16)

    @pl.when(step >= experts)
    def _():
        total = dot(slots_of(picked_ref[...], experts * capacity), res_ref[...])
        total += dot(shared_ref[...], weight_ref[0], NT)
        ring_store(out_refs, rank_ref[0], step - experts, total.astype(bf16))


def experts_out(picked, gates, act, out_t, shared_act):
    experts, capacity, hidden = act.shape
    group, width, width_mp = shared_act.shape[0], out_t.shape[1], lax.axis_size("mp")
    rows = group // width_mp
    return pl.pallas_call(
        functools.partial(branch_kernel, experts=experts),
        out_shape=(jax.ShapeDtypeStruct((rows, width), bf16),) * width_mp,
        grid_spec=pltpu.PrefetchScalarGridSpec(
            num_scalar_prefetch=1,
            grid=(experts + width_mp,),
            in_specs=[
                row_block(experts, rows, 2),
                per_expert(experts, capacity, 1),
                per_expert(experts, capacity, hidden),
                per_slab(experts, width, hidden),
                row_block(experts, rows, hidden),
            ],
            out_specs=(whole(rows, width),) * width_mp,
            scratch_shapes=[pltpu.VMEM((experts * capacity, width), bf16)],
        ),
        compiler_params=pltpu.CompilerParams(vmem_limit_bytes=VMEM),
        cost_estimate=SMALL,
        name="experts_out",
    )(lax.axis_index("mp").reshape(1), picked, gates, act, out_t, shared_act)


def adamw_update(master, first, second, gradient, fan_in):
    step_rate = 0.5 * fan_in ** (-0.5)
    first_new = beta_one * first + (1.0 - beta_one) * gradient
    second_new = beta_two * second + (1.0 - beta_two) * gradient * gradient
    first_hat = first_new / (1.0 - beta_one**STEP)
    second_hat = second_new / (1.0 - beta_two**STEP)
    master_new = master - step_rate * (
        first_hat / (jnp.sqrt(second_hat) + epsilon) + weight_decay * master
    )
    return (master_new, first_new, second_new, master_new.astype(bf16))


def body(
    patches,
    cotangent,
    conditioning,
    lengths,
    routes,
    ada_weight,
    ada_first,
    ada_second,
    router_weight,
    router_first,
    router_second,
    qkv_weight,
    qkv_first,
    qkv_second,
    proj_weight,
    proj_first,
    proj_second,
    shared_in_weight,
    shared_in_first,
    shared_in_second,
    shared_out_weight,
    shared_out_first,
    shared_out_second,
    expert_in_weight,
    expert_in_first,
    expert_in_second,
    expert_out_weight,
    expert_out_first,
    expert_out_second,
):
    rows, D = patches.shape
    width = lax.axis_size("mp")
    n_dp = lax.axis_size("dp")
    devices = width * n_dp
    group = rows * width
    capacity = 5 * group // 16
    heads_here = H // width
    model_rank = lax.axis_index("mp")
    item_count = lengths.shape[1]
    hidden = shared_in_weight.shape[1]
    ada_cols = ada_weight.shape[1]
    router_cols = router_weight.shape[0]

    out_slab = jnp.concatenate(
        [
            jnp.swapaxes(expert_out_weight.astype(bf16), 1, 2),
            shared_out_weight.astype(bf16).T[None],
        ],
        axis=0,
    )
    in_slab = jnp.concatenate(
        [expert_in_weight.astype(bf16), shared_in_weight.astype(bf16)[None]], axis=0
    )
    out_t = lax.all_gather(out_slab, "dp", axis=1, tiled=True)
    proj_block = proj_weight.astype(bf16).T
    proj_shape = proj_block.shape
    proj_rows = proj_block.size // D
    fill = -proj_rows % 32

    def riding(blocks):
        return jnp.pad(blocks, ((0, 0),) * (blocks.ndim - 2) + ((0, fill), (0, 0)))

    patches_blocks = ring_gather(
        after(jnp.concatenate([patches, riding(proj_block.reshape(-1, D))], axis=0), out_slab)
    )

    def over_dp(values):
        parts = lax.all_to_all(
            values.reshape((n_dp, values.shape[0] // n_dp) + values.shape[1:]), "dp", 0, 0, tiled=True
        )
        return jnp.sum(parts.astype(f32), axis=0)

    def from_dp(values):
        parts = jnp.broadcast_to(values[None], (n_dp,) + values.shape)
        return lax.all_to_all(parts, "dp", 0, 0, tiled=True).reshape((-1,) + values.shape[1:])

    cond_all = lax.all_gather(conditioning, "dp", axis=0, tiled=True)
    cond_act = jax.nn.silu(cond_all.astype(f32)).astype(bf16)
    columns = jnp.dot(cond_act, ada_weight.astype(bf16), preferred_element_type=f32)
    columns = jnp.repeat(columns.reshape(n_dp, item_count * ada_cols), width, axis=0)
    router_low = router_weight.astype(bf16).astype(f32)
    payload = jnp.concatenate(
        [columns, jnp.broadcast_to(router_low[None], (devices, router_cols))], axis=1
    )
    received = lax.all_to_all(payload, ("dp", "mp"), 0, 0, tiled=True)
    qkv_here = lax.all_gather(
        after(qkv_weight.astype(bf16), cond_all), "dp", axis=0, tiled=True
    )
    modulation = (
        received[:, : item_count * ada_cols]
        .reshape(devices, item_count, ada_cols)
        .transpose(1, 0, 2)
        .reshape(item_count, devices * ada_cols)
    )
    router_matrix = received[:, item_count * ada_cols :].reshape(D, E).astype(bf16)
    bounds = jnp.cumsum(lengths[0])
    places = jnp.arange(group, dtype=jnp.int32)
    segment = jnp.sum((places[:, None] >= bounds[None, :]).astype(jnp.int32), axis=1)
    segment_column = segment[:, None]
    segment_mine = lax.dynamic_slice_in_dim(segment_column, model_rank * rows, rows, 0)
    start, kind = key_windows(lengths[0], group)

    chosen = routes[:, :, None] == jnp.arange(E, dtype=jnp.int32)[None, None, :]
    names = chosen.any(axis=1)
    below = (places[:, None] > places[None, :]).astype(bf16)
    earlier = jnp.dot(below, names.astype(bf16), preferred_element_type=f32).astype(jnp.int32)
    place_of = jnp.where(names, earlier, -1).T
    picked = routes * capacity + jnp.sum(jnp.where(chosen, earlier[:, None, :], 0), axis=2)
    names_low = jnp.pad(names.astype(bf16), ((0, 0), (0, LANES - E)))

    cot_blocks = ring_gather(after(cotangent, *patches_blocks))
    patches_all, h_one_all, qkv, qkv_wide = norm_one(
        patches_blocks, rows, modulation, segment_column, qkv_here
    )
    proj_here = jnp.concatenate(
        [b[rows : rows + proj_rows].reshape(proj_shape) for b in patches_blocks], axis=1
    )
    near, far = (1, width - 1), tuple(range(2, width - 1))
    qkv, out_t, cot_near = lax.optimization_barrier((qkv, out_t, [cot_blocks[i] for i in near]))
    in_w = lax.all_gather(after(in_slab, out_t), "dp", axis=1, tiled=True)
    proj_t = from_dp(after(proj_here, qkv))
    mixed_here, logs, cot_far = lax.optimization_barrier(
        (*attend(qkv, start, kind), [cot_blocks[i] for i in far])
    )
    arrived = dict(zip(near + far, cot_near + cot_far))
    cot_blocks = [arrived.get(i, block) for i, block in enumerate(cot_blocks)]
    mixed_blocks = ring_gather(mixed_here)
    proj = after(proj_t, mixed_here).T
    proj, cot_blocks = lax.optimization_barrier((proj, cot_blocks))
    (grad_branch,) = by_rows(
        gated_kernel,
        1,
        after(cot_blocks, mixed_here),
        rows,
        modulation,
        segment_column,
        "grad_branch",
    )
    held = experts_before(place_of, names_low, grad_branch, out_t, capacity, E // 2)
    held = experts_before(place_of, names_low, grad_branch, out_t, capacity, E // 2, held)
    mixed_blocks, held = lax.optimization_barrier((mixed_blocks, held))
    branch_slots, named_slots, back_slots, back_shared = held
    h_two, x_one_mine, attn_mine, mixed_mine = norm_two(
        mixed_blocks, patches_all, proj, modulation, segment_column
    )

    (
        dispatched,
        expert_act,
        grad_expert_pre,
        gates,
        shared_act,
        grad_shared_pre,
        grad_logits,
        *grad_h_two,
    ) = experts_main(
        place_of,
        picked,
        h_two,
        in_w,
        router_matrix,
        named_slots,
        back_slots,
        back_shared,
    )
    two_terms = ring_scatter(grad_h_two)

    two_terms, grad_out_slab, mlp_part = sent_beside(
        two_terms,
        slab_product(branch_slots, expert_act, grad_branch, shared_act, "grad_out", gates),
        lambda near: experts_out(picked, after(gates, near), expert_act, out_t, shared_act),
    )
    grad_out_mine = lax.psum_scatter(grad_out_slab, "dp", scatter_dimension=1, tiled=True)
    grad_x_one, grad_attn, grad_mixed_mine, sums_two = back_two(
        two_terms, x_one_mine, attn_mine, cotangent, proj, modulation, segment_mine
    )
    grad_mixed = lax.all_to_all(grad_mixed_mine, "mp", 0, 0, tiled=True)
    mlp_terms = ring_scatter(mlp_part)
    grad_in_slab = slab_product(
        after(dispatched, grad_mixed_mine), grad_expert_pre, h_two, grad_shared_pre, "grad_in"
    )
    grad_router = jnp.einsum(
        "gd,eg->de", h_two.astype(f32), after(grad_logits, grad_mixed_mine), precision=highest
    )
    grad_mixed, grad_router, grad_in_slab, mlp_near, grad_out_mine = lax.optimization_barrier(
        (grad_mixed, grad_router, grad_in_slab, [mlp_terms[i] for i in near], grad_out_mine)
    )
    grad_in_mine = lax.psum_scatter(
        after(grad_in_slab, grad_out_mine), "dp", scatter_dimension=1, tiled=True
    )
    grad_mixed = grad_mixed.transpose(1, 0, 2).reshape(heads_here * HD, group)
    grad_proj_t = jnp.einsum(
        "gd,cg->dc", after(grad_attn, grad_mixed), mixed_mine, preferred_element_type=f32
    )
    grad_proj_t = over_dp(grad_proj_t.astype(bf16)).astype(bf16)
    grad_qkv, grad_proj_t, mlp_far = lax.optimization_barrier(
        (
            attend_back(qkv, grad_mixed, logs, start, kind),
            grad_proj_t,
            [mlp_terms[i] for i in far],
        )
    )
    proj_parts = grad_proj_t.reshape(proj_shape[0], width, proj_shape[1]).transpose(1, 0, 2)
    partial = ring_product(grad_qkv, qkv_wide, riding(proj_parts.reshape(width, -1, D)))
    one_terms = ring_scatter(partial)
    grad_qkv = after(grad_qkv, partial)
    grad_qkv_weight = jnp.einsum("gd,gc->dc", h_one_all, grad_qkv, preferred_element_type=f32)
    grad_qkv_weight = grad_qkv_weight.reshape(D, heads_here * 3, LANES)[:, :, :HD]
    grad_qkv_weight = grad_qkv_weight.reshape(D, heads_here * 3 * HD).astype(bf16)
    one_terms, grad_qkv_weight, (result, sums_gate, grad_qkv_mine, grad_in_mine) = sent_beside(
        one_terms,
        grad_qkv_weight,
        lambda made: (
            *own_rows(
                outcome_kernel,
                after([mlp_terms[0], *mlp_near, *mlp_far], made),
                x_one_mine,
                cotangent,
                modulation,
                segment_mine,
                1,
                "outcome",
            ),
            over_dp(made),
            grad_in_mine,
        ),
    )
    patch_grad, sums_one = own_rows(
        back_one_kernel, one_terms, patches, grad_x_one, modulation, segment_mine, 2, "back_one"
    )
    grad_proj_mine = sum(
        t[rows : rows + proj_rows].astype(f32) for t in one_terms
    ).reshape(proj_shape)
    grad_modulation = jnp.concatenate([sums_one, sums_two, sums_gate], axis=1)
    payload = jnp.concatenate(
        [
            grad_modulation.reshape(item_count, devices, ada_cols)
            .transpose(1, 0, 2)
            .reshape(devices, item_count * ada_cols),
            grad_router.reshape(devices, router_cols),
        ],
        axis=1,
    )
    received = lax.all_to_all(payload, ("dp", "mp"), 0, 0, tiled=True)
    router_grad = jnp.sum(received[:, item_count * ada_cols :], axis=0)
    columns = jnp.sum(
        received[:, : item_count * ada_cols].reshape(n_dp, width, item_count, ada_cols), axis=1
    ).reshape(n_dp * item_count, ada_cols)
    ada_grad = jnp.einsum("id,ic->dc", cond_act.astype(f32), columns, precision=highest)
    grad_out_mine, grad_in_mine = grad_out_mine.astype(f32), grad_in_mine.astype(f32)

    gradients = (
        ada_grad,
        router_grad,
        grad_qkv_mine,
        grad_proj_mine.T,
        grad_in_mine[E],
        grad_out_mine[E].T,
        grad_in_mine[:E],
        jnp.swapaxes(grad_out_mine[:E], 1, 2),
    )
    states_of = (
        (ada_weight, ada_first, ada_second),
        (router_weight, router_first, router_second),
        (qkv_weight, qkv_first, qkv_second),
        (proj_weight, proj_first, proj_second),
        (shared_in_weight, shared_in_first, shared_in_second),
        (shared_out_weight, shared_out_first, shared_out_second),
        (expert_in_weight, expert_in_first, expert_in_second),
        (expert_out_weight, expert_out_first, expert_out_second),
    )
    total_hidden = float(hidden * width)
    fan_ins = (D, D, D, 8.0 * D / group, D, total_hidden, D, total_hidden)
    updates = []
    for (master, first, second), gradient, fan_in in zip(states_of, gradients, fan_ins):
        updates.extend(adamw_update(master, first, second, gradient, float(fan_in)))
    return tuple([result, patch_grad] + updates)


def solution(mesh):
    tokens, data = P(("dp", "mp"), None), P("dp", None)
    ada, router = P(None, ("dp", "mp")), P(("dp", "mp"))
    deep, wide = P("dp", "mp"), P("mp", "dp")
    deep_experts, wide_experts = P(None, "dp", "mp"), P(None, "mp", "dp")
    kinds = (ada, router, deep, wide, deep, wide, deep_experts, wide_experts)
    in_specs = (tokens, tokens, data, data, data) + tuple(k for k in kinds for _ in range(3))
    out_specs = (tokens, tokens) + tuple(k for k in kinds for _ in range(4))
    return jax.shard_map(body, mesh=mesh, in_specs=in_specs, out_specs=out_specs, check_vma=False)
```
